32 devices in a mesh: prow: 4 (over y, core), pcol: 8 (over z, x).
Axes of the slice: x: 2, y: 2, z: 4, core: 2. Of those that a mesh axis runs over, the one named last changes fastest.
Arguments:
- trailing: float32 [8, 4, 128, 4, 8, 128], P(None, 'prow', None, None, 'pcol'), may hold values from -8 to 8, as said below
- reflectors: float32 [8, 4, 128, 256], P(None, 'prow', None, 'pcol'), may hold values from -0.5 to 0.5
- tfactor: float32 [256, 256], replicated, may hold values from -0.375 to 0.375
Outputs:
- updated: float32 [8, 4, 128, 4, 8, 128], P(None, 'prow', None, None, 'pcol')
The draws below stay inside these ranges and needn't reach their ends.
Inputs may be any that keep to these rules, and one draw needn't show every extreme that they name: trailing is symmetric as a matrix of order 4096.
All inputs are finite; a program needn't handle non-finite values.
Results may differ from the reference program's by a relative error of at most 0.00011.
Values sent between devices are 32-bit elements; how exact they have to be, the bound alone decides.
No kernel may reach another device: no remote copies, remote signals or barrier semaphores. Data moves between devices by JAX's collectives and lax.ppermute only.
A program may use at most 64 MiB of HBM per device.

```python
import jax
import jax.numpy as jnp
from jax import lax

TILE = 128
NB = 256
RT = 8
CT = 4
ORDER = 4096
N_PROW = 4


def draw_trailing(key, part):
    key = jax.random.fold_in(key, 11)
    base = jnp.clip(jax.random.normal(key, (ORDER, ORDER), jnp.float32), -5.5, 5.5)
    symmetric = (base + base.T) * 0.70710678
    return symmetric.reshape(RT, ORDER // (RT * TILE), TILE, CT, ORDER // (CT * TILE), TILE)


def block_scale(key, shape, split, smallest, high):
    def one(axis_at, blocks):
        heights = jax.random.uniform(jax.random.fold_in(jax.random.fold_in(key, 6), axis_at), (blocks,), jnp.float32, smallest / len(split), high / len(split))
        return jnp.repeat(jnp.exp(heights), shape[axis_at] // blocks).reshape((-1,) + (1,) * (len(shape) - axis_at - 1))

    level = one(*split[0])
    for cut in split[1:]:
        level = level * one(*cut)
    return level


def centred(rng, dims, width, most, cuts=(), dtype=jnp.bfloat16):
    values = jax.random.normal(rng, dims, jnp.float32) * width
    if len(cuts) > 0:
        values = block_scale(rng, dims, cuts, -0.22, 0.18) * values
    return jnp.clip(values, min=-most, max=most).astype(dtype)


def setup_inputs(seed: int = 0) -> dict:
    splits = jax.random.split(jax.random.key(seed), 4)
    return {
        "trailing": draw_trailing(jax.random.fold_in(splits[3], 71), 0),
        "reflectors": centred(splits[1], (RT, N_PROW, TILE, NB), ((NB * ORDER) ** -0.25), 0.5, ((1, 4), (3, 8)), jnp.float32),
        "tfactor": centred(splits[2], (NB, NB), NB ** -0.5, 0.375, (), jnp.float32),
    }


def matmul(left, right):
    return jnp.dot(left, right, precision=lax.Precision.HIGHEST, preferred_element_type=jnp.float32)


def reference(trailing, reflectors, tfactor):
    order_size = trailing.shape[0] * trailing.shape[1] * trailing.shape[2]
    full_matrix = trailing.reshape(order_size, order_size)
    vectors = reflectors.reshape(order_size, reflectors.shape[3])
    product = matmul(full_matrix, vectors)
    w_first = matmul(product, tfactor)
    inner_sum = matmul(vectors.T, w_first)
    correction = matmul(tfactor.T, inner_sum)
    w_full = w_first - 0.5 * matmul(vectors, correction)
    result = full_matrix - matmul(vectors, w_full.T) - matmul(w_full, vectors.T)
    return result.reshape(trailing.shape)
```

```python
import jax
import jax.numpy as jnp
from jax import lax
from jax.sharding import PartitionSpec as P


def matmul(left, right):
    return jnp.dot(left, right, precision=lax.Precision.HIGH, preferred_element_type=jnp.float32)


def swap(values, axis, mask):
    n = lax.axis_size(axis)
    return lax.ppermute(values, axis, [(i, i ^ mask) for i in range(n)])


def halving(n):
    masks = []
    while n > 1:
        n //= 2
        masks.append(n)
    return masks


def join(values, axis, mask):
    other = swap(values, axis, mask)
    high = (lax.axis_index(axis) & mask) != 0
    return jnp.stack([jnp.where(high, other, values), jnp.where(high, values, other)])


def gather(values, axis, masks):
    rank = values.ndim
    for mask in masks:
        values = join(values, axis, mask)
    order = sorted(range(len(masks)), key=lambda d: -masks[len(masks) - 1 - d])
    values = jnp.transpose(values, order + list(range(len(masks), values.ndim)))
    return values.reshape((-1,) + values.shape[len(masks):])


def per_device(trailing, reflectors, tfactor):
    row_tiles, _, tile, col_tiles = trailing.shape[:4]
    np_, nc = lax.axis_size("prow"), lax.axis_size("pcol")
    ratio = nc // np_
    ny = np_ // 2
    rows, cols = row_tiles * tile, col_tiles * tile
    nb = tfactor.shape[0]
    part = nb // np_
    block = trailing.reshape(rows, cols)
    prow, pcol = lax.axis_index("prow"), lax.axis_index("pcol")
    core, y = prow % 2, prow // 2
    group = pcol // np_

    def flat(p, q):
        return p * nc + q

    mine = jnp.transpose(reflectors.reshape(row_tiles, tile, -1), (2, 0, 1))
    masks = halving(nc)
    half = mine.shape[0] // 2
    first = gather(mine[:half], "pcol", masks)
    other_masks = masks[:-2] + [masks[-1], masks[-2]]
    second = gather(mine[half:], "pcol", other_masks)
    yt_rows = jnp.concatenate([first, second], axis=1).reshape(nb, row_tiles, tile)

    turn = [(flat(p, g * np_ + s), flat(s, g * np_ + p)) for p in range(np_) for g in range(ratio) for s in range(np_)]

    def columns(piece):
        piece = lax.ppermute(piece, ("prow", "pcol"), turn)
        return gather(piece, "prow", halving(np_)).reshape(nb, cols)

    grouped = yt_rows.reshape(np_, part, col_tiles, ratio, tile)
    y_group = lax.dynamic_index_in_dim(grouped, group, 3, keepdims=False)
    y_piece = lax.dynamic_index_in_dim(y_group, pcol % np_, 0, keepdims=False).reshape(part, cols)
    yt_cols = columns(y_piece)

    partial = matmul(yt_rows.reshape(nb, rows), block)
    by_core = partial.reshape(ny, 2, part, cols)
    keep = lax.dynamic_index_in_dim(by_core, core, 1, keepdims=False)
    send = lax.dynamic_index_in_dim(by_core, 1 - core, 1, keepdims=False)
    keep = keep + swap(send, "prow", 1)
    piece = jnp.zeros((part, cols), jnp.float32)
    for r in range(ny):
        perm = []
        for p in range(np_):
            for g in range(ratio):
                for s in range(np_):
                    perm.append((flat(p, g * np_ + s), flat(s, g * np_ + (((p // 2) ^ r) * 2 + p % 2))))
        message = lax.dynamic_index_in_dim(keep, y ^ r, 0, keepdims=False)
        piece = piece + lax.ppermute(message, ("prow", "pcol"), perm)

    inner = matmul(piece, y_group.reshape(nb, cols).T)
    for mask in halving(np_):
        inner = inner + swap(inner, "prow", mask)
    for mask in halving(ratio):
        inner = inner + swap(inner, "pcol", mask * np_)
    inner = gather(inner, "pcol", halving(np_)).reshape(nb, nb)

    zt_cols = columns(piece)
    half = part // 2
    first = gather(piece[:half], "pcol", masks)
    second = gather(piece[half:], "pcol", other_masks)
    zt = jnp.concatenate([first, second], axis=1).reshape(ratio, nb, col_tiles, tile)
    zt_rows = jnp.transpose(zt, (1, 2, 0, 3)).reshape(nb, rows)

    ut_rows = matmul(tfactor, yt_rows.reshape(nb, rows))
    ut_cols = matmul(tfactor, yt_cols)
    vt_cols = zt_cols - matmul(inner, ut_cols)
    result = block - matmul(zt_rows.T, ut_cols) - matmul(ut_rows.T, vt_cols)
    return result.reshape(trailing.shape)


def solution(mesh):
    return jax.shard_map(
        per_device,
        mesh=mesh,
        in_specs=(P(None, "prow", None, None, "pcol", None), P(None, "prow", None, "pcol"), P()),
        out_specs=P(None, "prow", None, None, "pcol", None),
        check_vma=False,
    )
```

```python
import functools

import jax
import jax.numpy as jnp
from jax import lax
from jax.experimental import pallas as pl
from jax.experimental.pallas import tpu as pltpu
from jax.sharding import PartitionSpec as P

BOTH = ("prow", "pcol")
F32 = jnp.float32
BF16 = jnp.bfloat16
VMEM = pltpu.CompilerParams(vmem_limit_bytes=48 * 1024 * 1024)


def split(values):
    high = values.astype(BF16)
    return high, (values - high.astype(F32)).astype(BF16)


def dot(left, right, dims=((1,), (0,))):
    return lax.dot_general(left, right, (dims, ((), ())), preferred_element_type=F32)


def dot3(left, right, dims=((1,), (0,))):
    (lh, ll), (rh, rl) = left, right
    return dot(lh, rh, dims) + (dot(lh, rl, dims) + dot(ll, rh, dims))


def swap(values, axis, mask):
    n = lax.axis_size(axis)
    return lax.ppermute(values, axis, [(i, i ^ mask) for i in range(n)])


def halving(n):
    masks = []
    while n > 1:
        n //= 2
        masks.append(n)
    return masks


def join(values, other, axis, mask):
    high = (lax.axis_index(axis) & mask) != 0
    pair = jnp.stack([jnp.where(high, other, values), jnp.where(high, values, other)])
    return pair.reshape((-1,) + values.shape[1:])


def gather(values, axis, masks):
    values = values[None]
    for mask in masks:
        values = join(values, swap(values, axis, mask), axis, mask)
    return values


def slot(index, masks):
    return sum(1 << j for j, mask in enumerate(masks) if index & mask)


def split_block_kernel(col_tiles, tile, a_ref, high_ref, low_ref):
    rows = high_ref.shape[0]
    for b in range(col_tiles):
        cols = slice(b * tile, (b + 1) * tile)
        high, low = split(a_ref[pl.ds(b, rows, stride=col_tiles), :])
        high_ref[:, cols] = high
        low_ref[:, cols] = low


def product_kernel(orders, core_ref, ah_ref, al_ref, first_ref, second_ref, y_ref, keep_ref, send_ref, yh, yl, total):
    nc, half, width, tile = first_ref.shape
    for chunk, (ref, masks) in enumerate(zip((first_ref, second_ref), orders)):
        for a in range(half):
            at = chunk * half + a
            for j in range(nc):
                y_ref[at, j * width : (j + 1) * width, :] = ref[slot(j, masks), a]
            cols = slice(at * tile, (at + 1) * tile)
            yh[:, cols], yl[:, cols] = split(y_ref[at])
    total[...] = dot3((yh[...], yl[...]), (ah_ref[...], al_ref[...]))
    count, part = keep_ref.shape[:2]
    core = core_ref[0]
    for y in range(count):
        keep_ref[y] = total[pl.ds(pl.multiple_of((2 * y + core) * part, part), part), :]
        send_ref[y] = total[pl.ds(pl.multiple_of((2 * y + 1 - core) * part, part), part), :]


def factor_kernel(order, t_ref, y_ref, cols_ref, urh_ref, url_ref, uch_ref, ucl_ref, scratch):
    row_tiles, nb, tile = y_ref.shape
    slots, ratio, col_tiles, width, _ = cols_ref.shape
    for g in range(ratio):
        for s in range(slots):
            at = (g * slots + s) * width
            for b in range(col_tiles):
                scratch[at : at + width, b * tile : (b + 1) * tile] = cols_ref[slot(s, order), g, b]
    factor = split(t_ref[...])
    uch_ref[...], ucl_ref[...] = split(dot3(factor, split(scratch[...])))
    for a in range(row_tiles):
        rows = slice(a * tile, (a + 1) * tile)
        urh_ref[rows, :], url_ref[rows, :] = split(dot3(factor, split(y_ref[a])).T)


def inner_kernel(group_ref, piece_ref, y_ref, out_ref):
    row_tiles, nb, tile = y_ref.shape
    col_tiles = piece_ref.shape[1] // tile
    ratio = row_tiles // col_tiles
    group = group_ref[0]
    total = jnp.zeros(out_ref.shape, F32)
    for b in range(col_tiles):
        left = split(piece_ref[:, b * tile : (b + 1) * tile])
        total += dot3(left, split(y_ref[b * ratio + group]), ((1,), (1,)))
    out_ref[...] = total


def update_kernel(
    orders, cols_order, a_ref, urh_ref, url_ref, uch_ref, ucl_ref, inner_ref, zc_ref, first_ref, second_ref,
    out_ref, zc, wh, wl,
):
    b_at = pl.program_id(0)
    nc, half, cols = first_ref.shape
    slots, part = zc_ref.shape[:2]
    ratio = nc // slots
    nb = slots * part
    tile = a_ref.shape[1]
    col_tiles = cols // tile

    @pl.when(b_at == 0)
    def _():
        for s in range(slots):
            zc[s * part : (s + 1) * part, :] = zc_ref[slot(s, cols_order)]
        w = zc[...] - dot3(split(inner_ref[...]), (uch_ref[...], ucl_ref[...]))
        wh[...], wl[...] = split(w)

    at = pl.ds(pl.multiple_of(b_at * tile, tile), tile)
    for g in range(ratio):
        pieces = []
        for s in range(slots):
            for ref, masks in zip((first_ref, second_ref), orders):
                pieces.append(ref[slot(g * slots + s, masks), :, at])
        z = split(jnp.concatenate(pieces, axis=0).T)
        rows = slice(g * tile, (g + 1) * tile)
        total = dot3((urh_ref[rows, :], url_ref[rows, :]), (wh[...], wl[...]))
        total += dot3(z, (uch_ref[...], ucl_ref[...]))
        for b in range(col_tiles):
            line = pl.ds(g * tile * col_tiles + b, tile, stride=col_tiles)
            out_ref[line, :] = a_ref[line, :] - total[:, b * tile : (b + 1) * tile]


def shape(*dims, dtype=F32):
    return jax.ShapeDtypeStruct(dims, dtype)


def per_device(trailing, reflectors, tfactor):
    row_tiles, _, tile, col_tiles = trailing.shape[:4]
    np_, nc = lax.axis_size("prow"), lax.axis_size("pcol")
    ratio = nc // np_
    ny = np_ // 2
    rows, cols = row_tiles * tile, col_tiles * tile
    nb = tfactor.shape[0]
    part = nb // np_
    half = row_tiles // 2
    block = trailing.reshape(rows * col_tiles, tile)
    prow, pcol = lax.axis_index("prow"), lax.axis_index("pcol")
    core, y = prow % 2, prow // 2
    group = pcol // np_
    scalar = pl.BlockSpec(memory_space=pltpu.SMEM)
    whole = pl.BlockSpec(memory_space=pltpu.VMEM)

    def flat(p, q):
        return p * nc + q

    def turn(g):
        return [
            (flat(p, h * np_ + s), flat(s, (h ^ g) * np_ + p))
            for p in range(np_)
            for h in range(ratio)
            for s in range(np_)
        ]

    mine = jnp.transpose(reflectors.reshape(row_tiles, tile, -1), (0, 2, 1))
    masks = halving(nc)
    orders = (masks, masks[:-2] + [masks[-1], masks[-2]])
    first = gather(mine[:half], "pcol", orders[0])
    second = gather(mine[half:], "pcol", orders[1])

    by_group = mine.reshape(col_tiles, ratio, -1, tile)
    arrived = jnp.stack(
        [
            lax.ppermute(lax.dynamic_index_in_dim(by_group, group ^ g, 1, keepdims=False), BOTH, turn(g))
            for g in range(ratio)
        ]
    )
    arrived = jnp.stack([lax.dynamic_index_in_dim(arrived, group ^ g, 0, keepdims=False) for g in range(ratio)])
    cols_order = halving(np_)
    y_cols = gather(arrived, "prow", cols_order)

    a_high, a_low = pl.pallas_call(
        functools.partial(split_block_kernel, col_tiles, tile),
        out_shape=[shape(rows, cols, dtype=BF16)] * 2,
        in_specs=[whole],
        out_specs=[whole] * 2,
        compiler_params=VMEM,
        cost_estimate=pl.CostEstimate(flops=rows * cols * 4, bytes_accessed=rows * cols * 8, transcendentals=0),
    )(block)

    y_rows, keep, send = pl.pallas_call(
        functools.partial(product_kernel, orders),
        out_shape=[shape(row_tiles, nb, tile), shape(ny, part, cols), shape(ny, part, cols)],
        in_specs=[scalar] + [whole] * 4,
        out_specs=[whole] * 3,
        scratch_shapes=[pltpu.VMEM((nb, rows), BF16), pltpu.VMEM((nb, rows), BF16), pltpu.VMEM((nb, cols), F32)],
        compiler_params=VMEM,
        cost_estimate=pl.CostEstimate(flops=6 * nb * rows * cols, bytes_accessed=rows * cols * 8, transcendentals=0),
    )(core.reshape(1).astype(jnp.int32), a_high, a_low, first, second)
    keep = keep + swap(send, "prow", 1)
    piece = jnp.zeros((part, cols), F32)
    for r in range(ny):
        perm = [
            (flat(p, g * np_ + s), flat(s, g * np_ + (((p // 2) ^ r) * 2 + p % 2)))
            for p in range(np_)
            for g in range(ratio)
            for s in range(np_)
        ]
        message = lax.dynamic_index_in_dim(keep, y ^ r, 0, keepdims=False)
        piece = piece + lax.ppermute(message, BOTH, perm)

    inner = pl.pallas_call(
        inner_kernel,
        out_shape=shape(part, nb),
        in_specs=[scalar] + [whole] * 2,
        out_specs=whole,
        compiler_params=VMEM,
    )(group.reshape(1).astype(jnp.int32), piece, y_rows)
    sharers = np_ * ratio
    bits = part * nb // sharers
    teams = [[flat(p, g * np_ + s) for p in range(np_) for g in range(ratio)] for s in range(np_)]
    inner = lax.all_to_all(
        inner.reshape(sharers, bits), BOTH, 0, 0, axis_index_groups=teams, tiled=True
    ).sum(axis=0)
    inner = lax.all_to_all(jnp.broadcast_to(inner, (np_ * nc, bits)), BOTH, 0, 0, tiled=True)
    inner = jnp.transpose(inner.reshape(np_, ratio, np_, bits), (2, 0, 1, 3)).reshape(nb, nb)

    z_first = gather(piece[: part // 2], "pcol", orders[0])
    z_second = gather(piece[part // 2 :], "pcol", orders[1])
    z_cols = gather(lax.ppermute(piece, BOTH, turn(0)), "prow", cols_order)

    urh, url, uch, ucl = pl.pallas_call(
        functools.partial(factor_kernel, cols_order),
        out_shape=[shape(rows, nb, dtype=BF16)] * 2 + [shape(nb, cols, dtype=BF16)] * 2,
        in_specs=[whole] * 3,
        out_specs=[whole] * 4,
        scratch_shapes=[pltpu.VMEM((nb, cols), F32)],
        compiler_params=VMEM,
        cost_estimate=pl.CostEstimate(flops=6 * nb * nb * (rows + cols), bytes_accessed=rows * nb * 8, transcendentals=0),
    )(tfactor, y_rows, y_cols)

    block_spec = pl.BlockSpec((ratio * tile * col_tiles, tile), lambda i: (i, 0))
    row_spec = pl.BlockSpec((ratio * tile, nb), lambda i: (i, 0))
    result = pl.pallas_call(
        functools.partial(update_kernel, orders, cols_order),
        grid=(col_tiles,),
        out_shape=shape(rows * col_tiles, tile),
        in_specs=[block_spec, row_spec, row_spec] + [whole] * 6,
        out_specs=block_spec,
        scratch_shapes=[pltpu.VMEM((nb, cols), F32), pltpu.VMEM((nb, cols), BF16), pltpu.VMEM((nb, cols), BF16)],
        compiler_params=VMEM,
        cost_estimate=pl.CostEstimate(flops=12 * nb * rows * cols, bytes_accessed=rows * cols * 8, transcendentals=0),
    )(block, urh, url, uch, ucl, inner, z_cols, z_first, z_second)
    return result.reshape(trailing.shape)


def solution(mesh):
    return jax.shard_map(
        per_device,
        mesh=mesh,
        in_specs=(P(None, "prow", None, None, "pcol", None), P(None, "prow", None, "pcol"), P()),
        out_specs=P(None, "prow", None, None, "pcol", None),
        check_vma=False,
    )
```

```python
import functools

import jax
import jax.numpy as jnp
from jax import lax
from jax.experimental import pallas as pl
from jax.experimental.pallas import tpu as pltpu
from jax.sharding import PartitionSpec as P

BOTH = ("prow", "pcol")
F32 = jnp.float32
BF16 = jnp.bfloat16
VMEM = pltpu.CompilerParams(vmem_limit_bytes=16 * 1024 * 1024)


def split(values):
    high = values.astype(BF16)
    return high, (values - high.astype(F32)).astype(BF16)


def dot(left, right, dims=((1,), (0,))):
    return lax.dot_general(left, right, (dims, ((), ())), preferred_element_type=F32)


def dot3(left, right, dims=((1,), (0,))):
    (lh, ll), (rh, rl) = left, right
    return dot(lh, rh, dims) + (dot(lh, rl, dims) + dot(ll, rh, dims))


def swap(values, axis, mask):
    n = lax.axis_size(axis)
    return lax.ppermute(values, axis, [(i, i ^ mask) for i in range(n)])


def halving(n):
    masks = []
    while n > 1:
        n //= 2
        masks.append(n)
    return masks


def join(values, other, axis, mask):
    high = (lax.axis_index(axis) & mask) != 0
    pair = jnp.stack([jnp.where(high, other, values), jnp.where(high, values, other)])
    return pair.reshape((-1,) + values.shape[1:])


def gather(values, axis, masks):
    values = values[None]
    for mask in masks:
        values = join(values, swap(values, axis, mask), axis, mask)
    return values


def gather_two(first, second, masks, other_masks):
    for mask, other in zip(masks, other_masks):
        first = join(first, swap(first, "pcol", mask), "pcol", mask)
        second = join(second, swap(second, "pcol", other), "pcol", other)
    return first, second


def slot(index, masks):
    return sum(1 << j for j, mask in enumerate(masks) if index & mask)


def split_block_kernel(col_tiles, tile, a_ref, high_ref, low_ref):
    rows = high_ref.shape[0]
    for b in range(col_tiles):
        cols = slice(b * tile, (b + 1) * tile)
        high, low = split(a_ref[pl.ds(b, rows, stride=col_tiles), :])
        high_ref[:, cols] = high
        low_ref[:, cols] = low


def product_kernel(
    orders, place_ref, ah_ref, al_ref, first_ref, second_ref, y_ref, part_ref, keep_ref, send_ref, yh, yl, total
):
    nc, half, width, tile = first_ref.shape
    for chunk, (ref, masks) in enumerate(zip((first_ref, second_ref), orders)):
        for a in range(half):
            at = chunk * half + a
            for j in range(nc):
                y_ref[at, j * width : (j + 1) * width, :] = ref[slot(j, masks), a]
            cols = slice(at * tile, (at + 1) * tile)
            yh[:, cols], yl[:, cols] = split(y_ref[at])
    total[...] = dot3((yh[...], yl[...]), (ah_ref[...], al_ref[...]))
    count, part, width = keep_ref.shape
    core, group, share = place_ref[0], place_ref[1], place_ref[2]
    for y in range(count):
        keep_ref[y] = total[pl.ds(pl.multiple_of((2 * y + core) * part, part), part), :]
        send_ref[y] = total[pl.ds(pl.multiple_of((2 * y + 1 - core) * part, part), part), :]
    col_tiles = width // tile
    ratio = 2 * half // col_tiles
    for b in range(col_tiles):
        values = y_ref[b * ratio + group, pl.ds(pl.multiple_of(share * part, part), part), :]
        part_ref[:, b * tile : (b + 1) * tile] = values


def row_factor_kernel(t_ref, y_ref, high_ref, low_ref):
    row_tiles, nb, tile = y_ref.shape
    factor = split(t_ref[...])
    for a in range(row_tiles):
        rows = slice(a * tile, (a + 1) * tile)
        high_ref[rows, :], low_ref[rows, :] = split(dot3(factor, split(y_ref[a])).T)


def pieces_kernel(count, group_ref, y_ref, part_ref, *refs):
    terms, (piece_ref, cols_ref, inner_ref) = refs[:count], refs[count:]
    row_tiles, nb, tile = y_ref.shape
    part, width = part_ref.shape
    half = part // 2
    col_tiles = width // tile
    ratio = row_tiles // col_tiles
    group = group_ref[0]
    piece = terms[0][...]
    for term in terms[1:]:
        piece += term[...]
    inner = jnp.zeros((part, nb), F32)
    for b in range(col_tiles):
        left = split(piece[:, b * tile : (b + 1) * tile])
        inner += dot3(left, split(y_ref[b * ratio + group]), ((1,), (1,)))
    for side in range(2):
        rows = slice(side * half, (side + 1) * half)
        piece_ref[side] = piece[rows]
        cols_ref[side] = piece[rows]
        cols_ref[2 + side] = part_ref[rows, :]
        inner_ref[:, side * nb : (side + 1) * nb] = inner[rows]


def columns_kernel(order, t_ref, cols_ref, high_ref, low_ref, z_ref, scratch):
    slots, half = cols_ref.shape[0], cols_ref.shape[2]
    for s in range(slots):
        for side in range(2):
            at = (2 * s + side) * half
            z_ref[at : at + half, :] = cols_ref[slot(s, order), side]
            scratch[at : at + half, :] = cols_ref[slot(s, order), 2 + side]
    high_ref[...], low_ref[...] = split(dot3(split(t_ref[...]), split(scratch[...])))


def update_kernel(
    orders, inner_order, a_ref, urh_ref, url_ref, uch_ref, ucl_ref, zc_ref, inner_ref, first_ref, second_ref,
    out_ref, inner, wh, wl,
):
    b_at = pl.program_id(0)
    nc, half, cols = first_ref.shape
    slots = inner_ref.shape[0]
    ratio = nc // slots
    nb = inner.shape[0]
    tile = a_ref.shape[1]
    col_tiles = cols // tile

    @pl.when(b_at == 0)
    def _():
        for s in range(slots):
            for side in range(2):
                at = (2 * s + side) * half
                inner[at : at + half, :] = inner_ref[slot(s, inner_order), :, side * nb : (side + 1) * nb]
        wh[...], wl[...] = split(zc_ref[...] - dot3(split(inner[...]), (uch_ref[...], ucl_ref[...])))

    at = pl.ds(pl.multiple_of(b_at * tile, tile), tile)
    for g in range(ratio):
        pieces = []
        for s in range(slots):
            for ref, masks in zip((first_ref, second_ref), orders):
                pieces.append(ref[slot(g * slots + s, masks), :, at])
        z = split(jnp.concatenate(pieces, axis=0).T)
        rows = slice(g * tile, (g + 1) * tile)
        total = dot3((urh_ref[rows, :], url_ref[rows, :]), (wh[...], wl[...]))
        total += dot3(z, (uch_ref[...], ucl_ref[...]))
        for b in range(col_tiles):
            line = pl.ds(g * tile * col_tiles + b, tile, stride=col_tiles)
            out_ref[line, :] = a_ref[line, :] - total[:, b * tile : (b + 1) * tile]


def shape(*dims, dtype=F32):
    return jax.ShapeDtypeStruct(dims, dtype)


def per_device(trailing, reflectors, tfactor):
    row_tiles, _, tile, col_tiles = trailing.shape[:4]
    np_, nc = lax.axis_size("prow"), lax.axis_size("pcol")
    ratio = nc // np_
    ny = np_ // 2
    rows, cols = row_tiles * tile, col_tiles * tile
    nb = tfactor.shape[0]
    part = nb // np_
    half = row_tiles // 2
    block = trailing.reshape(rows * col_tiles, tile)
    prow, pcol = lax.axis_index("prow"), lax.axis_index("pcol")
    core = prow % 2
    group = pcol // np_
    scalar = pl.BlockSpec(memory_space=pltpu.SMEM)
    whole = pl.BlockSpec(memory_space=pltpu.VMEM)

    def flat(p, q):
        return p * nc + q

    turn = [
        (flat(p, g * np_ + s), flat(s, g * np_ + p)) for p in range(np_) for g in range(ratio) for s in range(np_)
    ]

    masks = halving(nc)
    lead = masks[: len(masks) - len(halving(np_))]
    rest = masks[len(lead) :]
    turned = rest[:-2] + [rest[-1], rest[-2]]
    orders = (lead + rest, lead + turned)
    y = jnp.transpose(reflectors.reshape(row_tiles, tile, -1), (0, 2, 1))[None]
    for mask in lead:
        y = join(y, swap(y, "pcol", mask), "pcol", mask)
    first, second = gather_two(y[:, :half], y[:, half:], rest, turned)

    a_high, a_low = pl.pallas_call(
        functools.partial(split_block_kernel, col_tiles, tile),
        out_shape=[shape(rows, cols, dtype=BF16)] * 2,
        in_specs=[whole],
        out_specs=[whole] * 2,
        compiler_params=VMEM,
        cost_estimate=pl.CostEstimate(flops=rows * cols * 4, bytes_accessed=rows * cols * 8, transcendentals=0),
    )(block)

    y_rows, y_part, keep, send = pl.pallas_call(
        functools.partial(product_kernel, orders),
        out_shape=[shape(row_tiles, nb, tile), shape(part, cols), shape(ny, part, cols), shape(ny, part, cols)],
        in_specs=[scalar] + [whole] * 4,
        out_specs=[whole] * 4,
        scratch_shapes=[pltpu.VMEM((nb, rows), BF16), pltpu.VMEM((nb, rows), BF16), pltpu.VMEM((nb, cols), F32)],
        compiler_params=VMEM,
        cost_estimate=pl.CostEstimate(flops=6 * nb * rows * cols, bytes_accessed=rows * cols * 8, transcendentals=0),
    )(jnp.stack([core, group, pcol % np_]).astype(jnp.int32), a_high, a_low, first, second)
    keep = keep + swap(send, "prow", 1)
    terms = []
    for r in range(ny):
        perm = [
            (flat(p, g * np_ + s), flat(s, g * np_ + (((p // 2) ^ r) * 2 + p % 2)))
            for p in range(np_)
            for g in range(ratio)
            for s in range(np_)
        ]
        message = lax.dynamic_index_in_dim(keep, prow // 2 ^ r, 0, keepdims=False)
        terms.append(lax.ppermute(message, BOTH, perm))

    z, columns, inner = pl.pallas_call(
        functools.partial(pieces_kernel, ny),
        out_shape=[shape(2, part // 2, cols), shape(4, part // 2, cols), shape(part // 2, 2 * nb)],
        in_specs=[scalar] + [whole] * (2 + ny),
        out_specs=[whole] * 3,
        compiler_params=VMEM,
    )(group.reshape(1).astype(jnp.int32), y_rows, y_part, *terms)

    columns = lax.ppermute(columns, BOTH, turn)[None]
    z = z[None]
    for mask in lead:
        count = z.shape[0] * 2
        other = swap(jnp.concatenate([z.reshape(count, part // 2, cols), inner[None]]), "pcol", mask)
        z = join(z, other[:-1].reshape(z.shape), "pcol", mask)
        inner = inner + other[-1]
    z_first, z_second = gather_two(z[:, 0], z[:, 1], rest, turned)
    cols_order = halving(np_)
    for mask in cols_order:
        count = columns.shape[0] * 4
        other = swap(jnp.concatenate([columns.reshape(count, part // 2, cols), inner[None]]), "prow", mask)
        columns = join(columns, other[:-1].reshape(columns.shape), "prow", mask)
        inner = inner + other[-1]
    inner = gather(inner, "pcol", rest)

    urh, url = pl.pallas_call(
        row_factor_kernel,
        out_shape=[shape(rows, nb, dtype=BF16)] * 2,
        in_specs=[whole] * 2,
        out_specs=[whole] * 2,
        compiler_params=VMEM,
        cost_estimate=pl.CostEstimate(flops=6 * nb * nb * rows, bytes_accessed=rows * nb * 8, transcendentals=0),
    )(tfactor, y_rows)
    uch, ucl, zc = pl.pallas_call(
        functools.partial(columns_kernel, cols_order),
        out_shape=[shape(nb, cols, dtype=BF16)] * 2 + [shape(nb, cols)],
        in_specs=[whole] * 2,
        out_specs=[whole] * 3,
        scratch_shapes=[pltpu.VMEM((nb, cols), F32)],
        compiler_params=VMEM,
        cost_estimate=pl.CostEstimate(flops=6 * nb * nb * cols, bytes_accessed=cols * nb * 8, transcendentals=0),
    )(tfactor, columns)

    block_spec = pl.BlockSpec((ratio * tile * col_tiles, tile), lambda i: (i, 0))
    row_spec = pl.BlockSpec((ratio * tile, nb), lambda i: (i, 0))
    result = pl.pallas_call(
        functools.partial(update_kernel, orders, rest),
        grid=(col_tiles,),
        out_shape=shape(rows * col_tiles, tile),
        in_specs=[block_spec, row_spec, row_spec] + [whole] * 6,
        out_specs=block_spec,
        scratch_shapes=[pltpu.VMEM((nb, nb), F32), pltpu.VMEM((nb, cols), BF16), pltpu.VMEM((nb, cols), BF16)],
        compiler_params=VMEM,
        cost_estimate=pl.CostEstimate(flops=12 * nb * rows * cols, bytes_accessed=rows * cols * 8, transcendentals=0),
    )(block, urh, url, uch, ucl, zc, inner, z_first, z_second)
    return result.reshape(trailing.shape)


def solution(mesh):
    return jax.shard_map(
        per_device,
        mesh=mesh,
        in_specs=(P(None, "prow", None, None, "pcol", None), P(None, "prow", None, "pcol"), P()),
        out_specs=P(None, "prow", None, None, "pcol", None),
        check_vma=False,
    )
```

```python
import functools

import jax
import jax.numpy as jnp
from jax import lax
from jax.experimental import pallas as pl
from jax.experimental.pallas import tpu as pltpu
from jax.sharding import PartitionSpec as P

BOTH = ("prow", "pcol")
F32 = jnp.float32
BF16 = jnp.bfloat16
VMEM = pltpu.CompilerParams(vmem_limit_bytes=8 * 1024 * 1024)


def split(values):
    high = values.astype(BF16)
    return high, (values - high.astype(F32)).astype(BF16)


def dot(left, right, dims=((1,), (0,))):
    return lax.dot_general(left, right, (dims, ((), ())), preferred_element_type=F32)


def dot3(left, right, dims=((1,), (0,))):
    (lh, ll), (rh, rl) = left, right
    return dot(lh, rh, dims) + (dot(lh, rl, dims) + dot(ll, rh, dims))


def swap(values, axis, mask):
    n = lax.axis_size(axis)
    return lax.ppermute(values, axis, [(i, i ^ mask) for i in range(n)])


def halving(n):
    masks = []
    while n > 1:
        n //= 2
        masks.append(n)
    return masks


def join(values, other, axis, mask):
    high = (lax.axis_index(axis) & mask) != 0
    pair = jnp.stack([jnp.where(high, other, values), jnp.where(high, values, other)])
    return pair.reshape((-1,) + values.shape[1:])


def gather(values, axis, masks):
    values = values[None]
    for mask in masks:
        values = join(values, swap(values, axis, mask), axis, mask)
    return values


def slot(index, masks):
    return sum(1 << j for j, mask in enumerate(masks) if index & mask)


def split_block_kernel(col_tiles, tile, a_ref, high_ref, low_ref):
    rows = high_ref.shape[0]
    for b in range(col_tiles):
        cols = slice(b * tile, (b + 1) * tile)
        high, low = split(a_ref[pl.ds(b, rows, stride=col_tiles), :])
        high_ref[:, cols] = high
        low_ref[:, cols] = low


def product_kernel(
    orders, cols_order, core_ref, ah_ref, al_ref, first_ref, second_ref, cols_ref, y_ref, keep_ref, send_ref, yh, yl, total
):
    nc, half, width, tile = first_ref.shape
    for chunk, (ref, masks) in enumerate(zip((first_ref, second_ref), orders)):
        for a in range(half):
            at = chunk * half + a
            for j in range(nc):
                y_ref[at, j * width : (j + 1) * width, :] = ref[slot(j, masks), a]
            cols = slice(at * tile, (at + 1) * tile)
            yh[:, cols], yl[:, cols] = split(y_ref[at])
    total[...] = dot3((yh[...], yl[...]), (ah_ref[...], al_ref[...]))
    count, ratio, col_tiles = cols_ref.shape[:3]
    part = keep_ref.shape[0] // (2 * count)
    core = core_ref[0]
    for y in range(count):
        rows = slice(y * part, (y + 1) * part)
        keep_ref[rows, :] = total[pl.ds(pl.multiple_of((2 * y + core) * part, part), part), :]
        send_ref[rows, :] = total[pl.ds(pl.multiple_of((2 * y + 1 - core) * part, part), part), :]
        for g in range(ratio):
            at = count * part + (y * ratio + g) * width
            for b in range(col_tiles):
                values = cols_ref[slot(y, cols_order), g, b]
                keep_ref[at : at + width, b * tile : (b + 1) * tile] = values
                send_ref[at : at + width, b * tile : (b + 1) * tile] = values


def pieces_kernel(count, ratio, core_ref, kept_ref, came_ref, keep_ref, other_ref, piece_ref, inner_ref, y_ref):
    nb, cols = y_ref.shape
    half = piece_ref.shape[1]
    width = nb // (2 * count * ratio)
    core = core_ref[0]
    for y in range(count):
        for g in range(ratio):
            rows = slice(nb // 2 + (y * ratio + g) * width, nb // 2 + (y * ratio + g + 1) * width)
            for ref, c in ((keep_ref, core), (other_ref, 1 - core)):
                at = pl.multiple_of((g * 2 * count + 2 * y + c) * width, width)
                y_ref[pl.ds(at, width), :] = ref[rows, :]
    piece = kept_ref[...] + came_ref[...]
    inner = dot3(split(piece), split(y_ref[...]), ((1,), (1,)))
    for side in range(2):
        rows = slice(side * half, (side + 1) * half)
        piece_ref[side] = piece[rows]
        inner_ref[:, side * nb : (side + 1) * nb] = inner[rows]


def row_factor_kernel(t_ref, y_ref, high_ref, low_ref):
    row_tiles, nb, tile = y_ref.shape
    factor = split(t_ref[...])
    for a in range(row_tiles):
        rows = slice(a * tile, (a + 1) * tile)
        high_ref[rows, :], low_ref[rows, :] = split(dot3(factor, split(y_ref[a])).T)


def column_factor_kernel(t_ref, y_ref, high_ref, low_ref):
    high_ref[...], low_ref[...] = split(dot3(split(t_ref[...]), split(y_ref[...])))


def update_kernel(
    orders, cols_order, a_ref, urh_ref, url_ref, uch_ref, ucl_ref, cols_ref, first_ref, second_ref,
    out_ref, inner, zc, wh, wl,
):
    b_at = pl.program_id(0)
    nc, half, cols = first_ref.shape
    slots = cols_ref.shape[0]
    ratio = nc // slots
    nb = inner.shape[0]
    tile = a_ref.shape[1]
    col_tiles = cols // tile

    @pl.when(b_at == 0)
    def _():
        for s in range(slots):
            for side in range(2):
                at = (2 * s + side) * half
                zc[at : at + half, :] = cols_ref[slot(s, cols_order), side]
                inner[at : at + half, :] = cols_ref[slot(s, cols_order), 2, :, side * nb : (side + 1) * nb]
        wh[...], wl[...] = split(zc[...] - dot3(split(inner[...]), (uch_ref[...], ucl_ref[...])))

    at = pl.ds(pl.multiple_of(b_at * tile, tile), tile)
    for g in range(ratio):
        pieces = []
        for s in range(slots):
            for ref, masks in zip((first_ref, second_ref), orders):
                pieces.append(ref[slot(g * slots + s, masks), :, at])
        z = split(jnp.concatenate(pieces, axis=0).T)
        rows = slice(g * tile, (g + 1) * tile)
        total = dot3((urh_ref[rows, :], url_ref[rows, :]), (wh[...], wl[...]))
        total += dot3(z, (uch_ref[...], ucl_ref[...]))
        for b in range(col_tiles):
            line = pl.ds(g * tile * col_tiles + b, tile, stride=col_tiles)
            out_ref[line, :] = a_ref[line, :] - total[:, b * tile : (b + 1) * tile]


def shape(*dims, dtype=F32):
    return jax.ShapeDtypeStruct(dims, dtype)


def per_device(trailing, reflectors, tfactor):
    row_tiles, _, tile, col_tiles = trailing.shape[:4]
    np_, nc = lax.axis_size("prow"), lax.axis_size("pcol")
    ratio = nc // np_
    ny = np_ // 2
    rows, cols = row_tiles * tile, col_tiles * tile
    nb = tfactor.shape[0]
    part = nb // np_
    half = row_tiles // 2
    block = trailing.reshape(rows * col_tiles, tile)
    prow, pcol = lax.axis_index("prow"), lax.axis_index("pcol")
    core = prow % 2
    group = pcol // np_
    scalar = pl.BlockSpec(memory_space=pltpu.SMEM)
    whole = pl.BlockSpec(memory_space=pltpu.VMEM)

    def flat(p, q):
        return p * nc + q

    def turn(values, g):
        perm = [
            (flat(p, h * np_ + s), flat(s, (h ^ g) * np_ + p)) for p in range(np_) for h in range(ratio) for s in range(np_)
        ]
        return lax.ppermute(values, BOTH, perm)

    masks = halving(nc)
    lead = masks[: len(masks) - len(halving(np_))]
    rest = masks[len(lead) :]
    turned = rest[:-2] + [rest[-1], rest[-2]]
    orders = (lead + rest, lead + turned)
    cols_order = halving(np_)
    y = jnp.transpose(reflectors.reshape(row_tiles, tile, -1), (0, 2, 1))[None]
    for mask in lead:
        y = join(y, swap(y, "pcol", mask), "pcol", mask)
    y_cols = y.reshape(ratio, col_tiles, ratio, -1, tile)
    y_cols = turn(lax.dynamic_index_in_dim(y_cols, group, 2, keepdims=False), 0)[None]
    first, second = y[:, :half], y[:, half:]
    for mask, other in zip(rest, turned):
        first = join(first, swap(first, "pcol", mask), "pcol", mask)
        second = join(second, swap(second, "pcol", other), "pcol", other)
    for mask in cols_order[:-1]:
        y_cols = join(y_cols, swap(y_cols, "prow", mask), "prow", mask)

    a_high, a_low = pl.pallas_call(
        functools.partial(split_block_kernel, col_tiles, tile),
        out_shape=[shape(rows, cols, dtype=BF16)] * 2,
        in_specs=[whole],
        out_specs=[whole] * 2,
        compiler_params=VMEM,
        cost_estimate=pl.CostEstimate(flops=rows * cols * 4, bytes_accessed=rows * cols * 8, transcendentals=0),
    )(block)

    y_order = [mask // 2 for mask in cols_order[:-1]]
    core_at = core.reshape(1).astype(jnp.int32)
    y_rows, keep, send = pl.pallas_call(
        functools.partial(product_kernel, orders, y_order),
        out_shape=[shape(row_tiles, nb, tile), shape(nb, cols), shape(nb, cols)],
        in_specs=[scalar] + [whole] * 5,
        out_specs=[whole] * 3,
        scratch_shapes=[pltpu.VMEM((nb, rows), BF16), pltpu.VMEM((nb, rows), BF16), pltpu.VMEM((nb, cols), F32)],
        compiler_params=VMEM,
        cost_estimate=pl.CostEstimate(flops=6 * nb * rows * cols, bytes_accessed=rows * cols * 8, transcendentals=0),
    )(core_at, a_high, a_low, first, second, y_cols)
    other = swap(send, "prow", 1)
    urh, url = pl.pallas_call(
        row_factor_kernel,
        out_shape=[shape(rows, nb, dtype=BF16)] * 2,
        in_specs=[whole] * 2,
        out_specs=[whole] * 2,
        compiler_params=VMEM,
        cost_estimate=pl.CostEstimate(flops=6 * nb * nb * rows, bytes_accessed=rows * nb * 8, transcendentals=0),
    )(tfactor, y_rows)
    kept = (keep[: nb // 2] + other[: nb // 2]).reshape(ny, part, cols)
    came = jnp.zeros((part, cols), F32)
    for mask in y_order:
        pair = kept.reshape(2, mask, part, cols)
        bit = jnp.where((prow // 2) & mask != 0, 1, 0)
        kept = lax.dynamic_index_in_dim(pair, bit, 0, keepdims=False)
        came = swap(lax.dynamic_index_in_dim(pair, 1 - bit, 0, keepdims=False), "prow", 2 * mask)
        if mask > 1:
            kept = kept + came

    piece, inner, yt_cols = pl.pallas_call(
        functools.partial(pieces_kernel, ny, ratio),
        out_shape=[shape(2, part // 2, cols), shape(part // 2, 2 * nb), shape(nb, cols)],
        in_specs=[scalar] + [whole] * 4,
        out_specs=[whole] * 3,
        compiler_params=VMEM,
    )(core_at, kept.reshape(part, cols), came.reshape(part, cols), keep, other)

    uch, ucl = pl.pallas_call(
        column_factor_kernel,
        out_shape=[shape(nb, cols, dtype=BF16)] * 2,
        in_specs=[whole] * 2,
        out_specs=[whole] * 2,
        compiler_params=VMEM,
        cost_estimate=pl.CostEstimate(flops=6 * nb * nb * cols, bytes_accessed=cols * nb * 8, transcendentals=0),
    )(tfactor, yt_cols)

    arrived = [turn(piece, g) for g in range(ratio)]
    for mask in lead:
        inner = inner + swap(inner, "pcol", mask)
    for mask in rest[:-1]:
        inner = inner + swap(inner, "pcol", mask)
    arrived, inner = lax.optimization_barrier((arrived, inner))
    arrived = jnp.stack(arrived)
    z = jnp.stack([lax.dynamic_index_in_dim(arrived, group ^ g, 0, keepdims=False) for g in range(ratio)])
    first, second = z[:, 0], z[:, 1]
    for mask, other in zip(rest, turned):
        first = join(first, swap(first, "pcol", mask), "pcol", mask)
        if other == rest[-1]:
            came = swap(jnp.concatenate([second, inner[None]]), "pcol", other)
            second, inner = join(second, came[:-1], "pcol", other), inner + came[-1]
        else:
            second = join(second, swap(second, "pcol", other), "pcol", other)

    columns = gather(jnp.concatenate([piece, inner[None]]), "prow", cols_order)

    block_spec = pl.BlockSpec((ratio * tile * col_tiles, tile), lambda i: (i, 0))
    row_spec = pl.BlockSpec((ratio * tile, nb), lambda i: (i, 0))
    result = pl.pallas_call(
        functools.partial(update_kernel, orders, cols_order),
        grid=(col_tiles,),
        out_shape=shape(rows * col_tiles, tile),
        in_specs=[block_spec, row_spec, row_spec] + [whole] * 5,
        out_specs=block_spec,
        scratch_shapes=[
            pltpu.VMEM((nb, nb), F32),
            pltpu.VMEM((nb, cols), F32),
            pltpu.VMEM((nb, cols), BF16),
            pltpu.VMEM((nb, cols), BF16),
        ],
        compiler_params=VMEM,
        cost_estimate=pl.CostEstimate(flops=12 * nb * rows * cols, bytes_accessed=rows * cols * 8, transcendentals=0),
    )(block, urh, url, uch, ucl, columns, first, second)
    return result.reshape(trailing.shape)


def solution(mesh):
    return jax.shard_map(
        per_device,
        mesh=mesh,
        in_specs=(P(None, "prow", None, None, "pcol", None), P(None, "prow", None, "pcol"), P()),
        out_specs=P(None, "prow", None, None, "pcol", None),
        check_vma=False,
    )
```

```python
import functools

import jax
import jax.numpy as jnp
from jax import lax
from jax.experimental import pallas as pl
from jax.experimental.pallas import tpu as pltpu
from jax.sharding import PartitionSpec as P

BOTH = ("prow", "pcol")
F32 = jnp.float32
BF16 = jnp.bfloat16
VMEM = pltpu.CompilerParams(vmem_limit_bytes=8 * 1024 * 1024)


def split(values):
    high = values.astype(BF16)
    return high, (values - high.astype(F32)).astype(BF16)


def dot(left, right, dims=((1,), (0,))):
    return lax.dot_general(left, right, (dims, ((), ())), preferred_element_type=F32)


def dot3(left, right, dims=((1,), (0,))):
    (lh, ll), (rh, rl) = left, right
    return dot(lh, rh, dims) + (dot(lh, rl, dims) + dot(ll, rh, dims))


def swap(values, axis, mask):
    n = lax.axis_size(axis)
    return lax.ppermute(values, axis, [(i, i ^ mask) for i in range(n)])


def halving(n):
    masks = []
    while n > 1:
        n //= 2
        masks.append(n)
    return masks


def join(values, other, axis, mask):
    high = (lax.axis_index(axis) & mask) != 0
    pair = jnp.stack([jnp.where(high, other, values), jnp.where(high, values, other)])
    return pair.reshape((-1,) + values.shape[1:])


def gather(values, axis, masks):
    values = values[None]
    for mask in masks:
        values = join(values, swap(values, axis, mask), axis, mask)
    return values


def slot(index, masks):
    return sum(1 << j for j, mask in enumerate(masks) if index & mask)


def swap_three(values, axis):
    return [swap(values, axis, mask) for mask in (1, 2, 3)]


def split_block_kernel(col_tiles, tile, a_ref, y_ref, high_ref, low_ref, copy_ref):
    copy_ref[...] = y_ref[...]
    rows = high_ref.shape[0]
    for b in range(col_tiles):
        cols = slice(b * tile, (b + 1) * tile)
        high, low = split(a_ref[pl.ds(b, rows, stride=col_tiles), :])
        high_ref[:, cols] = high
        low_ref[:, cols] = low


def product_kernel(upper, place_ref, ah_ref, al_ref, *refs):
    came, (y_ref, keep_ref, send_ref, yh, yl, total) = refs[:4], refs[4:]
    blocks, row_tiles, width, tile = came[0].shape
    core, near = place_ref[0], place_ref[1]
    for a in range(row_tiles):
        for r, ref in enumerate(came):
            for u in range(blocks):
                at = pl.multiple_of((4 * u + (near ^ r)) * width, width)
                y_ref[a, pl.ds(at, width), :] = ref[slot(u, upper), a]
        cols = slice(a * tile, (a + 1) * tile)
        yh[:, cols], yl[:, cols] = split(y_ref[a])
    total[...] = dot3((yh[...], yl[...]), (ah_ref[...], al_ref[...]))
    count, part = keep_ref.shape[:2]
    for y in range(count):
        keep_ref[y] = total[pl.ds(pl.multiple_of((2 * y + core) * part, part), part), :]
        send_ref[y] = total[pl.ds(pl.multiple_of((2 * y + 1 - core) * part, part), part), :]


def inner_kernel(count, group_ref, y_ref, *refs):
    came, (first_ref, second_ref, inner_ref) = refs[:count], refs[count:]
    row_tiles, nb, tile = y_ref.shape
    part, cols = came[0].shape
    half = part // 2
    group = group_ref[0]
    inner = jnp.zeros((part, nb), F32)
    for g, ref in enumerate(came):
        at = group ^ g
        first_ref[at] = ref[:half, :]
        second_ref[at] = ref[half:, :]
        for b in range(cols // tile):
            left = split(ref[:, b * tile : (b + 1) * tile])
            inner += dot3(left, split(y_ref[b * count + at]), ((1,), (1,)))
    for side in range(2):
        inner_ref[:, side * nb : (side + 1) * nb] = inner[side * half : (side + 1) * half]


def row_factor_kernel(t_ref, y_ref, high_ref, low_ref):
    row_tiles, nb, tile = y_ref.shape
    factor = split(t_ref[...])
    for a in range(row_tiles):
        rows = slice(a * tile, (a + 1) * tile)
        high_ref[rows, :], low_ref[rows, :] = split(dot3(factor, split(y_ref[a])).T)


def column_factor_kernel(order, t_ref, z_in_ref, y_in_ref, high_ref, low_ref, z_ref, y):
    slots, _, half, _ = z_in_ref.shape
    for s in range(slots):
        for side in range(2):
            rows = slice((2 * s + side) * half, (2 * s + side + 1) * half)
            z_ref[rows, :] = z_in_ref[slot(s, order), side]
            y[rows, :] = y_in_ref[slot(s, order), side]
    high_ref[...], low_ref[...] = split(dot3(split(t_ref[...]), split(y[...])))


def update_kernel(
    orders, inner_upper, place_ref, a_ref, urh_ref, url_ref, uch_ref, ucl_ref, zc_ref, first_ref, second_ref, *refs
):
    inners, (out_ref, inner, zt, wh, wl) = refs[:4], refs[4:]
    b_at = pl.program_id(0)
    near = place_ref[1]
    ratio, nb, cols = zt.shape
    nc, half = first_ref.shape[:2]
    slots = nc // ratio
    tile = a_ref.shape[1]
    col_tiles = cols // tile

    @pl.when(b_at == 0)
    def _():
        for g in range(ratio):
            for s in range(slots):
                for side, (ref, masks) in enumerate(zip((first_ref, second_ref), orders)):
                    at = (2 * s + side) * half
                    zt[g, at : at + half, :] = ref[slot(g * slots + s, masks)]
        for r in range(4):
            for u in range(slots // 4):
                for side in range(2):
                    at = pl.multiple_of((2 * (u * 4 + (near ^ r)) + side) * half, half)
                    inner[pl.ds(at, half), :] = inners[r][slot(u, inner_upper), :, side * nb : (side + 1) * nb]
        wh[...], wl[...] = split(zc_ref[...] - dot3(split(inner[...]), (uch_ref[...], ucl_ref[...])))

    at = pl.ds(pl.multiple_of(b_at * tile, tile), tile)
    z = split(jnp.concatenate([zt[g, :, at].T for g in range(ratio)], axis=0))
    total = dot3((urh_ref[...], url_ref[...]), (wh[...], wl[...])) + dot3(z, (uch_ref[...], ucl_ref[...]))
    for g in range(ratio):
        for b in range(col_tiles):
            line = pl.ds(g * tile * col_tiles + b, tile, stride=col_tiles)
            out_ref[line, :] = a_ref[line, :] - total[g * tile : (g + 1) * tile, b * tile : (b + 1) * tile]


def shape(*dims, dtype=F32):
    return jax.ShapeDtypeStruct(dims, dtype)


def per_device(trailing, reflectors, tfactor):
    row_tiles, _, tile, col_tiles = trailing.shape[:4]
    np_, nc = lax.axis_size("prow"), lax.axis_size("pcol")
    ratio = nc // np_
    ny = np_ // 2
    rows, cols = row_tiles * tile, col_tiles * tile
    nb = tfactor.shape[0]
    part = nb // np_
    half = row_tiles // 2
    block = trailing.reshape(rows * col_tiles, tile)
    prow, pcol = lax.axis_index("prow"), lax.axis_index("pcol")
    core = prow % 2
    group = pcol // np_
    scalar = pl.BlockSpec(memory_space=pltpu.SMEM)
    whole = pl.BlockSpec(memory_space=pltpu.VMEM)

    def flat(p, q):
        return p * nc + q

    def turn(values, g):
        perm = [
            (flat(p, h * np_ + s), flat(s, (h ^ g) * np_ + p)) for p in range(np_) for h in range(ratio) for s in range(np_)
        ]
        return lax.ppermute(values, BOTH, perm)

    masks = halving(nc)
    lead = masks[: len(masks) - len(halving(np_))]
    rest = masks[len(lead) : -2]
    upper = [mask // 4 for mask in lead + rest]
    inner_upper = [mask // 4 for mask in rest]
    cols_order = halving(np_)
    place = jnp.stack([core, pcol % 4, group]).astype(jnp.int32)
    mine = jnp.transpose(reflectors.reshape(row_tiles, tile, -1), (0, 2, 1))
    a_high, a_low, copy = pl.pallas_call(
        functools.partial(split_block_kernel, col_tiles, tile),
        out_shape=[shape(rows, cols, dtype=BF16)] * 2 + [shape(*mine.shape)],
        in_specs=[whole] * 2,
        out_specs=[whole] * 3,
        compiler_params=VMEM,
        cost_estimate=pl.CostEstimate(flops=rows * cols * 4, bytes_accessed=rows * cols * 8, transcendentals=0),
    )(block, mine)
    y = copy[None]
    for at, mask in enumerate(lead + rest):
        y = join(y, swap(mine[None] if at == 0 else y, "pcol", mask), "pcol", mask)
    near_y = [y] + swap_three(y, "pcol")

    y_rows, keep, send = pl.pallas_call(
        functools.partial(product_kernel, upper),
        out_shape=[shape(row_tiles, nb, tile), shape(ny, part, cols), shape(ny, part, cols)],
        in_specs=[scalar] + [whole] * 6,
        out_specs=[whole] * 3,
        scratch_shapes=[pltpu.VMEM((nb, rows), BF16), pltpu.VMEM((nb, rows), BF16), pltpu.VMEM((nb, cols), F32)],
        compiler_params=VMEM,
        cost_estimate=pl.CostEstimate(flops=6 * nb * rows * cols, bytes_accessed=rows * cols * 8, transcendentals=0),
    )(place, a_high, a_low, *near_y)
    other = swap(send, "prow", 1)
    kept = keep + other
    y_piece = lax.dynamic_slice(
        y_rows.reshape(col_tiles, ratio, nb, tile), (0, group, (pcol % np_) * part, 0), (col_tiles, 1, part, tile)
    )
    y_piece = jnp.transpose(y_piece.reshape(col_tiles, part, tile), (1, 0, 2)).reshape(part, cols)
    y_piece, kept = lax.optimization_barrier((y_piece, kept))
    y_cols = turn(y_piece, 0).reshape(1, 2, part // 2, cols)
    for mask in [m // 2 for m in cols_order[:-1]]:
        pair = kept.reshape(2, mask, part, cols)
        bit = jnp.where((prow // 2) & mask != 0, 1, 0)
        kept = lax.dynamic_index_in_dim(pair, bit, 0, keepdims=False)
        kept = kept + swap(lax.dynamic_index_in_dim(pair, 1 - bit, 0, keepdims=False), "prow", 2 * mask)
    piece = kept.reshape(part, cols)
    for mask in cols_order[:-1]:
        y_cols = join(y_cols, swap(y_cols, "prow", mask), "prow", mask)

    arrived = [turn(piece, g) for g in range(ratio)]
    urh, url = pl.pallas_call(
        row_factor_kernel,
        out_shape=[shape(rows, nb, dtype=BF16)] * 2,
        in_specs=[whole] * 2,
        out_specs=[whole] * 2,
        compiler_params=VMEM,
        cost_estimate=pl.CostEstimate(flops=6 * nb * nb * rows, bytes_accessed=rows * nb * 8, transcendentals=0),
    )(tfactor, y_rows)
    first, second, inner = pl.pallas_call(
        functools.partial(inner_kernel, ratio),
        out_shape=[shape(ratio, part // 2, cols)] * 2 + [shape(part // 2, 2 * nb)],
        in_specs=[scalar] + [whole] * (1 + ratio),
        out_specs=[whole] * 3,
        compiler_params=VMEM,
    )(group.reshape(1).astype(jnp.int32), y_rows, *arrived)
    masks = halving(np_)
    turned = masks[:-2] + [masks[-1], masks[-2]]
    orders = (lead + masks, lead + turned)
    for mask, other in zip(masks, turned):
        first = join(first, swap(first, "pcol", mask), "pcol", mask)
        second = join(second, swap(second, "pcol", other), "pcol", other)

    z_cols = piece.reshape(1, 2, part // 2, cols)
    for mask in cols_order:
        z_shape, y_shape = z_cols.shape, y_cols.shape
        message = [inner[None], z_cols.reshape(-1, part // 2, cols)]
        if mask == cols_order[-1]:
            message.append(y_cols.reshape(-1, part // 2, cols))
        came = swap(jnp.concatenate(message), "prow", mask)
        inner = inner + came[0]
        count = z_shape[0] * 2
        z_cols = join(z_cols, came[1 : 1 + count].reshape(z_shape), "prow", mask)
        if mask == cols_order[-1]:
            y_cols = join(y_cols, came[1 + count :].reshape(y_shape), "prow", mask)
    inner = gather(inner, "pcol", rest)
    near_inner = [inner] + swap_three(inner, "pcol")
    uch, ucl, zc = pl.pallas_call(
        functools.partial(column_factor_kernel, cols_order),
        out_shape=[shape(nb, cols, dtype=BF16)] * 2 + [shape(nb, cols)],
        in_specs=[whole] * 3,
        out_specs=[whole] * 3,
        scratch_shapes=[pltpu.VMEM((nb, cols), F32)],
        compiler_params=VMEM,
        cost_estimate=pl.CostEstimate(flops=6 * nb * nb * cols, bytes_accessed=cols * nb * 8, transcendentals=0),
    )(tfactor, z_cols, y_cols)

    block_spec = pl.BlockSpec((ratio * tile * col_tiles, tile), lambda i: (i, 0))
    row_spec = pl.BlockSpec((ratio * tile, nb), lambda i: (i, 0))
    result = pl.pallas_call(
        functools.partial(update_kernel, orders, inner_upper),
        grid=(col_tiles,),
        out_shape=shape(rows * col_tiles, tile),
        in_specs=[scalar, block_spec, row_spec, row_spec] + [whole] * 9,
        out_specs=block_spec,
        scratch_shapes=[
            pltpu.VMEM((nb, nb), F32),
            pltpu.VMEM((ratio, nb, cols), F32),
            pltpu.VMEM((nb, cols), BF16),
            pltpu.VMEM((nb, cols), BF16),
        ],
        compiler_params=VMEM,
        cost_estimate=pl.CostEstimate(flops=12 * nb * rows * cols, bytes_accessed=rows * cols * 8, transcendentals=0),
    )(place, block, urh, url, uch, ucl, zc, first, second, *near_inner)
    return result.reshape(trailing.shape)


def solution(mesh):
    return jax.shard_map(
        per_device,
        mesh=mesh,
        in_specs=(P(None, "prow", None, None, "pcol", None), P(None, "prow", None, "pcol"), P()),
        out_specs=P(None, "prow", None, None, "pcol", None),
        check_vma=False,
    )
```

```python
import functools

import jax
import jax.numpy as jnp
from jax import lax
from jax.experimental import pallas as pl
from jax.experimental.pallas import tpu as pltpu
from jax.sharding import PartitionSpec as P

BOTH = ("prow", "pcol")
F32 = jnp.float32
BF16 = jnp.bfloat16
VMEM = pltpu.CompilerParams(vmem_limit_bytes=8 * 1024 * 1024)


def split(values):
    high = values.astype(BF16)
    return high, (values - high.astype(F32)).astype(BF16)


def dot(left, right, dims=((1,), (0,))):
    return lax.dot_general(left, right, (dims, ((), ())), preferred_element_type=F32)


def dot3(left, right, dims=((1,), (0,))):
    (lh, ll), (rh, rl) = left, right
    return dot(lh, rh, dims) + (dot(lh, rl, dims) + dot(ll, rh, dims))


def swap(values, axis, mask):
    n = lax.axis_size(axis)
    return lax.ppermute(values, axis, [(i, i ^ mask) for i in range(n)])


def halving(n):
    masks = []
    while n > 1:
        n //= 2
        masks.append(n)
    return masks


def join(values, other, high):
    pair = jnp.stack([jnp.where(high, other, values), jnp.where(high, values, other)])
    return pair.reshape((-1,) + values.shape[1:])


def gather(values, axis, masks, above):
    values = values[None]
    for mask in masks:
        values = join(values, swap(values, axis, mask), above[mask])
    return values


def slot(index, masks):
    return sum(1 << j for j, mask in enumerate(masks) if index & mask)


def swap_three(values, axis):
    return [swap(values, axis, mask) for mask in (1, 2, 3)]


def split_block_kernel(col_tiles, tile, a_ref, y_ref, high_ref, low_ref, copy_ref):
    copy_ref[...] = y_ref[...]
    rows = high_ref.shape[0]
    for b in range(col_tiles):
        cols = slice(b * tile, (b + 1) * tile)
        high, low = split(a_ref[pl.ds(b, rows, stride=col_tiles), :])
        high_ref[:, cols] = high
        low_ref[:, cols] = low


def product_kernel(upper, place_ref, ah_ref, al_ref, *refs):
    came, (y_ref, keep_ref, send_ref, yh, yl, total) = refs[:4], refs[4:]
    blocks, row_tiles, width, tile = came[0].shape
    core, near = place_ref[0], place_ref[1]
    for a in range(row_tiles):
        for r, ref in enumerate(came):
            for u in range(blocks):
                at = pl.multiple_of((4 * u + (near ^ r)) * width, width)
                y_ref[a, pl.ds(at, width), :] = ref[slot(u, upper), a]
        cols = slice(a * tile, (a + 1) * tile)
        yh[:, cols], yl[:, cols] = split(y_ref[a])
    total[...] = dot3((yh[...], yl[...]), (ah_ref[...], al_ref[...]))
    count, part = keep_ref.shape[:2]
    for y in range(count):
        keep_ref[y] = total[pl.ds(pl.multiple_of((2 * y + core) * part, part), part), :]
        send_ref[y] = total[pl.ds(pl.multiple_of((2 * y + 1 - core) * part, part), part), :]


def inner_kernel(count, place_ref, y_ref, *refs):
    came, (first_ref, second_ref, inner_ref) = refs[:count], refs[count:]
    row_tiles, nb, tile = y_ref.shape
    part, cols = came[0].shape
    half = part // 2
    group = place_ref[2]
    inner = jnp.zeros((part, nb), F32)
    for g, ref in enumerate(came):
        at = group ^ g
        first_ref[at] = ref[:half, :]
        second_ref[at] = ref[half:, :]
        for b in range(cols // tile):
            left = split(ref[:, b * tile : (b + 1) * tile])
            inner += dot3(left, split(y_ref[b * count + at]), ((1,), (1,)))
    for side in range(2):
        inner_ref[:, side * nb : (side + 1) * nb] = inner[side * half : (side + 1) * half]


def row_factor_kernel(t_ref, y_ref, high_ref, low_ref):
    row_tiles, nb, tile = y_ref.shape
    factor = split(t_ref[...])
    for a in range(row_tiles):
        rows = slice(a * tile, (a + 1) * tile)
        high_ref[rows, :], low_ref[rows, :] = split(dot3(factor, split(y_ref[a])).T)


def column_factor_kernel(order, t_ref, cols_ref, high_ref, low_ref, z_ref, y):
    slots, _, half, _ = cols_ref.shape
    for s in range(slots):
        for side in range(2):
            rows = slice((2 * s + side) * half, (2 * s + side + 1) * half)
            z_ref[rows, :] = cols_ref[slot(s, order), side]
            y[rows, :] = cols_ref[slot(s, order), 2 + side]
    high_ref[...], low_ref[...] = split(dot3(split(t_ref[...]), split(y[...])))


def update_kernel(
    orders, inner_upper, place_ref, a_ref, urh_ref, url_ref, uch_ref, ucl_ref, zc_ref, first_ref, second_ref, *refs
):
    inners, (out_ref, inner, zt, wh, wl) = refs[:4], refs[4:]
    b_at = pl.program_id(0)
    near = place_ref[1]
    ratio, nb, cols = zt.shape
    nc, half = first_ref.shape[:2]
    slots = nc // ratio
    tile = a_ref.shape[1]
    col_tiles = cols // tile

    @pl.when(b_at == 0)
    def _():
        for g in range(ratio):
            for s in range(slots):
                for side, (ref, masks) in enumerate(zip((first_ref, second_ref), orders)):
                    at = (2 * s + side) * half
                    zt[g, at : at + half, :] = ref[slot(g * slots + s, masks)]
        for r in range(4):
            for u in range(slots // 4):
                for side in range(2):
                    at = pl.multiple_of((2 * (u * 4 + (near ^ r)) + side) * half, half)
                    inner[pl.ds(at, half), :] = inners[r][slot(u, inner_upper), :, side * nb : (side + 1) * nb]
        wh[...], wl[...] = split(zc_ref[...] - dot3(split(inner[...]), (uch_ref[...], ucl_ref[...])))

    count = urh_ref.shape[0] // (ratio * tile)
    turned = []
    for b in range(count):
        at = pl.ds(pl.multiple_of((b_at * count + b) * tile, tile), tile)
        turned += [zt[g, :, at].T for g in range(ratio)]
    z = split(jnp.concatenate(turned, axis=0))
    total = dot3((urh_ref[...], url_ref[...]), (wh[...], wl[...])) + dot3(z, (uch_ref[...], ucl_ref[...]))
    for g in range(ratio * count):
        for b in range(col_tiles):
            line = pl.ds(g * tile * col_tiles + b, tile, stride=col_tiles)
            out_ref[line, :] = a_ref[line, :] - total[g * tile : (g + 1) * tile, b * tile : (b + 1) * tile]


def shape(*dims, dtype=F32):
    return jax.ShapeDtypeStruct(dims, dtype)


def per_device(trailing, reflectors, tfactor):
    row_tiles, _, tile, col_tiles = trailing.shape[:4]
    np_, nc = lax.axis_size("prow"), lax.axis_size("pcol")
    ratio = nc // np_
    ny = np_ // 2
    rows, cols = row_tiles * tile, col_tiles * tile
    nb = tfactor.shape[0]
    part = nb // np_
    half = row_tiles // 2
    block = trailing.reshape(rows * col_tiles, tile)
    mine = jnp.transpose(reflectors.reshape(row_tiles, tile, -1), (0, 2, 1))

    masks, cols_order = halving(nc), halving(np_)
    lead, rest = masks[: len(masks) - len(cols_order)], masks[len(masks) - len(cols_order) :]
    shift = len(cols_order)
    prow, pcol = lax.axis_index("prow").astype(jnp.int32), lax.axis_index("pcol").astype(jnp.int32)
    group = pcol >> shift
    where = {
        "place": jnp.stack([prow & 1, pcol & 3, group]),
        "group": group,
        "groups": [group ^ g for g in range(ratio)],
        "share": (pcol & (np_ - 1)) * part,
        "col": {mask: (pcol & mask) != 0 for mask in masks},
        "row": {mask: (prow & mask) != 0 for mask in cols_order},
        "half": {mask: [jnp.where((prow & mask) != 0, 1 - side, side) for side in range(2)] for mask in cols_order},
    }
    mine, where = lax.optimization_barrier((mine, where))
    place, group, col, row = where["place"], where["group"], where["col"], where["row"]
    scalar = pl.BlockSpec(memory_space=pltpu.SMEM)
    whole = pl.BlockSpec(memory_space=pltpu.VMEM)

    def flat(p, q):
        return p * nc + q

    def turn(values, g):
        perm = [
            (flat(p, h * np_ + s), flat(s, (h ^ g) * np_ + p)) for p in range(np_) for h in range(ratio) for s in range(np_)
        ]
        return lax.ppermute(values, BOTH, perm)

    upper = [mask // 4 for mask in masks[:-2]]
    inner_upper = [mask // 4 for mask in rest[:-2]]
    a_high, a_low, copy = pl.pallas_call(
        functools.partial(split_block_kernel, col_tiles, tile),
        out_shape=[shape(rows, cols, dtype=BF16)] * 2 + [shape(*mine.shape)],
        in_specs=[whole] * 2,
        out_specs=[whole] * 3,
        compiler_params=VMEM,
        cost_estimate=pl.CostEstimate(flops=rows * cols * 4, bytes_accessed=rows * cols * 8, transcendentals=0),
    )(block, mine)
    y = copy[None]
    for at, mask in enumerate(masks[:-2]):
        y = join(y, swap(mine[None] if at == 0 else y, "pcol", mask), col[mask])
    near_y = [y] + swap_three(y, "pcol")

    y_rows, keep, send = pl.pallas_call(
        functools.partial(product_kernel, upper),
        out_shape=[shape(row_tiles, nb, tile), shape(ny, part, cols), shape(ny, part, cols)],
        in_specs=[scalar] + [whole] * 6,
        out_specs=[whole] * 3,
        scratch_shapes=[pltpu.VMEM((nb, rows), BF16), pltpu.VMEM((nb, rows), BF16), pltpu.VMEM((nb, cols), F32)],
        compiler_params=VMEM,
        cost_estimate=pl.CostEstimate(flops=6 * nb * rows * cols, bytes_accessed=rows * cols * 8, transcendentals=0),
    )(place, a_high, a_low, *near_y)
    other = swap(send, "prow", 1)
    kept = keep + other
    y_piece = lax.dynamic_slice(
        y_rows.reshape(col_tiles, ratio, nb, tile), (0, group, where["share"], 0), (col_tiles, 1, part, tile)
    )
    y_piece = jnp.transpose(y_piece.reshape(col_tiles, part, tile), (1, 0, 2)).reshape(part, cols)
    y_piece, kept = lax.optimization_barrier((y_piece, kept))
    y_cols = turn(y_piece, 0).reshape(2, part // 2, cols)
    for mask in cols_order[:-1]:
        low, high = where["half"][mask]
        pair = kept.reshape(2, mask // 2, part, cols)
        kept = lax.dynamic_index_in_dim(pair, low, 0, keepdims=False)
        kept = kept + swap(lax.dynamic_index_in_dim(pair, high, 0, keepdims=False), "prow", mask)
    piece = kept.reshape(part, cols)

    arrived = [turn(piece, g) for g in range(ratio)]
    urh, url = pl.pallas_call(
        row_factor_kernel,
        out_shape=[shape(rows, nb, dtype=BF16)] * 2,
        in_specs=[whole] * 2,
        out_specs=[whole] * 2,
        compiler_params=VMEM,
        cost_estimate=pl.CostEstimate(flops=6 * nb * nb * rows, bytes_accessed=rows * nb * 8, transcendentals=0),
    )(tfactor, y_rows)
    arrived, urh, url = lax.optimization_barrier((arrived, urh, url))
    first, second, inner = pl.pallas_call(
        functools.partial(inner_kernel, ratio),
        out_shape=[shape(ratio, part // 2, cols)] * 2 + [shape(part // 2, 2 * nb)],
        in_specs=[scalar] + [whole] * (1 + ratio),
        out_specs=[whole] * 3,
        compiler_params=VMEM,
    )(place, y_rows, *arrived)
    for mask in cols_order:
        inner = inner + swap(inner, "prow", mask)
    inner = inner[None]
    for mask in rest[:-2]:
        first = join(first, swap(first, "pcol", mask), col[mask])
        second = join(second, swap(second, "pcol", mask), col[mask])
        inner = join(inner, swap(inner, "pcol", mask), col[mask])
    far, close = rest[-2:]
    orders = (lead + rest, lead + rest[:-2] + [close, far])
    first = join(first, swap(first, "pcol", far), col[far])
    second = join(second, swap(second, "pcol", close), col[close])
    first_came = swap(jnp.concatenate([first, inner]), "pcol", close)
    second_came = swap(jnp.concatenate([second, inner]), "pcol", far)
    blocks = first.shape[0]
    near_inner = [inner, first_came[blocks:], second_came[blocks:], swap(inner, "pcol", close + far)]
    first = join(first, first_came[:blocks], col[close])
    second = join(second, second_came[:blocks], col[far])

    columns = gather(jnp.concatenate([piece.reshape(2, part // 2, cols), y_cols]), "prow", cols_order, row)
    uch, ucl, zc = pl.pallas_call(
        functools.partial(column_factor_kernel, cols_order),
        out_shape=[shape(nb, cols, dtype=BF16)] * 2 + [shape(nb, cols)],
        in_specs=[whole] * 2,
        out_specs=[whole] * 3,
        scratch_shapes=[pltpu.VMEM((nb, cols), F32)],
        compiler_params=VMEM,
        cost_estimate=pl.CostEstimate(flops=6 * nb * nb * cols, bytes_accessed=cols * nb * 8, transcendentals=0),
    )(tfactor, columns)

    block_spec = pl.BlockSpec((rows * col_tiles // 2, tile), lambda i: (i, 0))
    row_spec = pl.BlockSpec((rows // 2, nb), lambda i: (i, 0))
    result = pl.pallas_call(
        functools.partial(update_kernel, orders, inner_upper),
        grid=(2,),
        out_shape=shape(rows * col_tiles, tile),
        in_specs=[scalar, block_spec, row_spec, row_spec] + [whole] * 9,
        out_specs=block_spec,
        scratch_shapes=[
            pltpu.VMEM((nb, nb), F32),
            pltpu.VMEM((ratio, nb, cols), F32),
            pltpu.VMEM((nb, cols), BF16),
            pltpu.VMEM((nb, cols), BF16),
        ],
        compiler_params=VMEM,
        cost_estimate=pl.CostEstimate(flops=12 * nb * rows * cols, bytes_accessed=rows * cols * 8, transcendentals=0),
    )(place, block, urh, url, uch, ucl, zc, first, second, *near_inner)
    return result.reshape(trailing.shape)


def solution(mesh):
    return jax.shard_map(
        per_device,
        mesh=mesh,
        in_specs=(P(None, "prow", None, None, "pcol", None), P(None, "prow", None, "pcol"), P()),
        out_specs=P(None, "prow", None, None, "pcol", None),
        check_vma=False,
    )
```

```python
import functools

import jax
import jax.numpy as jnp
from jax import lax
from jax.experimental import pallas as pl
from jax.experimental.pallas import tpu as pltpu
from jax.sharding import PartitionSpec as P

BOTH = ("prow", "pcol")
F32 = jnp.float32
BF16 = jnp.bfloat16
VMEM = pltpu.CompilerParams(vmem_limit_bytes=8 * 1024 * 1024)


def split(values):
    high = values.astype(BF16)
    return high, (values - high.astype(F32)).astype(BF16)


def dot(left, right, dims=((1,), (0,))):
    return lax.dot_general(left, right, (dims, ((), ())), preferred_element_type=F32)


def dot3(left, right, dims=((1,), (0,))):
    (lh, ll), (rh, rl) = left, right
    return dot(lh, rh, dims) + (dot(lh, rl, dims) + dot(ll, rh, dims))


def swap(values, axis, mask):
    n = lax.axis_size(axis)
    return lax.ppermute(values, axis, [(i, i ^ mask) for i in range(n)])


def halving(n):
    masks = []
    while n > 1:
        n //= 2
        masks.append(n)
    return masks


def join(values, other, high):
    pair = jnp.stack([jnp.where(high, other, values), jnp.where(high, values, other)])
    return pair.reshape((-1,) + values.shape[1:])


def gather(values, axis, masks, above):
    values = values[None]
    for mask in masks:
        values = join(values, swap(values, axis, mask), above[mask])
    return values


def slot(index, masks):
    return sum(1 << j for j, mask in enumerate(masks) if index & mask)


def swap_three(values, axis):
    return [swap(values, axis, mask) for mask in (1, 2, 3)]


def split_block_kernel(col_tiles, tile, a_ref, high_ref, low_ref):
    rows = high_ref.shape[0]
    for b in range(col_tiles):
        cols = slice(b * tile, (b + 1) * tile)
        high, low = split(a_ref[pl.ds(b, rows, stride=col_tiles), :])
        high_ref[:, cols] = high
        low_ref[:, cols] = low


def product_kernel(orders, ah_ref, al_ref, first_ref, second_ref, y_ref, keep_ref, send_ref, yh, yl, total):
    nc, half, width, tile = first_ref.shape
    for chunk, (ref, masks) in enumerate(zip((first_ref, second_ref), orders)):
        for a in range(half):
            at = chunk * half + a
            for j in range(nc):
                y_ref[at, j * width : (j + 1) * width, :] = ref[slot(j, masks), a]
            cols = slice(at * tile, (at + 1) * tile)
            yh[:, cols], yl[:, cols] = split(y_ref[at])
    total[...] = dot3((yh[...], yl[...]), (ah_ref[...], al_ref[...]))
    core = lax.axis_index("prow") & 1
    count, part = keep_ref.shape[:2]
    for y in range(count):
        keep_ref[y] = total[pl.ds(pl.multiple_of((2 * y + core) * part, part), part), :]
        send_ref[y] = total[pl.ds(pl.multiple_of((2 * y + 1 - core) * part, part), part), :]


def inner_kernel(count, shift, y_ref, *refs):
    came, (first_ref, second_ref, inner_ref) = refs[:count], refs[count:]
    row_tiles, nb, tile = y_ref.shape
    part, cols = came[0].shape
    half = part // 2
    group = lax.axis_index("pcol") >> shift
    inner = jnp.zeros((part, nb), F32)
    for g, ref in enumerate(came):
        at = group ^ g
        first_ref[at] = ref[:half, :]
        second_ref[at] = ref[half:, :]
        for b in range(cols // tile):
            left = split(ref[:, b * tile : (b + 1) * tile])
            inner += dot3(left, split(y_ref[b * count + at]), ((1,), (1,)))
    for side in range(2):
        inner_ref[:, side * nb : (side + 1) * nb] = inner[side * half : (side + 1) * half]


def row_factor_kernel(t_ref, y_ref, high_ref, low_ref):
    row_tiles, nb, tile = y_ref.shape
    factor = split(t_ref[...])
    for a in range(row_tiles):
        rows = slice(a * tile, (a + 1) * tile)
        high_ref[rows, :], low_ref[rows, :] = split(dot3(factor, split(y_ref[a])).T)


def column_factor_kernel(order, t_ref, cols_ref, high_ref, low_ref, z_ref, y):
    slots, _, half, _ = cols_ref.shape
    for s in range(slots):
        for side in range(2):
            rows = slice((2 * s + side) * half, (2 * s + side + 1) * half)
            z_ref[rows, :] = cols_ref[slot(s, order), side]
            y[rows, :] = cols_ref[slot(s, order), 2 + side]
    high_ref[...], low_ref[...] = split(dot3(split(t_ref[...]), split(y[...])))


def update_kernel(
    orders, inner_upper, a_ref, urh_ref, url_ref, uch_ref, ucl_ref, zc_ref, first_ref, second_ref, *refs
):
    inners, (out_ref, inner, zt, block, result, read, write) = refs[:4], refs[4:]
    near = lax.axis_index("pcol") & 3
    ratio, nb, cols = zt.shape
    nc, half = first_ref.shape[:2]
    slots = nc // ratio
    chunks, lines, tile = block.shape
    col_tiles = cols // tile
    reads = [pltpu.make_async_copy(a_ref.at[pl.ds(i * lines, lines)], block.at[i], read.at[i]) for i in range(chunks)]
    writes = [pltpu.make_async_copy(result.at[i], out_ref.at[pl.ds(i * lines, lines)], write.at[i]) for i in range(chunks)]
    for copy in reads:
        copy.start()
    for g in range(ratio):
        for s in range(slots):
            for side, (ref, masks) in enumerate(zip((first_ref, second_ref), orders)):
                at = (2 * s + side) * half
                zt[g, at : at + half, :] = ref[slot(g * slots + s, masks)]
    for r in range(4):
        for u in range(slots // 4):
            for side in range(2):
                at = pl.multiple_of((2 * (u * 4 + (near ^ r)) + side) * half, half)
                inner[pl.ds(at, half), :] = inners[r][slot(u, inner_upper), :, side * nb : (side + 1) * nb]
    uc = (uch_ref[...], ucl_ref[...])
    w = split(zc_ref[...] - dot3(split(inner[...]), uc))
    rows = lines // col_tiles
    count = rows // (ratio * tile)
    for i in range(chunks):
        at = slice(i * rows, (i + 1) * rows)
        turned = [zt[g, :, b * tile : (b + 1) * tile].T for b in range(i * count, (i + 1) * count) for g in range(ratio)]
        total = dot3(split(jnp.concatenate(turned, axis=0)), uc) + dot3((urh_ref[at, :], url_ref[at, :]), w)
        reads[i].wait()
        for g in range(ratio * count):
            for b in range(col_tiles):
                line = pl.ds(g * tile * col_tiles + b, tile, stride=col_tiles)
                result[i, line, :] = block[i, line, :] - total[g * tile : (g + 1) * tile, b * tile : (b + 1) * tile]
        writes[i].start()
    for copy in writes:
        copy.wait()


def shape(*dims, dtype=F32):
    return jax.ShapeDtypeStruct(dims, dtype)


def per_device(trailing, reflectors, tfactor):
    row_tiles, _, tile, col_tiles = trailing.shape[:4]
    np_, nc = lax.axis_size("prow"), lax.axis_size("pcol")
    ratio = nc // np_
    ny = np_ // 2
    rows, cols = row_tiles * tile, col_tiles * tile
    nb = tfactor.shape[0]
    part = nb // np_
    half = row_tiles // 2
    block = trailing.reshape(rows * col_tiles, tile)
    mine = jnp.transpose(reflectors.reshape(row_tiles, tile, -1), (0, 2, 1))

    masks, cols_order = halving(nc), halving(np_)
    lead, rest = masks[: len(masks) - len(cols_order)], masks[len(masks) - len(cols_order) :]
    shift = len(cols_order)
    prow, pcol = lax.axis_index("prow").astype(jnp.int32), lax.axis_index("pcol").astype(jnp.int32)
    group = pcol >> shift
    where = {
        "group": group,
        "groups": [group ^ g for g in range(ratio)],
        "share": (pcol & (np_ - 1)) * part,
        "col": {mask: (pcol & mask) != 0 for mask in masks},
        "row": {mask: (prow & mask) != 0 for mask in cols_order},
        "half": {mask: [jnp.where((prow & mask) != 0, 1 - side, side) for side in range(2)] for mask in cols_order},
    }
    mine, where = lax.optimization_barrier((mine, where))
    group, col, row = where["group"], where["col"], where["row"]
    whole = pl.BlockSpec(memory_space=pltpu.VMEM)

    def flat(p, q):
        return p * nc + q

    def turn(values, g):
        perm = [
            (flat(p, h * np_ + s), flat(s, (h ^ g) * np_ + p)) for p in range(np_) for h in range(ratio) for s in range(np_)
        ]
        return lax.ppermute(values, BOTH, perm)

    inner_upper = [mask // 4 for mask in rest[:-2]]
    far, close = rest[-2:]
    orders = (masks, masks[:-2] + [close, far])
    a_high, a_low = pl.pallas_call(
        functools.partial(split_block_kernel, col_tiles, tile),
        out_shape=[shape(rows, cols, dtype=BF16)] * 2,
        in_specs=[whole],
        out_specs=[whole] * 2,
        compiler_params=VMEM,
        cost_estimate=pl.CostEstimate(flops=rows * cols * 4, bytes_accessed=rows * cols * 8, transcendentals=0),
    )(block)
    first, second = lax.optimization_barrier(mine[None, :half]), lax.optimization_barrier(mine[None, half:])
    for at, (mask, other) in enumerate(zip(*orders)):
        first_came, second_came = swap(first, "pcol", mask), swap(second, "pcol", other)
        if at == 0:
            second_came, a_high, a_low = lax.optimization_barrier((second_came, a_high, a_low))
        first, second = join(first, first_came, col[mask]), join(second, second_came, col[other])

    y_rows, keep, send = pl.pallas_call(
        functools.partial(product_kernel, orders),
        out_shape=[shape(row_tiles, nb, tile), shape(ny, part, cols), shape(ny, part, cols)],
        in_specs=[whole] * 4,
        out_specs=[whole] * 3,
        scratch_shapes=[pltpu.VMEM((nb, rows), BF16), pltpu.VMEM((nb, rows), BF16), pltpu.VMEM((nb, cols), F32)],
        compiler_params=VMEM,
        cost_estimate=pl.CostEstimate(flops=6 * nb * rows * cols, bytes_accessed=rows * cols * 8, transcendentals=0),
    )(a_high, a_low, first, second)
    other = swap(send, "prow", 1)
    kept = keep + other
    y_piece = lax.dynamic_slice(
        y_rows.reshape(col_tiles, ratio, nb, tile), (0, group, where["share"], 0), (col_tiles, 1, part, tile)
    )
    y_piece = jnp.transpose(y_piece.reshape(col_tiles, part, tile), (1, 0, 2)).reshape(part, cols)
    y_cols = turn(y_piece, 0).reshape(2, part // 2, cols)
    for mask in cols_order[:-1]:
        low, high = where["half"][mask]
        pair = kept.reshape(2, mask // 2, part, cols)
        kept = lax.dynamic_index_in_dim(pair, low, 0, keepdims=False)
        kept = kept + swap(lax.dynamic_index_in_dim(pair, high, 0, keepdims=False), "prow", mask)
    piece, y_cols = lax.optimization_barrier((kept.reshape(part, cols), y_cols))

    arrived = [turn(piece, g) for g in range(ratio)]
    urh, url = pl.pallas_call(
        row_factor_kernel,
        out_shape=[shape(rows, nb, dtype=BF16)] * 2,
        in_specs=[whole] * 2,
        out_specs=[whole] * 2,
        compiler_params=VMEM,
        cost_estimate=pl.CostEstimate(flops=6 * nb * nb * rows, bytes_accessed=rows * nb * 8, transcendentals=0),
    )(tfactor, y_rows)
    arrived, urh, url = lax.optimization_barrier((arrived, urh, url))
    first, second, inner = pl.pallas_call(
        functools.partial(inner_kernel, ratio, shift),
        out_shape=[shape(ratio, part // 2, cols)] * 2 + [shape(part // 2, 2 * nb)],
        in_specs=[whole] * (1 + ratio),
        out_specs=[whole] * 3,
        compiler_params=VMEM,
    )(y_rows, *arrived)
    columns = jnp.concatenate([piece.reshape(2, part // 2, cols), y_cols])
    for mask in cols_order:
        inner = inner + swap(inner, "prow", mask)
        if mask == cols_order[-2]:
            columns, inner = lax.optimization_barrier((columns, inner))
    inner = inner[None]
    for mask in rest[:-2]:
        first = join(first, swap(first, "pcol", mask), col[mask])
        second = join(second, swap(second, "pcol", mask), col[mask])
        inner = join(inner, swap(inner, "pcol", mask), col[mask])
    first = join(first, swap(first, "pcol", far), col[far])
    second = join(second, swap(second, "pcol", close), col[close])
    first_came = swap(jnp.concatenate([first, inner]), "pcol", close)
    second_came = swap(jnp.concatenate([second, inner]), "pcol", far)
    blocks = first.shape[0]
    near_inner = [inner, first_came[blocks:], second_came[blocks:], swap(inner, "pcol", close + far)]
    first = join(first, first_came[:blocks], col[close])
    second = join(second, second_came[:blocks], col[far])

    columns = gather(columns, "prow", cols_order, row)
    uch, ucl, zc = pl.pallas_call(
        functools.partial(column_factor_kernel, cols_order),
        out_shape=[shape(nb, cols, dtype=BF16)] * 2 + [shape(nb, cols)],
        in_specs=[whole] * 2,
        out_specs=[whole] * 3,
        scratch_shapes=[pltpu.VMEM((nb, cols), F32)],
        compiler_params=VMEM,
        cost_estimate=pl.CostEstimate(flops=6 * nb * nb * cols, bytes_accessed=cols * nb * 8, transcendentals=0),
    )(tfactor, columns)

    chunks = 4
    lines = rows * col_tiles // chunks
    outside = pl.BlockSpec(memory_space=pltpu.HBM)
    result = pl.pallas_call(
        functools.partial(update_kernel, orders, inner_upper),
        out_shape=shape(rows * col_tiles, tile),
        in_specs=[outside] + [whole] * 11,
        out_specs=outside,
        scratch_shapes=[
            pltpu.VMEM((nb, nb), F32),
            pltpu.VMEM((ratio, nb, cols), F32),
            pltpu.VMEM((chunks, lines, tile), F32),
            pltpu.VMEM((chunks, lines, tile), F32),
            pltpu.SemaphoreType.DMA((chunks,)),
            pltpu.SemaphoreType.DMA((chunks,)),
        ],
        compiler_params=VMEM,
        cost_estimate=pl.CostEstimate(flops=12 * nb * rows * cols, bytes_accessed=rows * cols * 8, transcendentals=0),
    )(block, urh, url, uch, ucl, zc, first, second, *near_inner)
    return result.reshape(trailing.shape)


def solution(mesh):
    return jax.shard_map(
        per_device,
        mesh=mesh,
        in_specs=(P(None, "prow", None, None, "pcol", None), P(None, "prow", None, "pcol"), P()),
        out_specs=P(None, "prow", None, None, "pcol", None),
        check_vma=False,
    )
```

```python
import functools

import jax
import jax.numpy as jnp
from jax import lax
from jax.experimental import pallas as pl
from jax.experimental.pallas import tpu as pltpu
from jax.sharding import PartitionSpec as P

BOTH = ("prow", "pcol")
F32 = jnp.float32
BF16 = jnp.bfloat16
VMEM = pltpu.CompilerParams(vmem_limit_bytes=8 * 1024 * 1024)


def split(values):
    high = values.astype(BF16)
    return high, (values - high.astype(F32)).astype(BF16)


def dot(left, right, dims=((1,), (0,))):
    return lax.dot_general(left, right, (dims, ((), ())), preferred_element_type=F32)


def dot3(left, right, dims=((1,), (0,))):
    (lh, ll), (rh, rl) = left, right
    return dot(lh, rh, dims) + (dot(lh, rl, dims) + dot(ll, rh, dims))


def swap(values, axis, mask):
    n = lax.axis_size(axis)
    return lax.ppermute(values, axis, [(i, i ^ mask) for i in range(n)])


def halving(n):
    masks = []
    while n > 1:
        n //= 2
        masks.append(n)
    return masks


def join(values, other, high):
    pair = jnp.stack([jnp.where(high, other, values), jnp.where(high, values, other)])
    return pair.reshape((-1,) + values.shape[1:])


def gather(values, axis, masks, above):
    values = values[None]
    for mask in masks:
        values = join(values, swap(values, axis, mask), above[mask])
    return values


def slot(index, masks):
    return sum(1 << j for j, mask in enumerate(masks) if index & mask)


def swap_three(values, axis):
    return [swap(values, axis, mask) for mask in (1, 2, 3)]


def split_block_kernel(col_tiles, tile, a_ref, high_ref, low_ref):
    rows = high_ref.shape[0]
    for b in range(col_tiles):
        cols = slice(b * tile, (b + 1) * tile)
        high, low = split(a_ref[pl.ds(b, rows, stride=col_tiles), :])
        high_ref[:, cols] = high
        low_ref[:, cols] = low


def product_kernel(orders, ah_ref, al_ref, first_ref, second_ref, y_ref, keep_ref, send_ref, yh, yl, total):
    nc, half, width, tile = first_ref.shape
    for chunk, (ref, masks) in enumerate(zip((first_ref, second_ref), orders)):
        for a in range(half):
            at = chunk * half + a
            for j in range(nc):
                y_ref[at, j * width : (j + 1) * width, :] = ref[slot(j, masks), a]
            cols = slice(at * tile, (at + 1) * tile)
            yh[:, cols], yl[:, cols] = split(y_ref[at])
    total[...] = dot3((yh[...], yl[...]), (ah_ref[...], al_ref[...]))
    core = lax.axis_index("prow") & 1
    count, part = keep_ref.shape[:2]
    for y in range(count):
        keep_ref[y] = total[pl.ds(pl.multiple_of((2 * y + core) * part, part), part), :]
        send_ref[y] = total[pl.ds(pl.multiple_of((2 * y + 1 - core) * part, part), part), :]


def inner_kernel(shift, piece_ref, y_ref, inner_ref):
    row_tiles, nb, tile = y_ref.shape
    part, cols = piece_ref.shape
    col_tiles = cols // tile
    half = part // 2
    group = lax.axis_index("pcol") >> shift
    inner = jnp.zeros((part, nb), F32)
    for b in range(col_tiles):
        left = split(piece_ref[:, b * tile : (b + 1) * tile])
        inner += dot3(left, split(y_ref[b * (row_tiles // col_tiles) + group]), ((1,), (1,)))
    for side in range(2):
        inner_ref[:, side * nb : (side + 1) * nb] = inner[side * half : (side + 1) * half]


def row_factor_kernel(t_ref, y_ref, high_ref, low_ref):
    row_tiles, nb, tile = y_ref.shape
    factor = split(t_ref[...])
    for a in range(row_tiles):
        rows = slice(a * tile, (a + 1) * tile)
        high_ref[rows, :], low_ref[rows, :] = split(dot3(factor, split(y_ref[a])).T)


def column_factor_kernel(order, t_ref, cols_ref, high_ref, low_ref, z_ref, y):
    slots, _, half, _ = cols_ref.shape
    for s in range(slots):
        for side in range(2):
            rows = slice((2 * s + side) * half, (2 * s + side + 1) * half)
            z_ref[rows, :] = cols_ref[slot(s, order), side]
            y[rows, :] = cols_ref[slot(s, order), 2 + side]
    high_ref[...], low_ref[...] = split(dot3(split(t_ref[...]), split(y[...])))


def update_kernel(
    orders, inner_upper, a_ref, urh_ref, url_ref, uch_ref, ucl_ref, zc_ref, first_ref, second_ref, *refs
):
    inners, (out_ref, inner, zt, block, result, read, write) = refs[:4], refs[4:]
    near = lax.axis_index("pcol") & 3
    ratio, nb, cols = zt.shape
    nc, half = first_ref.shape[:2]
    slots = nc // ratio
    chunks, lines, tile = block.shape
    col_tiles = cols // tile
    reads = [pltpu.make_async_copy(a_ref.at[pl.ds(i * lines, lines)], block.at[i], read.at[i]) for i in range(chunks)]
    writes = [pltpu.make_async_copy(result.at[i], out_ref.at[pl.ds(i * lines, lines)], write.at[i]) for i in range(chunks)]
    for copy in reads:
        copy.start()
    for g in range(ratio):
        for s in range(slots):
            for side, (ref, masks) in enumerate(zip((first_ref, second_ref), orders)):
                at = (2 * s + side) * half
                zt[g, at : at + half, :] = ref[slot(g * slots + s, masks)]
    for r in range(4):
        for u in range(slots // 4):
            for side in range(2):
                at = pl.multiple_of((2 * (u * 4 + (near ^ r)) + side) * half, half)
                inner[pl.ds(at, half), :] = inners[r][slot(u, inner_upper), :, side * nb : (side + 1) * nb]
    uc = (uch_ref[...], ucl_ref[...])
    w = split(zc_ref[...] - dot3(split(inner[...]), uc))
    rows = lines // col_tiles
    count = rows // (ratio * tile)
    for i in range(chunks):
        at = slice(i * rows, (i + 1) * rows)
        turned = [zt[g, :, b * tile : (b + 1) * tile].T for b in range(i * count, (i + 1) * count) for g in range(ratio)]
        total = dot3(split(jnp.concatenate(turned, axis=0)), uc) + dot3((urh_ref[at, :], url_ref[at, :]), w)
        reads[i].wait()
        for g in range(ratio * count):
            for b in range(col_tiles):
                line = pl.ds(g * tile * col_tiles + b, tile, stride=col_tiles)
                result[i, line, :] = block[i, line, :] - total[g * tile : (g + 1) * tile, b * tile : (b + 1) * tile]
        writes[i].start()
    for copy in writes:
        copy.wait()


def shape(*dims, dtype=F32):
    return jax.ShapeDtypeStruct(dims, dtype)


def per_device(trailing, reflectors, tfactor):
    row_tiles, _, tile, col_tiles = trailing.shape[:4]
    np_, nc = lax.axis_size("prow"), lax.axis_size("pcol")
    ratio = nc // np_
    ny = np_ // 2
    rows, cols = row_tiles * tile, col_tiles * tile
    nb = tfactor.shape[0]
    part = nb // np_
    half = row_tiles // 2
    block = trailing.reshape(rows * col_tiles, tile)
    mine = jnp.transpose(reflectors.reshape(row_tiles, tile, -1), (0, 2, 1))

    masks, cols_order = halving(nc), halving(np_)
    lead, rest = masks[: len(masks) - len(cols_order)], masks[len(masks) - len(cols_order) :]
    shift = len(cols_order)
    prow, pcol = lax.axis_index("prow").astype(jnp.int32), lax.axis_index("pcol").astype(jnp.int32)
    group = pcol >> shift
    where = {
        "group": group,
        "share": (pcol & (np_ - 1)) * part,
        "col": {mask: (pcol & mask) != 0 for mask in masks},
        "row": {mask: (prow & mask) != 0 for mask in cols_order},
        "half": {mask: [jnp.where((prow & mask) != 0, 1 - side, side) for side in range(2)] for mask in cols_order},
    }
    mine, where = lax.optimization_barrier((mine, where))
    group, col, row = where["group"], where["col"], where["row"]
    whole = pl.BlockSpec(memory_space=pltpu.VMEM)

    def flat(p, q):
        return p * nc + q

    def turn(values):
        perm = [
            (flat(p, g * np_ + s), flat(s, g * np_ + p)) for p in range(np_) for g in range(ratio) for s in range(np_)
        ]
        return lax.ppermute(values, BOTH, perm)

    inner_upper = [mask // 4 for mask in rest[:-2]]
    far, close = rest[-2:]
    orders = (masks, masks[:-2] + [close, far])
    a_high, a_low = pl.pallas_call(
        functools.partial(split_block_kernel, col_tiles, tile),
        out_shape=[shape(rows, cols, dtype=BF16)] * 2,
        in_specs=[whole],
        out_specs=[whole] * 2,
        compiler_params=VMEM,
        cost_estimate=pl.CostEstimate(flops=rows * cols * 4, bytes_accessed=rows * cols * 8, transcendentals=0),
    )(block)
    first, second = lax.optimization_barrier(mine[None, :half]), lax.optimization_barrier(mine[None, half:])
    for at, (mask, other) in enumerate(zip(*orders)):
        first_came, second_came = swap(first, "pcol", mask), swap(second, "pcol", other)
        if at == 0:
            second_came, a_high, a_low = lax.optimization_barrier((second_came, a_high, a_low))
        first, second = join(first, first_came, col[mask]), join(second, second_came, col[other])

    y_rows, keep, send = pl.pallas_call(
        functools.partial(product_kernel, orders),
        out_shape=[shape(row_tiles, nb, tile), shape(ny, part, cols), shape(ny, part, cols)],
        in_specs=[whole] * 4,
        out_specs=[whole] * 3,
        scratch_shapes=[pltpu.VMEM((nb, rows), BF16), pltpu.VMEM((nb, rows), BF16), pltpu.VMEM((nb, cols), F32)],
        compiler_params=VMEM,
        cost_estimate=pl.CostEstimate(flops=6 * nb * rows * cols, bytes_accessed=rows * cols * 8, transcendentals=0),
    )(a_high, a_low, first, second)
    other = swap(send, "prow", 1)
    kept = keep + other
    y_piece = lax.dynamic_slice(
        y_rows.reshape(col_tiles, ratio, nb, tile), (0, group, where["share"], 0), (col_tiles, 1, part, tile)
    )
    y_piece = jnp.transpose(y_piece.reshape(col_tiles, part, tile), (1, 0, 2)).reshape(part, cols)
    for mask in cols_order[:-1]:
        low, high = where["half"][mask]
        pair = kept.reshape(2, mask // 2, part, cols)
        kept = lax.dynamic_index_in_dim(pair, low, 0, keepdims=False)
        kept = kept + swap(lax.dynamic_index_in_dim(pair, high, 0, keepdims=False), "prow", mask)
    piece = kept.reshape(part, cols)

    turned = turn(piece)
    y_cols = turn(y_piece).reshape(2, part // 2, cols)
    urh, url = pl.pallas_call(
        row_factor_kernel,
        out_shape=[shape(rows, nb, dtype=BF16)] * 2,
        in_specs=[whole] * 2,
        out_specs=[whole] * 2,
        compiler_params=VMEM,
        cost_estimate=pl.CostEstimate(flops=6 * nb * nb * rows, bytes_accessed=rows * nb * 8, transcendentals=0),
    )(tfactor, y_rows)
    turned, urh, url = lax.optimization_barrier((turned, urh, url))
    inner = pl.pallas_call(
        functools.partial(inner_kernel, shift),
        out_shape=shape(part // 2, 2 * nb),
        in_specs=[whole] * 2,
        out_specs=whole,
        compiler_params=VMEM,
        cost_estimate=pl.CostEstimate(flops=6 * nb * part * cols, bytes_accessed=cols * nb * 4, transcendentals=0),
    )(turned, y_rows)
    first, second = turned[None, : part // 2], turned[None, part // 2 :]
    first, second = lax.optimization_barrier(first), lax.optimization_barrier(second)
    for mask in lead + rest[:-2]:
        first = join(first, swap(first, "pcol", mask), col[mask])
        second = join(second, swap(second, "pcol", mask), col[mask])
    first = join(first, swap(first, "pcol", far), col[far])
    second = join(second, swap(second, "pcol", close), col[close])

    columns = jnp.concatenate([piece.reshape(2, part // 2, cols), y_cols])
    for mask in cols_order[::-1]:
        inner = inner + swap(inner, "prow", mask)
        if mask == 1:
            columns, inner = lax.optimization_barrier((columns, inner))
    for mask in lead:
        inner = inner + swap(inner, "pcol", mask)
    inner = inner[None]
    for mask in rest[:-2]:
        inner = join(inner, swap(inner, "pcol", mask), col[mask])
    first_came = swap(jnp.concatenate([first, inner]), "pcol", close)
    second_came = swap(jnp.concatenate([second, inner]), "pcol", far)
    blocks = first.shape[0]
    near_inner = [inner, first_came[blocks:], second_came[blocks:], swap(inner, "pcol", close + far)]
    first = join(first, first_came[:blocks], col[close])
    second = join(second, second_came[:blocks], col[far])

    columns = gather(columns, "prow", cols_order, row)
    uch, ucl, zc = pl.pallas_call(
        functools.partial(column_factor_kernel, cols_order),
        out_shape=[shape(nb, cols, dtype=BF16)] * 2 + [shape(nb, cols)],
        in_specs=[whole] * 2,
        out_specs=[whole] * 3,
        scratch_shapes=[pltpu.VMEM((nb, cols), F32)],
        compiler_params=VMEM,
        cost_estimate=pl.CostEstimate(flops=6 * nb * nb * cols, bytes_accessed=cols * nb * 8, transcendentals=0),
    )(tfactor, columns)

    chunks = 4
    lines = rows * col_tiles // chunks
    outside = pl.BlockSpec(memory_space=pltpu.HBM)
    result = pl.pallas_call(
        functools.partial(update_kernel, orders, inner_upper),
        out_shape=shape(rows * col_tiles, tile),
        in_specs=[outside] + [whole] * 11,
        out_specs=outside,
        scratch_shapes=[
            pltpu.VMEM((nb, nb), F32),
            pltpu.VMEM((ratio, nb, cols), F32),
            pltpu.VMEM((chunks, lines, tile), F32),
            pltpu.VMEM((chunks, lines, tile), F32),
            pltpu.SemaphoreType.DMA((chunks,)),
            pltpu.SemaphoreType.DMA((chunks,)),
        ],
        compiler_params=VMEM,
        cost_estimate=pl.CostEstimate(flops=12 * nb * rows * cols, bytes_accessed=rows * cols * 8, transcendentals=0),
    )(block, urh, url, uch, ucl, zc, first, second, *near_inner)
    return result.reshape(trailing.shape)


def solution(mesh):
    return jax.shard_map(
        per_device,
        mesh=mesh,
        in_specs=(P(None, "prow", None, None, "pcol", None), P(None, "prow", None, "pcol"), P()),
        out_specs=P(None, "prow", None, None, "pcol", None),
        check_vma=False,
    )
```

```python
import functools

import jax
import jax.numpy as jnp
from jax import lax
from jax.experimental import pallas as pl
from jax.experimental.pallas import tpu as pltpu
from jax.sharding import PartitionSpec as P

BOTH = ("prow", "pcol")
F32 = jnp.float32
BF16 = jnp.bfloat16
VMEM = pltpu.CompilerParams(vmem_limit_bytes=8 * 1024 * 1024)


def split(values):
    high = values.astype(BF16)
    return high, (values - high.astype(F32)).astype(BF16)


def dot(left, right, dims=((1,), (0,))):
    return lax.dot_general(left, right, (dims, ((), ())), preferred_element_type=F32)


def dot3(left, right, dims=((1,), (0,))):
    (lh, ll), (rh, rl) = left, right
    return dot(lh, rh, dims) + (dot(lh, rl, dims) + dot(ll, rh, dims))


def swap(values, axis, mask):
    n = lax.axis_size(axis)
    return lax.ppermute(values, axis, [(i, i ^ mask) for i in range(n)])


def halving(n):
    masks = []
    while n > 1:
        n //= 2
        masks.append(n)
    return masks


def join(values, other, high):
    pair = jnp.stack([jnp.where(high, other, values), jnp.where(high, values, other)])
    return pair.reshape((-1,) + values.shape[1:])


def gather(values, axis, masks, above):
    values = values[None]
    for mask in masks:
        values = join(values, swap(values, axis, mask), above[mask])
    return values


def slot(index, masks):
    return sum(1 << j for j, mask in enumerate(masks) if index & mask)


def swap_three(values, axis):
    return [swap(values, axis, mask) for mask in (1, 2, 3)]


def split_block_kernel(col_tiles, tile, a_ref, high_ref, low_ref):
    rows = high_ref.shape[0]
    for b in range(col_tiles):
        cols = slice(b * tile, (b + 1) * tile)
        high, low = split(a_ref[pl.ds(b, rows, stride=col_tiles), :])
        high_ref[:, cols] = high
        low_ref[:, cols] = low


def product_kernel(orders, ah_ref, al_ref, first_ref, second_ref, y_ref, keep_ref, send_ref, yh, yl, total):
    nc, half, width, tile = first_ref.shape
    for chunk, (ref, masks) in enumerate(zip((first_ref, second_ref), orders)):
        for a in range(half):
            at = chunk * half + a
            for j in range(nc):
                y_ref[at, j * width : (j + 1) * width, :] = ref[slot(j, masks), a]
            cols = slice(at * tile, (at + 1) * tile)
            yh[:, cols], yl[:, cols] = split(y_ref[at])
    total[...] = dot3((yh[...], yl[...]), (ah_ref[...], al_ref[...]))
    core = lax.axis_index("prow") & 1
    count, part = keep_ref.shape[:2]
    for y in range(count):
        keep_ref[y] = total[pl.ds(pl.multiple_of((2 * y + core) * part, part), part), :]
        send_ref[y] = total[pl.ds(pl.multiple_of((2 * y + 1 - core) * part, part), part), :]


def inner_kernel(shift, piece_ref, y_ref, inner_ref):
    row_tiles, nb, tile = y_ref.shape
    part, cols = piece_ref.shape
    col_tiles = cols // tile
    half = part // 2
    group = lax.axis_index("pcol") >> shift
    inner = jnp.zeros((part, nb), F32)
    for b in range(col_tiles):
        left = split(piece_ref[:, b * tile : (b + 1) * tile])
        inner += dot3(left, split(y_ref[b * (row_tiles // col_tiles) + group]), ((1,), (1,)))
    for side in range(2):
        inner_ref[:, side * nb : (side + 1) * nb] = inner[side * half : (side + 1) * half]


def stack_left(values):
    high, low = split(values)
    return jnp.concatenate([high, high, low], axis=1)


def stack_right(ref, values):
    rows = values.shape[0]
    high, low = split(values)
    ref[:rows, :] = high
    ref[rows : 2 * rows, :] = low
    ref[2 * rows :, :] = high


def row_factor_kernel(t_ref, y_ref, out_ref):
    row_tiles, nb, tile = y_ref.shape
    factor = split(t_ref[...])
    for a in range(row_tiles):
        out_ref[a * tile : (a + 1) * tile, :] = stack_left(dot3(factor, split(y_ref[a])).T)


def column_factor_kernel(order, t_ref, cols_ref, out_ref, z_ref, y):
    slots, _, half, _ = cols_ref.shape
    for s in range(slots):
        for side in range(2):
            rows = slice((2 * s + side) * half, (2 * s + side + 1) * half)
            z_ref[rows, :] = cols_ref[slot(s, order), side]
            y[rows, :] = cols_ref[slot(s, order), 2 + side]
    stack_right(out_ref, dot3(split(t_ref[...]), split(y[...])))


def update_kernel(
    orders, inner_upper, a_ref, ur_ref, uc_ref, zc_ref, first_ref, second_ref, *refs
):
    inners, (out_ref, inner, w, zt, block, result, read, write) = refs[:4], refs[4:]
    near = lax.axis_index("pcol") & 3
    ratio, nb, cols = zt.shape
    nc, half = first_ref.shape[:2]
    slots = nc // ratio
    chunks, lines, tile = block.shape
    col_tiles = cols // tile
    reads = [pltpu.make_async_copy(a_ref.at[pl.ds(i * lines, lines)], block.at[i], read.at[i]) for i in range(chunks)]
    writes = [pltpu.make_async_copy(result.at[i], out_ref.at[pl.ds(i * lines, lines)], write.at[i]) for i in range(chunks)]
    for copy in reads:
        copy.start()
    for g in range(ratio):
        for s in range(slots):
            for side, (ref, masks) in enumerate(zip((first_ref, second_ref), orders)):
                at = (2 * s + side) * half
                zt[g, at : at + half, :] = ref[slot(g * slots + s, masks)]
    for r in range(4):
        for u in range(slots // 4):
            for side in range(2):
                at = pl.multiple_of((2 * (u * 4 + (near ^ r)) + side) * half, half)
                inner[pl.ds(at, half), :] = inners[r][slot(u, inner_upper), :, side * nb : (side + 1) * nb]
    stack_right(w, zc_ref[...] - dot3(split(inner[...]), (uc_ref[:nb, :], uc_ref[nb : 2 * nb, :])))
    rows = lines // col_tiles
    count = rows // (ratio * tile)
    for i in range(chunks):
        at = slice(i * rows, (i + 1) * rows)
        turned = [zt[g, :, b * tile : (b + 1) * tile].T for b in range(i * count, (i + 1) * count) for g in range(ratio)]
        total = dot(stack_left(jnp.concatenate(turned, axis=0)), uc_ref[...]) + dot(ur_ref[at, :], w[...])
        reads[i].wait()
        for g in range(ratio * count):
            for b in range(col_tiles):
                line = pl.ds(g * tile * col_tiles + b, tile, stride=col_tiles)
                result[i, line, :] = block[i, line, :] - total[g * tile : (g + 1) * tile, b * tile : (b + 1) * tile]
        writes[i].start()
    for copy in writes:
        copy.wait()


def shape(*dims, dtype=F32):
    return jax.ShapeDtypeStruct(dims, dtype)


def per_device(trailing, reflectors, tfactor):
    row_tiles, _, tile, col_tiles = trailing.shape[:4]
    np_, nc = lax.axis_size("prow"), lax.axis_size("pcol")
    ratio = nc // np_
    ny = np_ // 2
    rows, cols = row_tiles * tile, col_tiles * tile
    nb = tfactor.shape[0]
    part = nb // np_
    half = row_tiles // 2
    block = trailing.reshape(rows * col_tiles, tile)
    mine = jnp.transpose(reflectors.reshape(row_tiles, tile, -1), (0, 2, 1))

    masks, cols_order = halving(nc), halving(np_)
    lead, rest = masks[: len(masks) - len(cols_order)], masks[len(masks) - len(cols_order) :]
    shift = len(cols_order)
    prow, pcol = lax.axis_index("prow").astype(jnp.int32), lax.axis_index("pcol").astype(jnp.int32)
    group = pcol >> shift
    where = {
        "group": group,
        "rounds": [(prow >> 1) ^ r for r in range(ny)],
        "share": (pcol & (np_ - 1)) * part,
        "col": {mask: (pcol & mask) != 0 for mask in masks},
        "row": {mask: (prow & mask) != 0 for mask in cols_order},
        "half": {mask: [jnp.where((prow & mask) != 0, 1 - side, side) for side in range(2)] for mask in cols_order},
    }
    mine, where = lax.optimization_barrier((mine, where))
    group, col, row = where["group"], where["col"], where["row"]
    whole = pl.BlockSpec(memory_space=pltpu.VMEM)

    def flat(p, q):
        return p * nc + q

    def turn(values, r):
        perm = [
            (flat(p, g * np_ + s), flat(s, g * np_ + (p ^ r))) for p in range(np_) for g in range(ratio) for s in range(np_)
        ]
        return lax.ppermute(values, BOTH, perm)

    inner_upper = [mask // 4 for mask in rest[:-2]]
    far, close = rest[-2:]
    orders = (masks, masks[:-2] + [close, far])
    a_high, a_low = pl.pallas_call(
        functools.partial(split_block_kernel, col_tiles, tile),
        out_shape=[shape(rows, cols, dtype=BF16)] * 2,
        in_specs=[whole],
        out_specs=[whole] * 2,
        compiler_params=VMEM,
        cost_estimate=pl.CostEstimate(flops=rows * cols * 4, bytes_accessed=rows * cols * 8, transcendentals=0),
    )(block)
    first, second = lax.optimization_barrier(mine[None, :half]), lax.optimization_barrier(mine[None, half:])
    for at, (mask, other) in enumerate(zip(*orders)):
        first_came, second_came = swap(first, "pcol", mask), swap(second, "pcol", other)
        if at == 0:
            second_came, a_high, a_low = lax.optimization_barrier((second_came, a_high, a_low))
        first, second = join(first, first_came, col[mask]), join(second, second_came, col[other])

    y_rows, keep, send = pl.pallas_call(
        functools.partial(product_kernel, orders),
        out_shape=[shape(row_tiles, nb, tile), shape(ny, part, cols), shape(ny, part, cols)],
        in_specs=[whole] * 4,
        out_specs=[whole] * 3,
        scratch_shapes=[pltpu.VMEM((nb, rows), BF16), pltpu.VMEM((nb, rows), BF16), pltpu.VMEM((nb, cols), F32)],
        compiler_params=VMEM,
        cost_estimate=pl.CostEstimate(flops=6 * nb * rows * cols, bytes_accessed=rows * cols * 8, transcendentals=0),
    )(a_high, a_low, first, second)
    other = swap(send, "prow", 1)
    kept = keep + other
    y_piece = lax.dynamic_slice(
        y_rows.reshape(col_tiles, ratio, nb, tile), (0, group, where["share"], 0), (col_tiles, 1, part, tile)
    )
    y_piece = jnp.transpose(y_piece.reshape(col_tiles, part, tile), (1, 0, 2)).reshape(part, cols)

    turned = []
    for r in range(ny):
        message = lax.dynamic_index_in_dim(kept, where["rounds"][r], 0, keepdims=False)
        turned.append(turn(message, 2 * r))
    turned = sum(turned[1:], turned[0])
    kept = lax.optimization_barrier(kept)
    for mask in cols_order[:-1]:
        low, high = where["half"][mask]
        pair = kept.reshape(2, mask // 2, part, cols)
        kept = lax.dynamic_index_in_dim(pair, low, 0, keepdims=False)
        kept = kept + swap(lax.dynamic_index_in_dim(pair, high, 0, keepdims=False), "prow", mask)
    piece = kept.reshape(part, cols)
    y_cols = turn(y_piece, 0).reshape(2, part // 2, cols)
    u_rows = pl.pallas_call(
        row_factor_kernel,
        out_shape=shape(rows, 3 * nb, dtype=BF16),
        in_specs=[whole] * 2,
        out_specs=whole,
        compiler_params=VMEM,
        cost_estimate=pl.CostEstimate(flops=6 * nb * nb * rows, bytes_accessed=rows * nb * 8, transcendentals=0),
    )(tfactor, y_rows)
    turned, u_rows = lax.optimization_barrier((turned, u_rows))
    inner = pl.pallas_call(
        functools.partial(inner_kernel, shift),
        out_shape=shape(part // 2, 2 * nb),
        in_specs=[whole] * 2,
        out_specs=whole,
        compiler_params=VMEM,
        cost_estimate=pl.CostEstimate(flops=6 * nb * part * cols, bytes_accessed=cols * nb * 4, transcendentals=0),
    )(turned, y_rows)
    first, second = turned[None, : part // 2], turned[None, part // 2 :]
    first, second = lax.optimization_barrier(first), lax.optimization_barrier(second)
    for mask in lead:
        first = join(first, swap(first, "pcol", mask), col[mask])
        came = swap(jnp.concatenate([second, inner[None]]), "pcol", mask)
        second, inner = join(second, came[:-1], col[mask]), inner + came[-1]
    for mask in rest[:-2]:
        first = join(first, swap(first, "pcol", mask), col[mask])
        second = join(second, swap(second, "pcol", mask), col[mask])
    first = join(first, swap(first, "pcol", far), col[far])
    second = join(second, swap(second, "pcol", close), col[close])

    columns = jnp.concatenate([piece.reshape(2, part // 2, cols), y_cols])
    for mask in cols_order[::-1]:
        inner = inner + swap(inner, "prow", mask)
        if mask == 1:
            columns, inner = lax.optimization_barrier((columns, inner))
    inner = inner[None]
    for mask in rest[:-2]:
        inner = join(inner, swap(inner, "pcol", mask), col[mask])
    first_came = swap(jnp.concatenate([first, inner]), "pcol", close)
    second_came = swap(jnp.concatenate([second, inner]), "pcol", far)
    blocks = first.shape[0]
    near_inner = [inner, first_came[blocks:], second_came[blocks:], swap(inner, "pcol", close + far)]
    first = join(first, first_came[:blocks], col[close])
    second = join(second, second_came[:blocks], col[far])

    columns = gather(columns, "prow", cols_order, row)
    u_cols, zc = pl.pallas_call(
        functools.partial(column_factor_kernel, cols_order),
        out_shape=[shape(3 * nb, cols, dtype=BF16), shape(nb, cols)],
        in_specs=[whole] * 2,
        out_specs=[whole] * 2,
        scratch_shapes=[pltpu.VMEM((nb, cols), F32)],
        compiler_params=VMEM,
        cost_estimate=pl.CostEstimate(flops=6 * nb * nb * cols, bytes_accessed=cols * nb * 8, transcendentals=0),
    )(tfactor, columns)

    chunks = 4
    lines = rows * col_tiles // chunks
    outside = pl.BlockSpec(memory_space=pltpu.HBM)
    result = pl.pallas_call(
        functools.partial(update_kernel, orders, inner_upper),
        out_shape=shape(rows * col_tiles, tile),
        in_specs=[outside] + [whole] * 9,
        out_specs=outside,
        scratch_shapes=[
            pltpu.VMEM((nb, nb), F32),
            pltpu.VMEM((3 * nb, cols), BF16),
            pltpu.VMEM((ratio, nb, cols), F32),
            pltpu.VMEM((chunks, lines, tile), F32),
            pltpu.VMEM((chunks, lines, tile), F32),
            pltpu.SemaphoreType.DMA((chunks,)),
            pltpu.SemaphoreType.DMA((chunks,)),
        ],
        compiler_params=VMEM,
        cost_estimate=pl.CostEstimate(flops=12 * nb * rows * cols, bytes_accessed=rows * cols * 8, transcendentals=0),
    )(block, u_rows, u_cols, zc, first, second, *near_inner)
    return result.reshape(trailing.shape)


def solution(mesh):
    return jax.shard_map(
        per_device,
        mesh=mesh,
        in_specs=(P(None, "prow", None, None, "pcol", None), P(None, "prow", None, "pcol"), P()),
        out_specs=P(None, "prow", None, None, "pcol", None),
        check_vma=False,
    )
```

```python
import functools

import jax
import jax.numpy as jnp
from jax import lax
from jax.experimental import pallas as pl
from jax.experimental.pallas import tpu as pltpu
from jax.sharding import PartitionSpec as P

BOTH = ("prow", "pcol")
F32 = jnp.float32
BF16 = jnp.bfloat16
VMEM = pltpu.CompilerParams(vmem_limit_bytes=8 * 1024 * 1024)


def split(values):
    high = values.astype(BF16)
    return high, (values - high.astype(F32)).astype(BF16)


def dot(left, right, dims=((1,), (0,))):
    return lax.dot_general(left, right, (dims, ((), ())), preferred_element_type=F32)


def dot3(left, right, dims=((1,), (0,))):
    (lh, ll), (rh, rl) = left, right
    return dot(lh, rh, dims) + (dot(lh, rl, dims) + dot(ll, rh, dims))


def swap(values, axis, mask):
    n = lax.axis_size(axis)
    return lax.ppermute(values, axis, [(i, i ^ mask) for i in range(n)])


def halving(n):
    masks = []
    while n > 1:
        n //= 2
        masks.append(n)
    return masks


def join(values, other, high):
    pair = jnp.stack([jnp.where(high, other, values), jnp.where(high, values, other)])
    return pair.reshape((-1,) + values.shape[1:])


def gather(values, axis, masks, above):
    values = values[None]
    for mask in masks:
        values = join(values, swap(values, axis, mask), above[mask])
    return values


def slot(index, masks):
    return sum(1 << j for j, mask in enumerate(masks) if index & mask)


def swap_three(values, axis):
    return [swap(values, axis, mask) for mask in (1, 2, 3)]


def split_block_kernel(col_tiles, tile, a_ref, high_ref, low_ref):
    rows = high_ref.shape[0]
    for b in range(col_tiles):
        cols = slice(b * tile, (b + 1) * tile)
        high, low = split(a_ref[pl.ds(b, rows, stride=col_tiles), :])
        high_ref[:, cols] = high
        low_ref[:, cols] = low


def product_kernel(orders, ah_ref, al_ref, first_ref, second_ref, y_ref, keep_ref, send_ref, yh, yl, total):
    nc, half, width, tile = first_ref.shape
    for chunk, (ref, masks) in enumerate(zip((first_ref, second_ref), orders)):
        for a in range(half):
            at = chunk * half + a
            for j in range(nc):
                y_ref[at, j * width : (j + 1) * width, :] = ref[slot(j, masks), a]
            cols = slice(at * tile, (at + 1) * tile)
            yh[:, cols], yl[:, cols] = split(y_ref[at])
    total[...] = dot3((yh[...], yl[...]), (ah_ref[...], al_ref[...]))
    core = lax.axis_index("prow") & 1
    count, part = keep_ref.shape[:2]
    for y in range(count):
        keep_ref[y] = total[pl.ds(pl.multiple_of((2 * y + core) * part, part), part), :]
        send_ref[y] = total[pl.ds(pl.multiple_of((2 * y + 1 - core) * part, part), part), :]


def inner_kernel(shift, piece_ref, y_ref, inner_ref):
    row_tiles, nb, tile = y_ref.shape
    part, cols = piece_ref.shape
    col_tiles = cols // tile
    half = part // 2
    group = lax.axis_index("pcol") >> shift
    inner = jnp.zeros((part, nb), F32)
    for b in range(col_tiles):
        left = split(piece_ref[:, b * tile : (b + 1) * tile])
        inner += dot3(left, split(y_ref[b * (row_tiles // col_tiles) + group]), ((1,), (1,)))
    for side in range(2):
        inner_ref[:, side * nb : (side + 1) * nb] = inner[side * half : (side + 1) * half]


def stack_left(values):
    high, low = split(values)
    return jnp.concatenate([high, high, low], axis=1)


def stack_right(ref, values):
    rows = values.shape[0]
    high, low = split(values)
    ref[:rows, :] = high
    ref[rows : 2 * rows, :] = low
    ref[2 * rows :, :] = high


def row_factor_kernel(t_ref, y_ref, out_ref):
    row_tiles, nb, tile = y_ref.shape
    factor = split(t_ref[...])
    for a in range(row_tiles):
        out_ref[a * tile : (a + 1) * tile, :] = stack_left(dot3(factor, split(y_ref[a])).T)


def column_factor_kernel(order, t_ref, cols_ref, out_ref, z_ref, y):
    slots, _, half, _ = cols_ref.shape
    for s in range(slots):
        for side in range(2):
            rows = slice((2 * s + side) * half, (2 * s + side + 1) * half)
            z_ref[rows, :] = cols_ref[slot(s, order), side]
            y[rows, :] = cols_ref[slot(s, order), 2 + side]
    stack_right(out_ref, dot3(split(t_ref[...]), split(y[...])))


def update_kernel(
    orders, inner_upper, a_ref, ur_ref, uc_ref, zc_ref, first_ref, second_ref, *refs
):
    inners, (out_ref, inner, w, zt, result, write) = refs[:4], refs[4:]
    near = lax.axis_index("pcol") & 3
    ratio, nb, cols = zt.shape
    nc, half = first_ref.shape[:2]
    slots = nc // ratio
    chunks, lines, tile = result.shape
    col_tiles = cols // tile
    writes = [pltpu.make_async_copy(result.at[i], out_ref.at[pl.ds(i * lines, lines)], write.at[i]) for i in range(chunks)]
    for g in range(ratio):
        for s in range(slots):
            for side, (ref, masks) in enumerate(zip((first_ref, second_ref), orders)):
                at = (2 * s + side) * half
                zt[g, at : at + half, :] = ref[slot(g * slots + s, masks)]
    for r in range(4):
        for u in range(slots // 4):
            for side in range(2):
                at = pl.multiple_of((2 * (u * 4 + (near ^ r)) + side) * half, half)
                inner[pl.ds(at, half), :] = inners[r][slot(u, inner_upper), :, side * nb : (side + 1) * nb]
    stack_right(w, zc_ref[...] - dot3(split(inner[...]), (uc_ref[:nb, :], uc_ref[nb : 2 * nb, :])))
    rows = lines // col_tiles
    count = rows // (ratio * tile)
    for i in range(chunks):
        at = slice(i * rows, (i + 1) * rows)
        turned = [zt[g, :, b * tile : (b + 1) * tile].T for b in range(i * count, (i + 1) * count) for g in range(ratio)]
        total = dot(stack_left(jnp.concatenate(turned, axis=0)), uc_ref[...]) + dot(ur_ref[at, :], w[...])
        for g in range(ratio * count):
            for b in range(col_tiles):
                at = g * tile * col_tiles + b
                values = a_ref[pl.ds(i * lines + at, tile, stride=col_tiles), :]
                result[i, pl.ds(at, tile, stride=col_tiles), :] = values - total[g * tile : (g + 1) * tile, b * tile : (b + 1) * tile]
        writes[i].start()
    for copy in writes:
        copy.wait()


def shape(*dims, dtype=F32):
    return jax.ShapeDtypeStruct(dims, dtype)


def per_device(trailing, reflectors, tfactor):
    row_tiles, _, tile, col_tiles = trailing.shape[:4]
    np_, nc = lax.axis_size("prow"), lax.axis_size("pcol")
    ratio = nc // np_
    ny = np_ // 2
    rows, cols = row_tiles * tile, col_tiles * tile
    nb = tfactor.shape[0]
    part = nb // np_
    half = row_tiles // 2
    block = trailing.reshape(rows * col_tiles, tile)
    mine = jnp.transpose(reflectors.reshape(row_tiles, tile, -1), (0, 2, 1))

    masks, cols_order = halving(nc), halving(np_)
    lead, rest = masks[: len(masks) - len(cols_order)], masks[len(masks) - len(cols_order) :]
    shift = len(cols_order)
    prow, pcol = lax.axis_index("prow").astype(jnp.int32), lax.axis_index("pcol").astype(jnp.int32)
    group = pcol >> shift
    where = {
        "group": group,
        "rounds": [(prow >> 1) ^ r for r in range(ny)],
        "share": (pcol & (np_ - 1)) * part,
        "col": {mask: (pcol & mask) != 0 for mask in masks},
        "row": {mask: (prow & mask) != 0 for mask in cols_order},
        "half": {mask: [jnp.where((prow & mask) != 0, 1 - side, side) for side in range(2)] for mask in cols_order},
    }
    mine, where = lax.optimization_barrier((mine, where))
    group, col, row = where["group"], where["col"], where["row"]
    whole = pl.BlockSpec(memory_space=pltpu.VMEM)

    def flat(p, q):
        return p * nc + q

    def turn(values, r):
        perm = [
            (flat(p, g * np_ + s), flat(s, g * np_ + (p ^ r))) for p in range(np_) for g in range(ratio) for s in range(np_)
        ]
        return lax.ppermute(values, BOTH, perm)

    inner_upper = [mask // 4 for mask in rest[:-2]]
    far, close = rest[-2:]
    orders = (masks, masks[:-2] + [close, far])
    a_high, a_low = pl.pallas_call(
        functools.partial(split_block_kernel, col_tiles, tile),
        out_shape=[shape(rows, cols, dtype=BF16)] * 2,
        in_specs=[whole],
        out_specs=[whole] * 2,
        compiler_params=VMEM,
        cost_estimate=pl.CostEstimate(flops=rows * cols * 4, bytes_accessed=rows * cols * 8, transcendentals=0),
    )(block)
    first, second = lax.optimization_barrier(mine[None, :half]), lax.optimization_barrier(mine[None, half:])
    for at, (mask, other) in enumerate(zip(*orders)):
        first_came, second_came = swap(first, "pcol", mask), swap(second, "pcol", other)
        if at == 0:
            second_came, a_high, a_low = lax.optimization_barrier((second_came, a_high, a_low))
        first, second = join(first, first_came, col[mask]), join(second, second_came, col[other])

    y_rows, keep, send = pl.pallas_call(
        functools.partial(product_kernel, orders),
        out_shape=[shape(row_tiles, nb, tile), shape(ny, part, cols), shape(ny, part, cols)],
        in_specs=[whole] * 4,
        out_specs=[whole] * 3,
        scratch_shapes=[pltpu.VMEM((nb, rows), BF16), pltpu.VMEM((nb, rows), BF16), pltpu.VMEM((nb, cols), F32)],
        compiler_params=VMEM,
        cost_estimate=pl.CostEstimate(flops=6 * nb * rows * cols, bytes_accessed=rows * cols * 8, transcendentals=0),
    )(a_high, a_low, first, second)
    other = swap(send, "prow", 1)
    kept = keep + other
    y_piece = lax.dynamic_slice(
        y_rows.reshape(col_tiles, ratio, nb, tile), (0, group, where["share"], 0), (col_tiles, 1, part, tile)
    )
    y_piece = jnp.transpose(y_piece.reshape(col_tiles, part, tile), (1, 0, 2)).reshape(part, cols)

    turned = []
    for r in range(ny):
        message = lax.dynamic_index_in_dim(kept, where["rounds"][r], 0, keepdims=False)
        turned.append(turn(message, 2 * r))
    turned = sum(turned[1:], turned[0])
    kept = lax.optimization_barrier(kept)
    for mask in cols_order[:-1]:
        low, high = where["half"][mask]
        pair = kept.reshape(2, mask // 2, part, cols)
        kept = lax.dynamic_index_in_dim(pair, low, 0, keepdims=False)
        kept = kept + swap(lax.dynamic_index_in_dim(pair, high, 0, keepdims=False), "prow", mask)
    piece = kept.reshape(part, cols)
    y_cols = turn(y_piece, 0).reshape(2, part // 2, cols)
    u_rows = pl.pallas_call(
        row_factor_kernel,
        out_shape=shape(rows, 3 * nb, dtype=BF16),
        in_specs=[whole] * 2,
        out_specs=whole,
        compiler_params=VMEM,
        cost_estimate=pl.CostEstimate(flops=6 * nb * nb * rows, bytes_accessed=rows * nb * 8, transcendentals=0),
    )(tfactor, y_rows)
    turned, u_rows = lax.optimization_barrier((turned, u_rows))
    inner = pl.pallas_call(
        functools.partial(inner_kernel, shift),
        out_shape=shape(part // 2, 2 * nb),
        in_specs=[whole] * 2,
        out_specs=whole,
        compiler_params=VMEM,
        cost_estimate=pl.CostEstimate(flops=6 * nb * part * cols, bytes_accessed=cols * nb * 4, transcendentals=0),
    )(turned, y_rows)
    first, second = turned[None, : part // 2], turned[None, part // 2 :]
    first, second = lax.optimization_barrier(first), lax.optimization_barrier(second)
    columns = jnp.concatenate([piece.reshape(2, part // 2, cols), y_cols])
    for mask in lead:
        first = join(first, swap(first, "pcol", mask), col[mask])
        first, columns = lax.optimization_barrier((first, columns))
        came = swap(jnp.concatenate([second, inner[None]]), "pcol", mask)
        second, inner = join(second, came[:-1], col[mask]), inner + came[-1]
    for mask in rest[:-2]:
        first = join(first, swap(first, "pcol", mask), col[mask])
        second = join(second, swap(second, "pcol", mask), col[mask])
    first = join(first, swap(first, "pcol", far), col[far])
    second = join(second, swap(second, "pcol", close), col[close])
    first, inner = lax.optimization_barrier((first, inner))

    for mask in cols_order[::-1]:
        inner = inner + swap(inner, "prow", mask)
    inner = inner[None]
    for mask in rest[:-2]:
        inner = join(inner, swap(inner, "pcol", mask), col[mask])
    near_inner = [inner] + [swap(inner, "pcol", mask) for mask in (close, far, close + far)]
    first = join(first, swap(first, "pcol", close), col[close])
    second = join(second, swap(second, "pcol", far), col[far])

    columns = gather(columns, "prow", cols_order, row)
    u_cols, zc = pl.pallas_call(
        functools.partial(column_factor_kernel, cols_order),
        out_shape=[shape(3 * nb, cols, dtype=BF16), shape(nb, cols)],
        in_specs=[whole] * 2,
        out_specs=[whole] * 2,
        scratch_shapes=[pltpu.VMEM((nb, cols), F32)],
        compiler_params=VMEM,
        cost_estimate=pl.CostEstimate(flops=6 * nb * nb * cols, bytes_accessed=cols * nb * 8, transcendentals=0),
    )(tfactor, columns)

    chunks = 4
    lines = rows * col_tiles // chunks
    outside = pl.BlockSpec(memory_space=pltpu.HBM)
    result = pl.pallas_call(
        functools.partial(update_kernel, orders, inner_upper),
        out_shape=shape(rows * col_tiles, tile),
        in_specs=[whole] * 10,
        out_specs=outside,
        scratch_shapes=[
            pltpu.VMEM((nb, nb), F32),
            pltpu.VMEM((3 * nb, cols), BF16),
            pltpu.VMEM((ratio, nb, cols), F32),
            pltpu.VMEM((chunks, lines, tile), F32),
            pltpu.SemaphoreType.DMA((chunks,)),
        ],
        compiler_params=VMEM,
        cost_estimate=pl.CostEstimate(flops=12 * nb * rows * cols, bytes_accessed=rows * cols * 8, transcendentals=0),
    )(block, u_rows, u_cols, zc, first, second, *near_inner)
    return result.reshape(trailing.shape)


def solution(mesh):
    return jax.shard_map(
        per_device,
        mesh=mesh,
        in_specs=(P(None, "prow", None, None, "pcol", None), P(None, "prow", None, "pcol"), P()),
        out_specs=P(None, "prow", None, None, "pcol", None),
        check_vma=False,
    )
```

```python
import functools

import jax
import jax.numpy as jnp
from jax import lax
from jax.experimental import pallas as pl
from jax.experimental.pallas import tpu as pltpu
from jax.sharding import PartitionSpec as P

BOTH = ("prow", "pcol")
F32 = jnp.float32
BF16 = jnp.bfloat16
VMEM = pltpu.CompilerParams(vmem_limit_bytes=8 * 1024 * 1024)


def split(values):
    high = values.astype(BF16)
    return high, (values - high.astype(F32)).astype(BF16)


def dot(left, right, dims=((1,), (0,))):
    return lax.dot_general(left, right, (dims, ((), ())), preferred_element_type=F32)


def dot3(left, right, dims=((1,), (0,))):
    (lh, ll), (rh, rl) = left, right
    return dot(lh, rh, dims) + (dot(lh, rl, dims) + dot(ll, rh, dims))


def swap(values, axis, mask):
    n = lax.axis_size(axis)
    return lax.ppermute(values, axis, [(i, i ^ mask) for i in range(n)])


def halving(n):
    masks = []
    while n > 1:
        n //= 2
        masks.append(n)
    return masks


def join(values, other, high):
    pair = jnp.stack([jnp.where(high, other, values), jnp.where(high, values, other)])
    return pair.reshape((-1,) + values.shape[1:])


def gather(values, axis, masks, above):
    values = values[None]
    for mask in masks:
        values = join(values, swap(values, axis, mask), above[mask])
    return values


def slot(index, masks):
    return sum(1 << j for j, mask in enumerate(masks) if index & mask)


def swap_three(values, axis):
    return [swap(values, axis, mask) for mask in (1, 2, 3)]


def split_block_kernel(col_tiles, tile, a_ref, high_ref, low_ref):
    rows = high_ref.shape[0]
    for b in range(col_tiles):
        cols = slice(b * tile, (b + 1) * tile)
        high, low = split(a_ref[pl.ds(b, rows, stride=col_tiles), :])
        high_ref[:, cols] = high
        low_ref[:, cols] = low


def product_kernel(orders, ah_ref, al_ref, first_ref, second_ref, y_ref, keep_ref, send_ref, yh, yl, total):
    nc, half, width, tile = first_ref.shape
    for chunk, (ref, masks) in enumerate(zip((first_ref, second_ref), orders)):
        for a in range(half):
            at = chunk * half + a
            for j in range(nc):
                y_ref[at, j * width : (j + 1) * width, :] = ref[slot(j, masks), a]
            cols = slice(at * tile, (at + 1) * tile)
            yh[:, cols], yl[:, cols] = split(y_ref[at])
    total[...] = dot3((yh[...], yl[...]), (ah_ref[...], al_ref[...]))
    core = lax.axis_index("prow") & 1
    count, part = keep_ref.shape[:2]
    for y in range(count):
        keep_ref[y] = total[pl.ds(pl.multiple_of((2 * y + core) * part, part), part), :]
        send_ref[y] = total[pl.ds(pl.multiple_of((2 * y + 1 - core) * part, part), part), :]


def inner_kernel(first_ref, second_ref, y_ref, inner_ref):
    row_tiles, nb, tile = y_ref.shape
    ratio, half, cols = first_ref.shape
    inner = jnp.zeros((2 * half, nb), F32)
    for g in range(ratio):
        for b in range(cols // tile):
            at = slice(b * tile, (b + 1) * tile)
            left = jnp.concatenate([first_ref[g, :, at], second_ref[g, :, at]], axis=0)
            inner += dot3(split(left), split(y_ref[b * ratio + g]), ((1,), (1,)))
    for side in range(2):
        inner_ref[:, side * nb : (side + 1) * nb] = inner[side * half : (side + 1) * half]


def stack_left(values):
    high, low = split(values)
    return jnp.concatenate([high, high, low], axis=1)


def stack_right(ref, values):
    rows = values.shape[0]
    high, low = split(values)
    ref[:rows, :] = high
    ref[rows : 2 * rows, :] = low
    ref[2 * rows :, :] = high


def row_factor_kernel(t_ref, y_ref, out_ref):
    row_tiles, nb, tile = y_ref.shape
    factor = split(t_ref[...])
    for a in range(row_tiles):
        out_ref[a * tile : (a + 1) * tile, :] = stack_left(dot3(factor, split(y_ref[a])).T)


def column_factor_kernel(order, t_ref, cols_ref, out_ref, z_ref, y):
    slots, _, half, _ = cols_ref.shape
    for s in range(slots):
        for side in range(2):
            rows = slice((2 * s + side) * half, (2 * s + side + 1) * half)
            z_ref[rows, :] = cols_ref[slot(s, order), side]
            y[rows, :] = cols_ref[slot(s, order), 2 + side]
    stack_right(out_ref, dot3(split(t_ref[...]), split(y[...])))


def update_kernel(
    orders, inner_upper, a_ref, ur_ref, uc_ref, zc_ref, first_ref, second_ref, *refs
):
    inners, (out_ref, inner, w, zt, result, write) = refs[:4], refs[4:]
    near = lax.axis_index("pcol") & 3
    ratio, nb, cols = zt.shape
    nc, half = first_ref.shape[:2]
    slots = nc // ratio
    chunks, lines, tile = result.shape
    col_tiles = cols // tile
    writes = [pltpu.make_async_copy(result.at[i], out_ref.at[pl.ds(i * lines, lines)], write.at[i]) for i in range(chunks)]
    for g in range(ratio):
        for s in range(slots):
            for side, (ref, masks) in enumerate(zip((first_ref, second_ref), orders)):
                at = (2 * s + side) * half
                zt[g, at : at + half, :] = ref[slot(g * slots + s, masks)]
    for r in range(4):
        for u in range(slots // 4):
            for side in range(2):
                at = pl.multiple_of((2 * (u * 4 + (near ^ r)) + side) * half, half)
                inner[pl.ds(at, half), :] = inners[r][slot(u, inner_upper), :, side * nb : (side + 1) * nb]
    stack_right(w, zc_ref[...] - dot3(split(inner[...]), (uc_ref[:nb, :], uc_ref[nb : 2 * nb, :])))
    rows = lines // col_tiles
    count = rows // (ratio * tile)
    for i in range(chunks):
        at = slice(i * rows, (i + 1) * rows)
        turned = [zt[g, :, b * tile : (b + 1) * tile].T for b in range(i * count, (i + 1) * count) for g in range(ratio)]
        total = dot(stack_left(jnp.concatenate(turned, axis=0)), uc_ref[...]) + dot(ur_ref[at, :], w[...])
        for g in range(ratio * count):
            for b in range(col_tiles):
                at = g * tile * col_tiles + b
                values = a_ref[pl.ds(i * lines + at, tile, stride=col_tiles), :]
                result[i, pl.ds(at, tile, stride=col_tiles), :] = values - total[g * tile : (g + 1) * tile, b * tile : (b + 1) * tile]
        writes[i].start()
    for copy in writes:
        copy.wait()


def shape(*dims, dtype=F32):
    return jax.ShapeDtypeStruct(dims, dtype)


def per_device(trailing, reflectors, tfactor):
    row_tiles, _, tile, col_tiles = trailing.shape[:4]
    np_, nc = lax.axis_size("prow"), lax.axis_size("pcol")
    ratio = nc // np_
    ny = np_ // 2
    rows, cols = row_tiles * tile, col_tiles * tile
    nb = tfactor.shape[0]
    part = nb // np_
    half = row_tiles // 2
    block = trailing.reshape(rows * col_tiles, tile)
    mine = jnp.transpose(reflectors.reshape(row_tiles, tile, -1), (0, 2, 1))

    masks, cols_order = halving(nc), halving(np_)
    lead, rest = masks[: len(masks) - len(cols_order)], masks[len(masks) - len(cols_order) :]
    shift = len(cols_order)
    prow, pcol = lax.axis_index("prow").astype(jnp.int32), lax.axis_index("pcol").astype(jnp.int32)
    group = pcol >> shift
    where = {
        "group": group,
        "rounds": [(prow >> 1) ^ r for r in range(ny)],
        "share": (pcol & (np_ - 1)) * part,
        "col": {mask: (pcol & mask) != 0 for mask in masks},
        "row": {mask: (prow & mask) != 0 for mask in cols_order},
        "half": {mask: [jnp.where((prow & mask) != 0, 1 - side, side) for side in range(2)] for mask in cols_order},
    }
    mine, where = lax.optimization_barrier((mine, where))
    group, col, row = where["group"], where["col"], where["row"]
    whole = pl.BlockSpec(memory_space=pltpu.VMEM)

    def flat(p, q):
        return p * nc + q

    def turn(values, r):
        perm = [
            (flat(p, g * np_ + s), flat(s, g * np_ + (p ^ r))) for p in range(np_) for g in range(ratio) for s in range(np_)
        ]
        return lax.ppermute(values, BOTH, perm)

    inner_upper = [mask // 4 for mask in rest[:-2]]
    far, close = rest[-2:]
    orders = (masks, masks[:-2] + [close, far])
    a_high, a_low = pl.pallas_call(
        functools.partial(split_block_kernel, col_tiles, tile),
        out_shape=[shape(rows, cols, dtype=BF16)] * 2,
        in_specs=[whole],
        out_specs=[whole] * 2,
        compiler_params=VMEM,
        cost_estimate=pl.CostEstimate(flops=rows * cols * 4, bytes_accessed=rows * cols * 8, transcendentals=0),
    )(block)
    first, second = lax.optimization_barrier(mine[None, :half]), lax.optimization_barrier(mine[None, half:])
    for at, (mask, other) in enumerate(zip(*orders)):
        first_came, second_came = swap(first, "pcol", mask), swap(second, "pcol", other)
        if at == 0:
            second_came, a_high, a_low = lax.optimization_barrier((second_came, a_high, a_low))
        first, second = join(first, first_came, col[mask]), join(second, second_came, col[other])

    y_rows, keep, send = pl.pallas_call(
        functools.partial(product_kernel, orders),
        out_shape=[shape(row_tiles, nb, tile), shape(ny, part, cols), shape(ny, part, cols)],
        in_specs=[whole] * 4,
        out_specs=[whole] * 3,
        scratch_shapes=[pltpu.VMEM((nb, rows), BF16), pltpu.VMEM((nb, rows), BF16), pltpu.VMEM((nb, cols), F32)],
        compiler_params=VMEM,
        cost_estimate=pl.CostEstimate(flops=6 * nb * rows * cols, bytes_accessed=rows * cols * 8, transcendentals=0),
    )(a_high, a_low, first, second)
    other = swap(send, "prow", 1)
    kept = keep + other
    y_piece = lax.dynamic_slice(
        y_rows.reshape(col_tiles, ratio, nb, tile), (0, group, where["share"], 0), (col_tiles, 1, part, tile)
    )
    y_piece = jnp.transpose(y_piece.reshape(col_tiles, part, tile), (1, 0, 2)).reshape(part, cols)

    turned = []
    for r in range(ny):
        message = lax.dynamic_index_in_dim(kept, where["rounds"][r], 0, keepdims=False)
        turned.append(turn(message, 2 * r))
    turned = sum(turned[1:], turned[0])
    y_piece, kept = lax.optimization_barrier((y_piece, kept))
    for mask in cols_order[:-1]:
        low, high = where["half"][mask]
        pair = kept.reshape(2, mask // 2, part, cols)
        kept = lax.dynamic_index_in_dim(pair, low, 0, keepdims=False)
        kept = kept + swap(lax.dynamic_index_in_dim(pair, high, 0, keepdims=False), "prow", mask)
    piece = kept.reshape(part, cols)
    y_cols = turn(y_piece, 0).reshape(2, part // 2, cols)
    u_rows = pl.pallas_call(
        row_factor_kernel,
        out_shape=shape(rows, 3 * nb, dtype=BF16),
        in_specs=[whole] * 2,
        out_specs=whole,
        compiler_params=VMEM,
        cost_estimate=pl.CostEstimate(flops=6 * nb * nb * rows, bytes_accessed=rows * nb * 8, transcendentals=0),
    )(tfactor, y_rows)
    turned, u_rows = lax.optimization_barrier((turned, u_rows))
    first, second = turned[None, : part // 2], turned[None, part // 2 :]
    first, second = lax.optimization_barrier(first), lax.optimization_barrier(second)
    columns = jnp.concatenate([piece.reshape(2, part // 2, cols), y_cols])
    for mask in lead:
        first = join(first, swap(first, "pcol", mask), col[mask])
        second = join(second, swap(second, "pcol", mask), col[mask])
    first, columns = lax.optimization_barrier((first, columns))
    first_group, second_group = first, second
    for mask in rest[:-2]:
        first = join(first, swap(first, "pcol", mask), col[mask])
        second = join(second, swap(second, "pcol", mask), col[mask])
    first = join(first, swap(first, "pcol", far), col[far])
    second = join(second, swap(second, "pcol", close), col[close])

    columns = gather(columns, "prow", cols_order, row)
    first, y_rows = lax.optimization_barrier((first, y_rows))
    inner = pl.pallas_call(
        inner_kernel,
        out_shape=shape(part // 2, 2 * nb),
        in_specs=[whole] * 3,
        out_specs=whole,
        compiler_params=VMEM,
        cost_estimate=pl.CostEstimate(flops=6 * nb * part * cols, bytes_accessed=cols * nb * 4, transcendentals=0),
    )(first_group, second_group, y_rows)
    for mask in cols_order[::-1]:
        inner = inner + swap(inner, "prow", mask)
    inner = inner[None]
    for mask in rest[:-2]:
        inner = join(inner, swap(inner, "pcol", mask), col[mask])
    near_inner = [inner] + [swap(inner, "pcol", mask) for mask in (close, far, close + far)]
    first = join(first, swap(first, "pcol", close), col[close])
    second = join(second, swap(second, "pcol", far), col[far])

    u_cols, zc = pl.pallas_call(
        functools.partial(column_factor_kernel, cols_order),
        out_shape=[shape(3 * nb, cols, dtype=BF16), shape(nb, cols)],
        in_specs=[whole] * 2,
        out_specs=[whole] * 2,
        scratch_shapes=[pltpu.VMEM((nb, cols), F32)],
        compiler_params=VMEM,
        cost_estimate=pl.CostEstimate(flops=6 * nb * nb * cols, bytes_accessed=cols * nb * 8, transcendentals=0),
    )(tfactor, columns)

    chunks = 4
    lines = rows * col_tiles // chunks
    outside = pl.BlockSpec(memory_space=pltpu.HBM)
    result = pl.pallas_call(
        functools.partial(update_kernel, orders, inner_upper),
        out_shape=shape(rows * col_tiles, tile),
        in_specs=[whole] * 10,
        out_specs=outside,
        scratch_shapes=[
            pltpu.VMEM((nb, nb), F32),
            pltpu.VMEM((3 * nb, cols), BF16),
            pltpu.VMEM((ratio, nb, cols), F32),
            pltpu.VMEM((chunks, lines, tile), F32),
            pltpu.SemaphoreType.DMA((chunks,)),
        ],
        compiler_params=VMEM,
        cost_estimate=pl.CostEstimate(flops=12 * nb * rows * cols, bytes_accessed=rows * cols * 8, transcendentals=0),
    )(block, u_rows, u_cols, zc, first, second, *near_inner)
    return result.reshape(trailing.shape)


def solution(mesh):
    return jax.shard_map(
        per_device,
        mesh=mesh,
        in_specs=(P(None, "prow", None, None, "pcol", None), P(None, "prow", None, "pcol"), P()),
        out_specs=P(None, "prow", None, None, "pcol", None),
        check_vma=False,
    )
```

```python
import functools

import jax
import jax.numpy as jnp
from jax import lax
from jax.experimental import pallas as pl
from jax.experimental.pallas import tpu as pltpu
from jax.sharding import PartitionSpec as P

BOTH = ("prow", "pcol")
F32 = jnp.float32
BF16 = jnp.bfloat16
VMEM = pltpu.CompilerParams(vmem_limit_bytes=8 * 1024 * 1024)


def split(values):
    high = values.astype(BF16)
    return high, (values - high.astype(F32)).astype(BF16)


def dot(left, right, dims=((1,), (0,))):
    return lax.dot_general(left, right, (dims, ((), ())), preferred_element_type=F32)


def dot3(left, right, dims=((1,), (0,))):
    (lh, ll), (rh, rl) = left, right
    return dot(lh, rh, dims) + (dot(lh, rl, dims) + dot(ll, rh, dims))


def swap(values, axis, mask):
    n = lax.axis_size(axis)
    return lax.ppermute(values, axis, [(i, i ^ mask) for i in range(n)])


def halving(n):
    masks = []
    while n > 1:
        n //= 2
        masks.append(n)
    return masks


def join(values, other, high):
    pair = jnp.stack([jnp.where(high, other, values), jnp.where(high, values, other)])
    return pair.reshape((-1,) + values.shape[1:])


def gather(values, axis, masks, above):
    values = values[None]
    for mask in masks:
        values = join(values, swap(values, axis, mask), above[mask])
    return values


def slot(index, masks):
    return sum(1 << j for j, mask in enumerate(masks) if index & mask)


def swap_three(values, axis):
    return [swap(values, axis, mask) for mask in (1, 2, 3)]


def split_block_kernel(col_tiles, tile, a_ref, high_ref, low_ref):
    rows = high_ref.shape[0]
    for b in range(col_tiles):
        cols = slice(b * tile, (b + 1) * tile)
        high, low = split(a_ref[pl.ds(b, rows, stride=col_tiles), :])
        high_ref[:, cols] = high
        low_ref[:, cols] = low


def product_kernel(orders, ah_ref, al_ref, first_ref, second_ref, y_ref, keep_ref, send_ref, yh, yl, total):
    nc, half, width, tile = first_ref.shape
    for chunk, (ref, masks) in enumerate(zip((first_ref, second_ref), orders)):
        for a in range(half):
            at = chunk * half + a
            for j in range(nc):
                y_ref[at, j * width : (j + 1) * width, :] = ref[slot(j, masks), a]
            cols = slice(at * tile, (at + 1) * tile)
            yh[:, cols], yl[:, cols] = split(y_ref[at])
    total[...] = dot3((yh[...], yl[...]), (ah_ref[...], al_ref[...]))
    core = lax.axis_index("prow") & 1
    count, part = keep_ref.shape[:2]
    for y in range(count):
        keep_ref[y] = total[pl.ds(pl.multiple_of((2 * y + core) * part, part), part), :]
        send_ref[y] = total[pl.ds(pl.multiple_of((2 * y + 1 - core) * part, part), part), :]


def inner_kernel(first_ref, second_ref, y_ref, inner_ref):
    row_tiles, nb, tile = y_ref.shape
    ratio, half, cols = first_ref.shape
    inner = jnp.zeros((2 * half, nb), F32)
    for g in range(ratio):
        for b in range(cols // tile):
            at = slice(b * tile, (b + 1) * tile)
            left = jnp.concatenate([first_ref[g, :, at], second_ref[g, :, at]], axis=0)
            inner += dot3(split(left), split(y_ref[b * ratio + g]), ((1,), (1,)))
    for side in range(2):
        inner_ref[:, side * nb : (side + 1) * nb] = inner[side * half : (side + 1) * half]


def stack_left(values):
    high, low = split(values)
    return jnp.concatenate([high, high, low], axis=1)


def stack_right(ref, values):
    rows = values.shape[0]
    high, low = split(values)
    ref[:rows, :] = high
    ref[rows : 2 * rows, :] = low
    ref[2 * rows :, :] = high


def row_factor_kernel(t_ref, y_ref, out_ref):
    row_tiles, nb, tile = y_ref.shape
    factor = split(t_ref[...])
    for a in range(row_tiles):
        out_ref[a * tile : (a + 1) * tile, :] = stack_left(dot3(factor, split(y_ref[a])).T)


def column_factor_kernel(order, t_ref, cols_ref, out_ref, z_ref, y):
    slots, _, half, _ = cols_ref.shape
    for s in range(slots):
        for side in range(2):
            rows = slice((2 * s + side) * half, (2 * s + side + 1) * half)
            z_ref[rows, :] = cols_ref[slot(s, order), side]
            y[rows, :] = cols_ref[slot(s, order), 2 + side]
    stack_right(out_ref, dot3(split(t_ref[...]), split(y[...])))


def update_kernel(
    orders, inner_upper, a_ref, ur_ref, uc_ref, zc_ref, *refs
):
    (first_ref, *second_refs), inners, (out_ref, inner, w, zt, result, write) = refs[:3], refs[3:7], refs[7:]
    pcol = lax.axis_index("pcol")
    near = pcol & 3
    ratio, nb, cols = zt.shape
    half = first_ref.shape[1]
    slots = nb // (2 * half)
    chunks, lines, tile = result.shape
    col_tiles = cols // tile
    writes = [pltpu.make_async_copy(result.at[i], out_ref.at[pl.ds(i * lines, lines)], write.at[i]) for i in range(chunks)]
    first_order, second_order = orders
    last = second_order[-1]
    bit = (pcol // last) & 1
    for g in range(ratio):
        for s in range(slots):
            zt[g, 2 * s * half : (2 * s + 1) * half, :] = first_ref[slot(g * slots + s, first_order)]
            if s & last == 0:
                for ref, place in zip(second_refs, (bit, 1 - bit)):
                    at = pl.multiple_of((2 * s + 1) * half + place * (2 * last * half), half)
                    zt[g, pl.ds(at, half), :] = ref[slot(g * slots + s, second_order[:-1])]
    for r in range(4):
        for u in range(slots // 4):
            for side in range(2):
                at = pl.multiple_of((2 * (u * 4 + (near ^ r)) + side) * half, half)
                inner[pl.ds(at, half), :] = inners[r][slot(u, inner_upper), :, side * nb : (side + 1) * nb]
    stack_right(w, zc_ref[...] - dot3(split(inner[...]), (uc_ref[:nb, :], uc_ref[nb : 2 * nb, :])))
    rows = lines // col_tiles
    count = rows // (ratio * tile)
    wide = 2
    for i in range(0, chunks, wide):
        turned = []
        for b in range(i * count, (i + wide) * count):
            turned += [zt[g, :, b * tile : (b + 1) * tile].T for g in range(ratio)]
        at = slice(i * rows, (i + wide) * rows)
        total = dot(stack_left(jnp.concatenate(turned, axis=0)), uc_ref[...]) + dot(ur_ref[at, :], w[...])
        for j in range(wide):
            for g in range(ratio * count):
                for b in range(col_tiles):
                    at = g * tile * col_tiles + b
                    values = a_ref[pl.ds((i + j) * lines + at, tile, stride=col_tiles), :]
                    part = total[j * rows + g * tile : j * rows + (g + 1) * tile, b * tile : (b + 1) * tile]
                    result[i + j, pl.ds(at, tile, stride=col_tiles), :] = values - part
            writes[i + j].start()
    for copy in writes:
        copy.wait()


def shape(*dims, dtype=F32):
    return jax.ShapeDtypeStruct(dims, dtype)


def per_device(trailing, reflectors, tfactor):
    row_tiles, _, tile, col_tiles = trailing.shape[:4]
    np_, nc = lax.axis_size("prow"), lax.axis_size("pcol")
    ratio = nc // np_
    ny = np_ // 2
    rows, cols = row_tiles * tile, col_tiles * tile
    nb = tfactor.shape[0]
    part = nb // np_
    half = row_tiles // 2
    block = trailing.reshape(rows * col_tiles, tile)
    mine = jnp.transpose(reflectors.reshape(row_tiles, tile, -1), (0, 2, 1))

    masks, cols_order = halving(nc), halving(np_)
    lead, rest = masks[: len(masks) - len(cols_order)], masks[len(masks) - len(cols_order) :]
    shift = len(cols_order)
    prow, pcol = lax.axis_index("prow").astype(jnp.int32), lax.axis_index("pcol").astype(jnp.int32)
    group = pcol >> shift
    where = {
        "group": group,
        "rounds": [(prow >> 1) ^ r for r in range(ny)],
        "share": (pcol & (np_ - 1)) * part,
        "col": {mask: (pcol & mask) != 0 for mask in masks},
        "row": {mask: (prow & mask) != 0 for mask in cols_order},
        "half": {mask: [jnp.where((prow & mask) != 0, 1 - side, side) for side in range(2)] for mask in cols_order},
    }
    mine, where = lax.optimization_barrier((mine, where))
    group, col, row = where["group"], where["col"], where["row"]
    whole = pl.BlockSpec(memory_space=pltpu.VMEM)

    def flat(p, q):
        return p * nc + q

    def turn(values, r):
        perm = [
            (flat(p, g * np_ + s), flat(s, g * np_ + (p ^ r))) for p in range(np_) for g in range(ratio) for s in range(np_)
        ]
        return lax.ppermute(values, BOTH, perm)

    inner_upper = [mask // 4 for mask in rest[:-2]]
    far, close = rest[-2:]
    orders = (masks, masks[:-2] + [close, far])
    a_high, a_low = pl.pallas_call(
        functools.partial(split_block_kernel, col_tiles, tile),
        out_shape=[shape(rows, cols, dtype=BF16)] * 2,
        in_specs=[whole],
        out_specs=[whole] * 2,
        compiler_params=VMEM,
        cost_estimate=pl.CostEstimate(flops=rows * cols * 4, bytes_accessed=rows * cols * 8, transcendentals=0),
    )(block)
    first, second = lax.optimization_barrier(mine[None, :half]), lax.optimization_barrier(mine[None, half:])
    for at, (mask, other) in enumerate(zip(*orders)):
        first_came, second_came = swap(first, "pcol", mask), swap(second, "pcol", other)
        if at == 0:
            second_came, a_high, a_low = lax.optimization_barrier((second_came, a_high, a_low))
        first, second = join(first, first_came, col[mask]), join(second, second_came, col[other])

    y_rows, keep, send = pl.pallas_call(
        functools.partial(product_kernel, orders),
        out_shape=[shape(row_tiles, nb, tile), shape(ny, part, cols), shape(ny, part, cols)],
        in_specs=[whole] * 4,
        out_specs=[whole] * 3,
        scratch_shapes=[pltpu.VMEM((nb, rows), BF16), pltpu.VMEM((nb, rows), BF16), pltpu.VMEM((nb, cols), F32)],
        compiler_params=VMEM,
        cost_estimate=pl.CostEstimate(flops=6 * nb * rows * cols, bytes_accessed=rows * cols * 8, transcendentals=0),
    )(a_high, a_low, first, second)
    other = swap(send, "prow", 1)
    kept = keep + other
    y_piece = lax.dynamic_slice(
        y_rows.reshape(col_tiles, ratio, nb, tile), (0, group, where["share"], 0), (col_tiles, 1, part, tile)
    )
    y_piece = jnp.transpose(y_piece.reshape(col_tiles, part, tile), (1, 0, 2)).reshape(part, cols)

    turned = []
    for r in range(ny):
        message = lax.dynamic_index_in_dim(kept, where["rounds"][r], 0, keepdims=False)
        turned.append(turn(message, 2 * r))
    turned = sum(turned[1:], turned[0])
    y_piece, kept = lax.optimization_barrier((y_piece, kept))
    for mask in cols_order[:-1]:
        low, high = where["half"][mask]
        pair = kept.reshape(2, mask // 2, part, cols)
        kept = lax.dynamic_index_in_dim(pair, low, 0, keepdims=False)
        kept = kept + swap(lax.dynamic_index_in_dim(pair, high, 0, keepdims=False), "prow", mask)
    piece = kept.reshape(part, cols)
    y_cols = turn(y_piece, 0).reshape(2, part // 2, cols)
    u_rows = pl.pallas_call(
        row_factor_kernel,
        out_shape=shape(rows, 3 * nb, dtype=BF16),
        in_specs=[whole] * 2,
        out_specs=whole,
        compiler_params=VMEM,
        cost_estimate=pl.CostEstimate(flops=6 * nb * nb * rows, bytes_accessed=rows * nb * 8, transcendentals=0),
    )(tfactor, y_rows)
    turned, u_rows = lax.optimization_barrier((turned, u_rows))
    first, second = turned[None, : part // 2], turned[None, part // 2 :]
    first, second = lax.optimization_barrier(first), lax.optimization_barrier(second)
    columns = jnp.concatenate([piece.reshape(2, part // 2, cols), y_cols])
    for mask in lead:
        first = join(first, swap(first, "pcol", mask), col[mask])
        second = join(second, swap(second, "pcol", mask), col[mask])
    first, columns = lax.optimization_barrier((first, columns))
    first_group, second_group = first, second
    for mask in rest[:-2]:
        first = join(first, swap(first, "pcol", mask), col[mask])
        second = join(second, swap(second, "pcol", mask), col[mask])
    first = join(first, swap(first, "pcol", far), col[far])
    second = join(second, swap(second, "pcol", close), col[close])

    columns = gather(columns, "prow", cols_order, row)
    first, y_rows = lax.optimization_barrier((first, y_rows))
    inner = pl.pallas_call(
        inner_kernel,
        out_shape=shape(part // 2, 2 * nb),
        in_specs=[whole] * 3,
        out_specs=whole,
        compiler_params=VMEM,
        cost_estimate=pl.CostEstimate(flops=6 * nb * part * cols, bytes_accessed=cols * nb * 4, transcendentals=0),
    )(first_group, second_group, y_rows)
    for mask in cols_order[::-1]:
        inner = inner + swap(inner, "prow", mask)
    inner = inner[None]
    for mask in rest[:-2]:
        inner = join(inner, swap(inner, "pcol", mask), col[mask])
    u_cols, zc = pl.pallas_call(
        functools.partial(column_factor_kernel, cols_order),
        out_shape=[shape(3 * nb, cols, dtype=BF16), shape(nb, cols)],
        in_specs=[whole] * 2,
        out_specs=[whole] * 2,
        scratch_shapes=[pltpu.VMEM((nb, cols), F32)],
        compiler_params=VMEM,
        cost_estimate=pl.CostEstimate(flops=6 * nb * nb * cols, bytes_accessed=cols * nb * 8, transcendentals=0),
    )(tfactor, columns)

    near_inner = [inner] + [swap(inner, "pcol", mask) for mask in (close, far, close + far)]
    first = join(first, swap(first, "pcol", close), col[close])
    second_came = swap(second, "pcol", far)

    chunks = 4
    lines = rows * col_tiles // chunks
    outside = pl.BlockSpec(memory_space=pltpu.HBM)
    result = pl.pallas_call(
        functools.partial(update_kernel, orders, inner_upper),
        out_shape=shape(rows * col_tiles, tile),
        in_specs=[whole] * 11,
        out_specs=outside,
        scratch_shapes=[
            pltpu.VMEM((nb, nb), F32),
            pltpu.VMEM((3 * nb, cols), BF16),
            pltpu.VMEM((ratio, nb, cols), F32),
            pltpu.VMEM((chunks, lines, tile), F32),
            pltpu.SemaphoreType.DMA((chunks,)),
        ],
        compiler_params=VMEM,
        cost_estimate=pl.CostEstimate(flops=12 * nb * rows * cols, bytes_accessed=rows * cols * 8, transcendentals=0),
    )(block, u_rows, u_cols, zc, first, second, second_came, *near_inner)
    return result.reshape(trailing.shape)


def solution(mesh):
    return jax.shard_map(
        per_device,
        mesh=mesh,
        in_specs=(P(None, "prow", None, None, "pcol", None), P(None, "prow", None, "pcol"), P()),
        out_specs=P(None, "prow", None, None, "pcol", None),
        check_vma=False,
    )
```

```python
import functools

import jax
import jax.numpy as jnp
from jax import lax
from jax.experimental import pallas as pl
from jax.experimental.pallas import tpu as pltpu
from jax.sharding import PartitionSpec as P

BOTH = ("prow", "pcol")
F32 = jnp.float32
BF16 = jnp.bfloat16
VMEM = pltpu.CompilerParams(vmem_limit_bytes=8 * 1024 * 1024)


def split(values):
    high = values.astype(BF16)
    return high, (values - high.astype(F32)).astype(BF16)


def dot(left, right, dims=((1,), (0,))):
    return lax.dot_general(left, right, (dims, ((), ())), preferred_element_type=F32)


def dot3(left, right, dims=((1,), (0,))):
    (lh, ll), (rh, rl) = left, right
    return dot(lh, rh, dims) + (dot(lh, rl, dims) + dot(ll, rh, dims))


def swap(values, axis, mask):
    n = lax.axis_size(axis)
    return lax.ppermute(values, axis, [(i, i ^ mask) for i in range(n)])


def halving(n):
    masks = []
    while n > 1:
        n //= 2
        masks.append(n)
    return masks


def join(values, other, high):
    pair = jnp.stack([jnp.where(high, other, values), jnp.where(high, values, other)])
    return pair.reshape((-1,) + values.shape[1:])


def slot(index, masks):
    return sum(1 << j for j, mask in enumerate(masks) if index & mask)


def swap_three(values, axis):
    return [swap(values, axis, mask) for mask in (1, 2, 3)]


def split_block_kernel(col_tiles, tile, a_ref, high_ref, low_ref):
    rows = high_ref.shape[0]
    for b in range(col_tiles):
        cols = slice(b * tile, (b + 1) * tile)
        high, low = split(a_ref[pl.ds(b, rows, stride=col_tiles), :])
        high_ref[:, cols] = high
        low_ref[:, cols] = low


def product_kernel(orders, ah_ref, al_ref, first_ref, second_ref, y_ref, keep_ref, send_ref, yh, yl, total):
    nc, half, width, tile = first_ref.shape
    for chunk, (ref, masks) in enumerate(zip((first_ref, second_ref), orders)):
        for a in range(half):
            at = chunk * half + a
            for j in range(nc):
                y_ref[at, j * width : (j + 1) * width, :] = ref[slot(j, masks), a]
            cols = slice(at * tile, (at + 1) * tile)
            yh[:, cols], yl[:, cols] = split(y_ref[at])
    total[...] = dot3((yh[...], yl[...]), (ah_ref[...], al_ref[...]))
    core = lax.axis_index("prow") & 1
    count, part = keep_ref.shape[:2]
    for y in range(count):
        keep_ref[y] = total[pl.ds(pl.multiple_of((2 * y + core) * part, part), part), :]
        send_ref[y] = total[pl.ds(pl.multiple_of((2 * y + 1 - core) * part, part), part), :]


def inner_kernel(first_ref, second_ref, y_ref, inner_ref):
    row_tiles, nb, tile = y_ref.shape
    ratio, half, cols = first_ref.shape
    inner = jnp.zeros((2 * half, nb), F32)
    for g in range(ratio):
        for b in range(cols // tile):
            at = slice(b * tile, (b + 1) * tile)
            left = jnp.concatenate([first_ref[g, :, at], second_ref[g, :, at]], axis=0)
            inner += dot3(split(left), split(y_ref[b * ratio + g]), ((1,), (1,)))
    for side in range(2):
        inner_ref[:, side * nb : (side + 1) * nb] = inner[side * half : (side + 1) * half]


def stack_left(values):
    high, low = split(values)
    return jnp.concatenate([high, high, low], axis=1)


def stack_right(ref, values):
    rows = values.shape[0]
    high, low = split(values)
    ref[:rows, :] = high
    ref[rows : 2 * rows, :] = low
    ref[2 * rows :, :] = high


def row_factor_kernel(t_ref, y_ref, out_ref):
    row_tiles, nb, tile = y_ref.shape
    factor = split(t_ref[...])
    for a in range(row_tiles):
        out_ref[a * tile : (a + 1) * tile, :] = stack_left(dot3(factor, split(y_ref[a])).T)


def column_factor_kernel(order, t_ref, cols_ref, out_ref, z_ref, y):
    slots, _, half, _ = cols_ref.shape
    for s in range(slots):
        for side in range(2):
            rows = slice((2 * s + side) * half, (2 * s + side + 1) * half)
            z_ref[rows, :] = cols_ref[slot(s, order), side]
            y[rows, :] = cols_ref[slot(s, order), 2 + side]
    stack_right(out_ref, dot3(split(t_ref[...]), split(y[...])))


def update_kernel(
    orders, inner_upper, a_ref, ur_ref, uc_ref, zc_ref, *refs
):
    pairs, inners, (out_ref, inner, w, zt, result, write) = (refs[:2], refs[2:4]), refs[4:8], refs[8:]
    pcol = lax.axis_index("pcol")
    near = pcol & 3
    ratio, nb, cols = zt.shape
    half = refs[0].shape[1]
    slots = nb // (2 * half)
    chunks, lines, tile = result.shape
    col_tiles = cols // tile
    writes = [pltpu.make_async_copy(result.at[i], out_ref.at[pl.ds(i * lines, lines)], write.at[i]) for i in range(chunks)]
    for side, (pair, masks) in enumerate(zip(pairs, orders)):
        last = masks[-1]
        bit = (pcol // last) & 1
        for ref, place in zip(pair, (bit, 1 - bit)):
            for g in range(ratio):
                for s in range(slots):
                    if s & last == 0:
                        at = pl.multiple_of((2 * s + side) * half + place * (2 * last * half), half)
                        zt[g, pl.ds(at, half), :] = ref[slot(g * slots + s, masks[:-1])]
    for r in range(4):
        for u in range(slots // 4):
            for side in range(2):
                at = pl.multiple_of((2 * (u * 4 + (near ^ r)) + side) * half, half)
                inner[pl.ds(at, half), :] = inners[r][slot(u, inner_upper), :, side * nb : (side + 1) * nb]
    stack_right(w, zc_ref[...] - dot3(split(inner[...]), (uc_ref[:nb, :], uc_ref[nb : 2 * nb, :])))
    rows = lines // col_tiles
    count = rows // (ratio * tile)
    wide = 2
    for i in range(0, chunks, wide):
        turned = []
        for b in range(i * count, (i + wide) * count):
            turned += [zt[g, :, b * tile : (b + 1) * tile].T for g in range(ratio)]
        at = slice(i * rows, (i + wide) * rows)
        total = dot(stack_left(jnp.concatenate(turned, axis=0)), uc_ref[...]) + dot(ur_ref[at, :], w[...])
        for j in range(wide):
            for g in range(ratio * count):
                for b in range(col_tiles):
                    at = g * tile * col_tiles + b
                    values = a_ref[pl.ds((i + j) * lines + at, tile, stride=col_tiles), :]
                    part = total[j * rows + g * tile : j * rows + (g + 1) * tile, b * tile : (b + 1) * tile]
                    result[i + j, pl.ds(at, tile, stride=col_tiles), :] = values - part
            writes[i + j].start()
    for copy in writes:
        copy.wait()


def shape(*dims, dtype=F32):
    return jax.ShapeDtypeStruct(dims, dtype)


def per_device(trailing, reflectors, tfactor):
    row_tiles, _, tile, col_tiles = trailing.shape[:4]
    np_, nc = lax.axis_size("prow"), lax.axis_size("pcol")
    ratio = nc // np_
    ny = np_ // 2
    rows, cols = row_tiles * tile, col_tiles * tile
    nb = tfactor.shape[0]
    part = nb // np_
    half = row_tiles // 2
    block = trailing.reshape(rows * col_tiles, tile)
    mine = jnp.transpose(reflectors.reshape(row_tiles, tile, -1), (0, 2, 1))

    masks, cols_order = halving(nc), halving(np_)
    lead, rest = masks[: len(masks) - len(cols_order)], masks[len(masks) - len(cols_order) :]
    shift = len(cols_order)
    prow, pcol = lax.axis_index("prow").astype(jnp.int32), lax.axis_index("pcol").astype(jnp.int32)
    group = pcol >> shift
    where = {
        "group": group,
        "rounds": [(prow >> 1) ^ r for r in range(ny)],
        "share": (pcol & (np_ - 1)) * part,
        "col": {mask: (pcol & mask) != 0 for mask in masks},
        "row": {mask: (prow & mask) != 0 for mask in cols_order},
        "half": {mask: [jnp.where((prow & mask) != 0, 1 - side, side) for side in range(2)] for mask in cols_order},
    }
    mine, where = lax.optimization_barrier((mine, where))
    group, col, row = where["group"], where["col"], where["row"]
    whole = pl.BlockSpec(memory_space=pltpu.VMEM)

    def flat(p, q):
        return p * nc + q

    def turn(values, r):
        perm = [
            (flat(p, g * np_ + s), flat(s, g * np_ + (p ^ r))) for p in range(np_) for g in range(ratio) for s in range(np_)
        ]
        return lax.ppermute(values, BOTH, perm)

    inner_upper = [mask // 4 for mask in rest[:-2]]
    far, close = rest[-2:]
    orders = (masks, masks[:-2] + [close, far])
    a_high, a_low = pl.pallas_call(
        functools.partial(split_block_kernel, col_tiles, tile),
        out_shape=[shape(rows, cols, dtype=BF16)] * 2,
        in_specs=[whole],
        out_specs=[whole] * 2,
        compiler_params=VMEM,
        cost_estimate=pl.CostEstimate(flops=rows * cols * 4, bytes_accessed=rows * cols * 8, transcendentals=0),
    )(block)
    first, second = lax.optimization_barrier(mine[None, :half]), lax.optimization_barrier(mine[None, half:])
    for at, (mask, other) in enumerate(zip(*orders)):
        first_came, second_came = swap(first, "pcol", mask), swap(second, "pcol", other)
        if at == 0:
            second_came, a_high, a_low = lax.optimization_barrier((second_came, a_high, a_low))
        first, second = join(first, first_came, col[mask]), join(second, second_came, col[other])

    y_rows, keep, send = pl.pallas_call(
        functools.partial(product_kernel, orders),
        out_shape=[shape(row_tiles, nb, tile), shape(ny, part, cols), shape(ny, part, cols)],
        in_specs=[whole] * 4,
        out_specs=[whole] * 3,
        scratch_shapes=[pltpu.VMEM((nb, rows), BF16), pltpu.VMEM((nb, rows), BF16), pltpu.VMEM((nb, cols), F32)],
        compiler_params=VMEM,
        cost_estimate=pl.CostEstimate(flops=6 * nb * rows * cols, bytes_accessed=rows * cols * 8, transcendentals=0),
    )(a_high, a_low, first, second)
    other = swap(send, "prow", 1)
    kept = keep + other
    y_piece = lax.dynamic_slice(
        y_rows.reshape(col_tiles, ratio, nb, tile), (0, group, where["share"], 0), (col_tiles, 1, part, tile)
    )
    y_piece = jnp.transpose(y_piece.reshape(col_tiles, part, tile), (1, 0, 2)).reshape(part, cols)

    turned = []
    for r in range(ny):
        message = lax.dynamic_index_in_dim(kept, where["rounds"][r], 0, keepdims=False)
        turned.append(turn(message, 2 * r))
    turned = sum(turned[1:], turned[0])
    y_piece, kept = lax.optimization_barrier((y_piece, kept))
    for mask in cols_order[:-1]:
        low, high = where["half"][mask]
        pair = kept.reshape(2, mask // 2, part, cols)
        kept = lax.dynamic_index_in_dim(pair, low, 0, keepdims=False)
        kept = kept + swap(lax.dynamic_index_in_dim(pair, high, 0, keepdims=False), "prow", mask)
    piece = kept.reshape(part, cols)
    y_cols = turn(y_piece, 0).reshape(1, 2, part // 2, cols)
    u_rows = pl.pallas_call(
        row_factor_kernel,
        out_shape=shape(rows, 3 * nb, dtype=BF16),
        in_specs=[whole] * 2,
        out_specs=whole,
        compiler_params=VMEM,
        cost_estimate=pl.CostEstimate(flops=6 * nb * nb * rows, bytes_accessed=rows * nb * 8, transcendentals=0),
    )(tfactor, y_rows)
    turned, u_rows = lax.optimization_barrier((turned, u_rows))
    first, second = turned[None, : part // 2], turned[None, part // 2 :]
    first, second = lax.optimization_barrier(first), lax.optimization_barrier(second)
    z_cols = piece.reshape(1, 2, part // 2, cols)
    for mask in cols_order[:-1]:
        y_cols = join(y_cols, swap(y_cols, "prow", mask), row[mask])
    z_cols, y_cols = lax.optimization_barrier((z_cols, y_cols))
    for mask in lead:
        first = join(first, swap(first, "pcol", mask), col[mask])
        second = join(second, swap(second, "pcol", mask), col[mask])
    first, z_cols = lax.optimization_barrier((first, z_cols))
    first_group, second_group = first, second
    for mask in rest[:-2]:
        first = join(first, swap(first, "pcol", mask), col[mask])
        second = join(second, swap(second, "pcol", mask), col[mask])
    first = join(first, swap(first, "pcol", far), col[far])
    second = join(second, swap(second, "pcol", close), col[close])

    near_row = cols_order[-1]
    for mask in cols_order[:-1]:
        z_cols = join(z_cols, swap(z_cols, "prow", mask), row[mask])
    columns = jnp.concatenate([z_cols, y_cols], axis=1)
    columns = join(columns, swap(columns, "prow", near_row), row[near_row])
    inner = pl.pallas_call(
        inner_kernel,
        out_shape=shape(part // 2, 2 * nb),
        in_specs=[whole] * 3,
        out_specs=whole,
        compiler_params=VMEM,
        cost_estimate=pl.CostEstimate(flops=6 * nb * part * cols, bytes_accessed=cols * nb * 4, transcendentals=0),
    )(first_group, second_group, y_rows)
    for mask in cols_order[::-1]:
        inner = inner + swap(inner, "prow", mask)
    inner = inner[None]
    for mask in rest[:-2]:
        inner = join(inner, swap(inner, "pcol", mask), col[mask])
    u_cols, zc = pl.pallas_call(
        functools.partial(column_factor_kernel, cols_order),
        out_shape=[shape(3 * nb, cols, dtype=BF16), shape(nb, cols)],
        in_specs=[whole] * 2,
        out_specs=[whole] * 2,
        scratch_shapes=[pltpu.VMEM((nb, cols), F32)],
        compiler_params=VMEM,
        cost_estimate=pl.CostEstimate(flops=6 * nb * nb * cols, bytes_accessed=cols * nb * 8, transcendentals=0),
    )(tfactor, columns)

    near_inner = [inner] + [swap(inner, "pcol", mask) for mask in (close, far, close + far)]
    first_came, second_came = swap(first, "pcol", close), swap(second, "pcol", far)

    chunks = 4
    lines = rows * col_tiles // chunks
    outside = pl.BlockSpec(memory_space=pltpu.HBM)
    result = pl.pallas_call(
        functools.partial(update_kernel, orders, inner_upper),
        out_shape=shape(rows * col_tiles, tile),
        in_specs=[whole] * 12,
        out_specs=outside,
        scratch_shapes=[
            pltpu.VMEM((nb, nb), F32),
            pltpu.VMEM((3 * nb, cols), BF16),
            pltpu.VMEM((ratio, nb, cols), F32),
            pltpu.VMEM((chunks, lines, tile), F32),
            pltpu.SemaphoreType.DMA((chunks,)),
        ],
        compiler_params=VMEM,
        cost_estimate=pl.CostEstimate(flops=12 * nb * rows * cols, bytes_accessed=rows * cols * 8, transcendentals=0),
    )(block, u_rows, u_cols, zc, first, first_came, second, second_came, *near_inner)
    return result.reshape(trailing.shape)


def solution(mesh):
    return jax.shard_map(
        per_device,
        mesh=mesh,
        in_specs=(P(None, "prow", None, None, "pcol", None), P(None, "prow", None, "pcol"), P()),
        out_specs=P(None, "prow", None, None, "pcol", None),
        check_vma=False,
    )
```

```python
import functools

import jax
import jax.numpy as jnp
from jax import lax
from jax.experimental import pallas as pl
from jax.experimental.pallas import tpu as pltpu
from jax.sharding import PartitionSpec as P

BOTH = ("prow", "pcol")
F32 = jnp.float32
BF16 = jnp.bfloat16
VMEM = pltpu.CompilerParams(vmem_limit_bytes=8 * 1024 * 1024)


def split(values):
    high = values.astype(BF16)
    return high, (values - high.astype(F32)).astype(BF16)


def dot(left, right, dims=((1,), (0,))):
    return lax.dot_general(left, right, (dims, ((), ())), preferred_element_type=F32)


def dot3(left, right, dims=((1,), (0,))):
    (lh, ll), (rh, rl) = left, right
    return dot(lh, rh, dims) + (dot(lh, rl, dims) + dot(ll, rh, dims))


def swap(values, axis, mask):
    n = lax.axis_size(axis)
    return lax.ppermute(values, axis, [(i, i ^ mask) for i in range(n)])


def halving(n):
    masks = []
    while n > 1:
        n //= 2
        masks.append(n)
    return masks


def join(values, other, high):
    pair = jnp.stack([jnp.where(high, other, values), jnp.where(high, values, other)])
    return pair.reshape((-1,) + values.shape[1:])


def gather(values, axis, masks, above):
    values = values[None]
    for mask in masks:
        values = join(values, swap(values, axis, mask), above[mask])
    return values


def slot(index, masks):
    return sum(1 << j for j, mask in enumerate(masks) if index & mask)


def swap_three(values, axis):
    return [swap(values, axis, mask) for mask in (1, 2, 3)]


def split_block_kernel(col_tiles, tile, a_ref, high_ref, low_ref):
    rows = high_ref.shape[0]
    for b in range(col_tiles):
        cols = slice(b * tile, (b + 1) * tile)
        high, low = split(a_ref[pl.ds(b, rows, stride=col_tiles), :])
        high_ref[:, cols] = high
        low_ref[:, cols] = low


def product_kernel(orders, ah_ref, al_ref, first_ref, second_ref, y_ref, keep_ref, send_ref, yh, yl, total):
    nc, half, width, tile = first_ref.shape
    for chunk, (ref, masks) in enumerate(zip((first_ref, second_ref), orders)):
        for a in range(half):
            at = chunk * half + a
            for j in range(nc):
                y_ref[at, j * width : (j + 1) * width, :] = ref[slot(j, masks), a]
            cols = slice(at * tile, (at + 1) * tile)
            yh[:, cols], yl[:, cols] = split(y_ref[at])
    total[...] = dot3((yh[...], yl[...]), (ah_ref[...], al_ref[...]))
    core = lax.axis_index("prow") & 1
    count, part = keep_ref.shape[:2]
    for y in range(count):
        keep_ref[y] = total[pl.ds(pl.multiple_of((2 * y + core) * part, part), part), :]
        send_ref[y] = total[pl.ds(pl.multiple_of((2 * y + 1 - core) * part, part), part), :]


def inner_kernel(first_ref, second_ref, y_ref, inner_ref):
    row_tiles, nb, tile = y_ref.shape
    ratio, half, cols = first_ref.shape
    inner = jnp.zeros((2 * half, nb), F32)
    for g in range(ratio):
        for b in range(cols // tile):
            at = slice(b * tile, (b + 1) * tile)
            left = jnp.concatenate([first_ref[g, :, at], second_ref[g, :, at]], axis=0)
            inner += dot3(split(left), split(y_ref[b * ratio + g]), ((1,), (1,)))
    for side in range(2):
        inner_ref[:, side * nb : (side + 1) * nb] = inner[side * half : (side + 1) * half]


def stack_left(values):
    high, low = split(values)
    return jnp.concatenate([high, high, low], axis=1)


def stack_right(ref, values):
    rows = values.shape[0]
    high, low = split(values)
    ref[:rows, :] = high
    ref[rows : 2 * rows, :] = low
    ref[2 * rows :, :] = high


def row_factor_kernel(t_ref, y_ref, out_ref):
    row_tiles, nb, tile = y_ref.shape
    factor = split(t_ref[...])
    for a in range(row_tiles):
        out_ref[a * tile : (a + 1) * tile, :] = stack_left(dot3(factor, split(y_ref[a])).T)


def column_factor_kernel(order, t_ref, cols_ref, out_ref, z_ref, y):
    slots, _, half, _ = cols_ref.shape
    for s in range(slots):
        for side in range(2):
            rows = slice((2 * s + side) * half, (2 * s + side + 1) * half)
            z_ref[rows, :] = cols_ref[slot(s, order), side]
            y[rows, :] = cols_ref[slot(s, order), 2 + side]
    stack_right(out_ref, dot3(split(t_ref[...]), split(y[...])))


def rows_kernel(orders, a_ref, uc_ref, first_ref, second_ref, came_ref, out_ref, zt):
    ratio, nb, cols = zt.shape
    half = first_ref.shape[1]
    slots = nb // (2 * half)
    rows = out_ref.shape[0]
    tile = a_ref.shape[1]
    col_tiles = cols // tile
    first_order, second_order = orders
    last = second_order[-1]
    bit = (lax.axis_index("pcol") // last) & 1
    for g in range(ratio):
        for s in range(slots):
            zt[g, 2 * s * half : (2 * s + 1) * half, :] = first_ref[slot(g * slots + s, first_order)]
            if s & last == 0:
                for ref, place in ((second_ref, bit), (came_ref, 1 - bit)):
                    at = pl.multiple_of((2 * s + 1) * half + place * (2 * last * half), half)
                    zt[g, pl.ds(at, half), :] = ref[slot(g * slots + s, second_order[:-1])]
    wide = 2
    for i in range(0, col_tiles, wide):
        turned = [zt[g, :, b * tile : (b + 1) * tile].T for b in range(i, i + wide) for g in range(ratio)]
        total = dot(stack_left(jnp.concatenate(turned, axis=0)), uc_ref[...])
        for g in range(ratio * wide):
            at = i * ratio + g
            for b in range(col_tiles):
                values = a_ref[pl.ds(at * tile * col_tiles + b, tile, stride=col_tiles), :]
                cut = slice(b * tile, (b + 1) * tile)
                out_ref[at * tile : (at + 1) * tile, cut] = values - total[g * tile : (g + 1) * tile, cut]


def update_kernel(inner_upper, rest_ref, ur_ref, uc_ref, zc_ref, *refs):
    inners, (out_ref, inner, w, result, write) = refs[:4], refs[4:]
    near = lax.axis_index("pcol") & 3
    nb, cols = zc_ref.shape
    half = inners[0].shape[1]
    slots = nb // (2 * half)
    chunks, lines, tile = result.shape
    col_tiles = cols // tile
    rows = lines // col_tiles
    writes = [pltpu.make_async_copy(result.at[i], out_ref.at[pl.ds(i * lines, lines)], write.at[i]) for i in range(chunks)]
    for r in range(4):
        for u in range(slots // 4):
            for side in range(2):
                at = pl.multiple_of((2 * (u * 4 + (near ^ r)) + side) * half, half)
                inner[pl.ds(at, half), :] = inners[r][slot(u, inner_upper), :, side * nb : (side + 1) * nb]
    stack_right(w, zc_ref[...] - dot3(split(inner[...]), (uc_ref[:nb, :], uc_ref[nb : 2 * nb, :])))
    for i in range(chunks):
        at = slice(i * rows, (i + 1) * rows)
        total = rest_ref[at, :] - dot(ur_ref[at, :], w[...])
        for g in range(rows // tile):
            for b in range(col_tiles):
                line = pl.ds(g * tile * col_tiles + b, tile, stride=col_tiles)
                result[i, line, :] = total[g * tile : (g + 1) * tile, b * tile : (b + 1) * tile]
        writes[i].start()
    for copy in writes:
        copy.wait()


def shape(*dims, dtype=F32):
    return jax.ShapeDtypeStruct(dims, dtype)


def per_device(trailing, reflectors, tfactor):
    row_tiles, _, tile, col_tiles = trailing.shape[:4]
    np_, nc = lax.axis_size("prow"), lax.axis_size("pcol")
    ratio = nc // np_
    ny = np_ // 2
    rows, cols = row_tiles * tile, col_tiles * tile
    nb = tfactor.shape[0]
    part = nb // np_
    half = row_tiles // 2
    block = trailing.reshape(rows * col_tiles, tile)
    mine = jnp.transpose(reflectors.reshape(row_tiles, tile, -1), (0, 2, 1))

    masks, cols_order = halving(nc), halving(np_)
    lead, rest = masks[: len(masks) - len(cols_order)], masks[len(masks) - len(cols_order) :]
    shift = len(cols_order)
    prow, pcol = lax.axis_index("prow").astype(jnp.int32), lax.axis_index("pcol").astype(jnp.int32)
    group = pcol >> shift
    where = {
        "group": group,
        "rounds": [(prow >> 1) ^ r for r in range(ny)],
        "share": (pcol & (np_ - 1)) * part,
        "col": {mask: (pcol & mask) != 0 for mask in masks},
        "row": {mask: (prow & mask) != 0 for mask in cols_order},
        "half": {mask: [jnp.where((prow & mask) != 0, 1 - side, side) for side in range(2)] for mask in cols_order},
    }
    mine, where = lax.optimization_barrier((mine, where))
    group, col, row = where["group"], where["col"], where["row"]
    whole = pl.BlockSpec(memory_space=pltpu.VMEM)

    def flat(p, q):
        return p * nc + q

    def turn(values, r):
        perm = [
            (flat(p, g * np_ + s), flat(s, g * np_ + (p ^ r))) for p in range(np_) for g in range(ratio) for s in range(np_)
        ]
        return lax.ppermute(values, BOTH, perm)

    inner_upper = [mask // 4 for mask in rest[:-2]]
    far, close = rest[-2:]
    orders = (masks, masks[:-2] + [close, far])
    a_high, a_low = pl.pallas_call(
        functools.partial(split_block_kernel, col_tiles, tile),
        out_shape=[shape(rows, cols, dtype=BF16)] * 2,
        in_specs=[whole],
        out_specs=[whole] * 2,
        compiler_params=VMEM,
        cost_estimate=pl.CostEstimate(flops=rows * cols * 4, bytes_accessed=rows * cols * 8, transcendentals=0),
    )(block)
    first, second = lax.optimization_barrier(mine[None, :half]), lax.optimization_barrier(mine[None, half:])
    for at, (mask, other) in enumerate(zip(*orders)):
        first_came, second_came = swap(first, "pcol", mask), swap(second, "pcol", other)
        if at == 0:
            second_came, a_high, a_low = lax.optimization_barrier((second_came, a_high, a_low))
        first, second = join(first, first_came, col[mask]), join(second, second_came, col[other])

    y_rows, keep, send = pl.pallas_call(
        functools.partial(product_kernel, orders),
        out_shape=[shape(row_tiles, nb, tile), shape(ny, part, cols), shape(ny, part, cols)],
        in_specs=[whole] * 4,
        out_specs=[whole] * 3,
        scratch_shapes=[pltpu.VMEM((nb, rows), BF16), pltpu.VMEM((nb, rows), BF16), pltpu.VMEM((nb, cols), F32)],
        compiler_params=VMEM,
        cost_estimate=pl.CostEstimate(flops=6 * nb * rows * cols, bytes_accessed=rows * cols * 8, transcendentals=0),
    )(a_high, a_low, first, second)
    other = swap(send, "prow", 1)
    kept = keep + other
    y_piece = lax.dynamic_slice(
        y_rows.reshape(col_tiles, ratio, nb, tile), (0, group, where["share"], 0), (col_tiles, 1, part, tile)
    )
    y_piece = jnp.transpose(y_piece.reshape(col_tiles, part, tile), (1, 0, 2)).reshape(part, cols)

    turned = []
    for r in range(ny):
        message = lax.dynamic_index_in_dim(kept, where["rounds"][r], 0, keepdims=False)
        turned.append(turn(message, 2 * r))
    turned = sum(turned[1:], turned[0])
    y_piece, kept = lax.optimization_barrier((y_piece, kept))
    for mask in cols_order[:-1]:
        low, high = where["half"][mask]
        pair = kept.reshape(2, mask // 2, part, cols)
        kept = lax.dynamic_index_in_dim(pair, low, 0, keepdims=False)
        kept = kept + swap(lax.dynamic_index_in_dim(pair, high, 0, keepdims=False), "prow", mask)
    piece = kept.reshape(part, cols)
    y_cols = turn(y_piece, 0).reshape(2, part // 2, cols)
    u_rows = pl.pallas_call(
        row_factor_kernel,
        out_shape=shape(rows, 3 * nb, dtype=BF16),
        in_specs=[whole] * 2,
        out_specs=whole,
        compiler_params=VMEM,
        cost_estimate=pl.CostEstimate(flops=6 * nb * nb * rows, bytes_accessed=rows * nb * 8, transcendentals=0),
    )(tfactor, y_rows)
    turned, u_rows = lax.optimization_barrier((turned, u_rows))
    first, second = turned[None, : part // 2], turned[None, part // 2 :]
    first, second = lax.optimization_barrier(first), lax.optimization_barrier(second)
    columns = jnp.concatenate([piece.reshape(2, part // 2, cols), y_cols])
    for mask in lead:
        first = join(first, swap(first, "pcol", mask), col[mask])
        second = join(second, swap(second, "pcol", mask), col[mask])
    first, columns = lax.optimization_barrier((first, columns))
    first_group, second_group = first, second
    for mask in rest[:-2]:
        first = join(first, swap(first, "pcol", mask), col[mask])
        second = join(second, swap(second, "pcol", mask), col[mask])
    first = join(first, swap(first, "pcol", far), col[far])
    second = join(second, swap(second, "pcol", close), col[close])

    columns = gather(columns, "prow", cols_order, row)
    first, y_rows = lax.optimization_barrier((first, y_rows))
    inner = pl.pallas_call(
        inner_kernel,
        out_shape=shape(part // 2, 2 * nb),
        in_specs=[whole] * 3,
        out_specs=whole,
        compiler_params=VMEM,
        cost_estimate=pl.CostEstimate(flops=6 * nb * part * cols, bytes_accessed=cols * nb * 4, transcendentals=0),
    )(first_group, second_group, y_rows)
    for mask in cols_order[::-1]:
        inner = inner + swap(inner, "prow", mask)
    inner = inner[None]
    for mask in rest[:-2]:
        inner = join(inner, swap(inner, "pcol", mask), col[mask])
    u_cols, zc = pl.pallas_call(
        functools.partial(column_factor_kernel, cols_order),
        out_shape=[shape(3 * nb, cols, dtype=BF16), shape(nb, cols)],
        in_specs=[whole] * 2,
        out_specs=[whole] * 2,
        scratch_shapes=[pltpu.VMEM((nb, cols), F32)],
        compiler_params=VMEM,
        cost_estimate=pl.CostEstimate(flops=6 * nb * nb * cols, bytes_accessed=cols * nb * 8, transcendentals=0),
    )(tfactor, columns)

    near_inner = [inner] + [swap(inner, "pcol", mask) for mask in (close, far, close + far)]
    first = join(first, swap(first, "pcol", close), col[close])
    second_came = swap(second, "pcol", far)

    remainder = pl.pallas_call(
        functools.partial(rows_kernel, orders),
        out_shape=shape(rows, cols),
        in_specs=[whole] * 5,
        out_specs=whole,
        scratch_shapes=[pltpu.VMEM((ratio, nb, cols), F32)],
        compiler_params=VMEM,
        cost_estimate=pl.CostEstimate(flops=6 * nb * rows * cols, bytes_accessed=rows * cols * 8, transcendentals=0),
    )(block, u_cols, first, second, second_came)
    chunks = 4
    lines = rows * col_tiles // chunks
    result = pl.pallas_call(
        functools.partial(update_kernel, inner_upper),
        out_shape=shape(rows * col_tiles, tile),
        in_specs=[whole] * 8,
        out_specs=pl.BlockSpec(memory_space=pltpu.HBM),
        scratch_shapes=[
            pltpu.VMEM((nb, nb), F32),
            pltpu.VMEM((3 * nb, cols), BF16),
            pltpu.VMEM((chunks, lines, tile), F32),
            pltpu.SemaphoreType.DMA((chunks,)),
        ],
        compiler_params=VMEM,
        cost_estimate=pl.CostEstimate(flops=6 * nb * rows * cols, bytes_accessed=rows * cols * 8, transcendentals=0),
    )(remainder, u_rows, u_cols, zc, *near_inner)
    return result.reshape(trailing.shape)


def solution(mesh):
    return jax.shard_map(
        per_device,
        mesh=mesh,
        in_specs=(P(None, "prow", None, None, "pcol", None), P(None, "prow", None, "pcol"), P()),
        out_specs=P(None, "prow", None, None, "pcol", None),
        check_vma=False,
    )
```

```python
import functools

import jax
import jax.numpy as jnp
from jax import lax
from jax.experimental import pallas as pl
from jax.experimental.pallas import tpu as pltpu
from jax.sharding import PartitionSpec as P

BOTH = ("prow", "pcol")
F32 = jnp.float32
BF16 = jnp.bfloat16
VMEM = pltpu.CompilerParams(vmem_limit_bytes=8 * 1024 * 1024)


def split(values):
    high = values.astype(BF16)
    return high, (values - high.astype(F32)).astype(BF16)


def dot(left, right, dims=((1,), (0,))):
    return lax.dot_general(left, right, (dims, ((), ())), preferred_element_type=F32)


def dot3(left, right, dims=((1,), (0,))):
    (lh, ll), (rh, rl) = left, right
    return dot(lh, rh, dims) + (dot(lh, rl, dims) + dot(ll, rh, dims))


def swap(values, axis, mask):
    n = lax.axis_size(axis)
    return lax.ppermute(values, axis, [(i, i ^ mask) for i in range(n)])


def halving(n):
    masks = []
    while n > 1:
        n //= 2
        masks.append(n)
    return masks


def join(values, other, high):
    pair = jnp.stack([jnp.where(high, other, values), jnp.where(high, values, other)])
    return pair.reshape((-1,) + values.shape[1:])


def gather(values, axis, masks, above):
    values = values[None]
    for mask in masks:
        values = join(values, swap(values, axis, mask), above[mask])
    return values


def slot(index, masks):
    return sum(1 << j for j, mask in enumerate(masks) if index & mask)


def swap_three(values, axis):
    return [swap(values, axis, mask) for mask in (1, 2, 3)]


def split_block_kernel(col_tiles, tile, a_ref, high_ref, low_ref, copy_ref):
    rows = high_ref.shape[0]
    for b in range(col_tiles):
        cols = slice(b * tile, (b + 1) * tile)
        values = a_ref[pl.ds(b, rows, stride=col_tiles), :]
        copy_ref[:, cols] = values
        high, low = split(values)
        high_ref[:, cols] = high
        low_ref[:, cols] = low


def product_kernel(orders, ah_ref, al_ref, first_ref, second_ref, y_ref, keep_ref, send_ref, yh, yl, total):
    nc, half, width, tile = first_ref.shape
    for chunk, (ref, masks) in enumerate(zip((first_ref, second_ref), orders)):
        for a in range(half):
            at = chunk * half + a
            for j in range(nc):
                y_ref[at, j * width : (j + 1) * width, :] = ref[slot(j, masks), a]
            cols = slice(at * tile, (at + 1) * tile)
            yh[:, cols], yl[:, cols] = split(y_ref[at])
    total[...] = dot3((yh[...], yl[...]), (ah_ref[...], al_ref[...]))
    core = lax.axis_index("prow") & 1
    count, part = keep_ref.shape[:2]
    for y in range(count):
        keep_ref[y] = total[pl.ds(pl.multiple_of((2 * y + core) * part, part), part), :]
        send_ref[y] = total[pl.ds(pl.multiple_of((2 * y + 1 - core) * part, part), part), :]


def inner_kernel(first_ref, second_ref, y_ref, inner_ref):
    row_tiles, nb, tile = y_ref.shape
    ratio, half, cols = first_ref.shape
    inner = jnp.zeros((2 * half, nb), F32)
    for g in range(ratio):
        for b in range(cols // tile):
            at = slice(b * tile, (b + 1) * tile)
            left = jnp.concatenate([first_ref[g, :, at], second_ref[g, :, at]], axis=0)
            inner += dot3(split(left), split(y_ref[b * ratio + g]), ((1,), (1,)))
    for side in range(2):
        inner_ref[:, side * nb : (side + 1) * nb] = inner[side * half : (side + 1) * half]


def stack_left(values):
    high, low = split(values)
    return jnp.concatenate([high, high, low], axis=1)


def stack_right(ref, values):
    rows = values.shape[0]
    high, low = split(values)
    ref[:rows, :] = high
    ref[rows : 2 * rows, :] = low
    ref[2 * rows :, :] = high


def row_factor_kernel(t_ref, y_ref, out_ref):
    row_tiles, nb, tile = y_ref.shape
    factor = split(t_ref[...])
    for a in range(row_tiles):
        out_ref[a * tile : (a + 1) * tile, :] = stack_left(dot3(factor, split(y_ref[a])).T)


def column_factor_kernel(order, t_ref, cols_ref, out_ref, z_ref, y):
    slots, _, half, _ = cols_ref.shape
    for s in range(slots):
        for side in range(2):
            rows = slice((2 * s + side) * half, (2 * s + side + 1) * half)
            z_ref[rows, :] = cols_ref[slot(s, order), side]
            y[rows, :] = cols_ref[slot(s, order), 2 + side]
    stack_right(out_ref, dot3(split(t_ref[...]), split(y[...])))


def rows_kernel(orders, col_tiles, a_ref, uc_ref, first_ref, second_ref, came_ref, out_ref, zt):
    ratio, nb, cols = zt.shape
    half = first_ref.shape[1]
    slots = nb // (2 * half)
    tile = cols // col_tiles
    first_order, second_order = orders
    last = second_order[-1]
    bit = (lax.axis_index("pcol") // last) & 1
    for g in range(ratio):
        for s in range(slots):
            zt[g, 2 * s * half : (2 * s + 1) * half, :] = first_ref[slot(g * slots + s, first_order)]
            if s & last == 0:
                for ref, place in ((second_ref, bit), (came_ref, 1 - bit)):
                    at = pl.multiple_of((2 * s + 1) * half + place * (2 * last * half), half)
                    zt[g, pl.ds(at, half), :] = ref[slot(g * slots + s, second_order[:-1])]
    wide = 2
    for i in range(0, col_tiles, wide):
        turned = [zt[g, :, b * tile : (b + 1) * tile].T for b in range(i, i + wide) for g in range(ratio)]
        total = dot(stack_left(jnp.concatenate(turned, axis=0)), uc_ref[...])
        for g in range(ratio * wide):
            at = i * ratio + g
            cut = slice(at * tile, (at + 1) * tile)
            out_ref[cut, :] = a_ref[cut, :] - total[g * tile : (g + 1) * tile, :]


def update_kernel(inner_upper, rest_ref, ur_ref, uc_ref, zc_ref, *refs):
    inners, (out_ref, inner, w, result, write) = refs[:4], refs[4:]
    near = lax.axis_index("pcol") & 3
    nb, cols = zc_ref.shape
    half = inners[0].shape[1]
    slots = nb // (2 * half)
    chunks, lines, tile = result.shape
    col_tiles = cols // tile
    rows = lines // col_tiles
    writes = [pltpu.make_async_copy(result.at[i], out_ref.at[pl.ds(i * lines, lines)], write.at[i]) for i in range(chunks)]
    for r in range(4):
        for u in range(slots // 4):
            for side in range(2):
                at = pl.multiple_of((2 * (u * 4 + (near ^ r)) + side) * half, half)
                inner[pl.ds(at, half), :] = inners[r][slot(u, inner_upper), :, side * nb : (side + 1) * nb]
    stack_right(w, zc_ref[...] - dot3(split(inner[...]), (uc_ref[:nb, :], uc_ref[nb : 2 * nb, :])))
    for i in range(chunks):
        at = slice(i * rows, (i + 1) * rows)
        total = rest_ref[at, :] - dot(ur_ref[at, :], w[...])
        for g in range(rows // tile):
            for b in range(col_tiles):
                line = pl.ds(g * tile * col_tiles + b, tile, stride=col_tiles)
                result[i, line, :] = total[g * tile : (g + 1) * tile, b * tile : (b + 1) * tile]
        writes[i].start()
    for copy in writes:
        copy.wait()


def shape(*dims, dtype=F32):
    return jax.ShapeDtypeStruct(dims, dtype)


def per_device(trailing, reflectors, tfactor):
    row_tiles, _, tile, col_tiles = trailing.shape[:4]
    np_, nc = lax.axis_size("prow"), lax.axis_size("pcol")
    ratio = nc // np_
    ny = np_ // 2
    rows, cols = row_tiles * tile, col_tiles * tile
    nb = tfactor.shape[0]
    part = nb // np_
    half = row_tiles // 2
    block = trailing.reshape(rows * col_tiles, tile)
    mine = jnp.transpose(reflectors.reshape(row_tiles, tile, -1), (0, 2, 1))

    masks, cols_order = halving(nc), halving(np_)
    lead, rest = masks[: len(masks) - len(cols_order)], masks[len(masks) - len(cols_order) :]
    shift = len(cols_order)
    prow, pcol = lax.axis_index("prow").astype(jnp.int32), lax.axis_index("pcol").astype(jnp.int32)
    group = pcol >> shift
    where = {
        "group": group,
        "rounds": [(prow >> 1) ^ r for r in range(ny)],
        "share": (pcol & (np_ - 1)) * part,
        "col": {mask: (pcol & mask) != 0 for mask in masks},
        "row": {mask: (prow & mask) != 0 for mask in cols_order},
        "half": {mask: [jnp.where((prow & mask) != 0, 1 - side, side) for side in range(2)] for mask in cols_order},
    }
    mine, where = lax.optimization_barrier((mine, where))
    group, col, row = where["group"], where["col"], where["row"]
    whole = pl.BlockSpec(memory_space=pltpu.VMEM)

    def flat(p, q):
        return p * nc + q

    def turn(values, r):
        perm = [
            (flat(p, g * np_ + s), flat(s, g * np_ + (p ^ r))) for p in range(np_) for g in range(ratio) for s in range(np_)
        ]
        return lax.ppermute(values, BOTH, perm)

    inner_upper = [mask // 4 for mask in rest[:-2]]
    far, close = rest[-2:]
    orders = (masks, masks[:-2] + [close, far])
    a_high, a_low, a_full = pl.pallas_call(
        functools.partial(split_block_kernel, col_tiles, tile),
        out_shape=[shape(rows, cols, dtype=BF16)] * 2 + [shape(rows, cols)],
        in_specs=[whole],
        out_specs=[whole] * 3,
        compiler_params=VMEM,
        cost_estimate=pl.CostEstimate(flops=rows * cols * 4, bytes_accessed=rows * cols * 8, transcendentals=0),
    )(block)
    first, second = lax.optimization_barrier(mine[None, :half]), lax.optimization_barrier(mine[None, half:])
    for at, (mask, other) in enumerate(zip(*orders)):
        first_came, second_came = swap(first, "pcol", mask), swap(second, "pcol", other)
        if at == 0:
            second_came, a_high, a_low = lax.optimization_barrier((second_came, a_high, a_low))
        first, second = join(first, first_came, col[mask]), join(second, second_came, col[other])

    y_rows, keep, send = pl.pallas_call(
        functools.partial(product_kernel, orders),
        out_shape=[shape(row_tiles, nb, tile), shape(ny, part, cols), shape(ny, part, cols)],
        in_specs=[whole] * 4,
        out_specs=[whole] * 3,
        scratch_shapes=[pltpu.VMEM((nb, rows), BF16), pltpu.VMEM((nb, rows), BF16), pltpu.VMEM((nb, cols), F32)],
        compiler_params=VMEM,
        cost_estimate=pl.CostEstimate(flops=6 * nb * rows * cols, bytes_accessed=rows * cols * 8, transcendentals=0),
    )(a_high, a_low, first, second)
    other = swap(send, "prow", 1)
    kept = keep + other
    y_piece = lax.dynamic_slice(
        y_rows.reshape(col_tiles, ratio, nb, tile), (0, group, where["share"], 0), (col_tiles, 1, part, tile)
    )
    y_piece = jnp.transpose(y_piece.reshape(col_tiles, part, tile), (1, 0, 2)).reshape(part, cols)

    turned = []
    for r in range(ny):
        message = lax.dynamic_index_in_dim(kept, where["rounds"][r], 0, keepdims=False)
        turned.append(turn(message, 2 * r))
    turned = sum(turned[1:], turned[0])
    y_piece, kept = lax.optimization_barrier((y_piece, kept))
    for mask in cols_order[:-1]:
        low, high = where["half"][mask]
        pair = kept.reshape(2, mask // 2, part, cols)
        kept = lax.dynamic_index_in_dim(pair, low, 0, keepdims=False)
        kept = kept + swap(lax.dynamic_index_in_dim(pair, high, 0, keepdims=False), "prow", mask)
    piece = kept.reshape(part, cols)
    y_cols = turn(y_piece, 0).reshape(2, part // 2, cols)
    u_rows = pl.pallas_call(
        row_factor_kernel,
        out_shape=shape(rows, 3 * nb, dtype=BF16),
        in_specs=[whole] * 2,
        out_specs=whole,
        compiler_params=VMEM,
        cost_estimate=pl.CostEstimate(flops=6 * nb * nb * rows, bytes_accessed=rows * nb * 8, transcendentals=0),
    )(tfactor, y_rows)
    turned, u_rows = lax.optimization_barrier((turned, u_rows))
    first, second = turned[None, : part // 2], turned[None, part // 2 :]
    first, second = lax.optimization_barrier(first), lax.optimization_barrier(second)
    columns = jnp.concatenate([piece.reshape(2, part // 2, cols), y_cols])
    for mask in lead:
        first = join(first, swap(first, "pcol", mask), col[mask])
        second = join(second, swap(second, "pcol", mask), col[mask])
    first, columns = lax.optimization_barrier((first, columns))
    first_group, second_group = first, second
    for mask in rest[:-2]:
        first = join(first, swap(first, "pcol", mask), col[mask])
        second = join(second, swap(second, "pcol", mask), col[mask])
    first = join(first, swap(first, "pcol", far), col[far])
    second = join(second, swap(second, "pcol", close), col[close])

    columns = gather(columns, "prow", cols_order, row)
    first, y_rows = lax.optimization_barrier((first, y_rows))
    inner = pl.pallas_call(
        inner_kernel,
        out_shape=shape(part // 2, 2 * nb),
        in_specs=[whole] * 3,
        out_specs=whole,
        compiler_params=VMEM,
        cost_estimate=pl.CostEstimate(flops=6 * nb * part * cols, bytes_accessed=cols * nb * 4, transcendentals=0),
    )(first_group, second_group, y_rows)
    for mask in cols_order[::-1]:
        inner = inner + swap(inner, "prow", mask)
    inner = inner[None]
    for mask in rest[:-2]:
        inner = join(inner, swap(inner, "pcol", mask), col[mask])
    u_cols, zc = pl.pallas_call(
        functools.partial(column_factor_kernel, cols_order),
        out_shape=[shape(3 * nb, cols, dtype=BF16), shape(nb, cols)],
        in_specs=[whole] * 2,
        out_specs=[whole] * 2,
        scratch_shapes=[pltpu.VMEM((nb, cols), F32)],
        compiler_params=VMEM,
        cost_estimate=pl.CostEstimate(flops=6 * nb * nb * cols, bytes_accessed=cols * nb * 8, transcendentals=0),
    )(tfactor, columns)

    near_inner = [inner] + [swap(inner, "pcol", mask) for mask in (close, far, close + far)]
    first = join(first, swap(first, "pcol", close), col[close])
    second_came = swap(second, "pcol", far)

    remainder = pl.pallas_call(
        functools.partial(rows_kernel, orders, col_tiles),
        out_shape=shape(rows, cols),
        in_specs=[whole] * 5,
        out_specs=whole,
        scratch_shapes=[pltpu.VMEM((ratio, nb, cols), F32)],
        compiler_params=VMEM,
        cost_estimate=pl.CostEstimate(flops=6 * nb * rows * cols, bytes_accessed=rows * cols * 8, transcendentals=0),
    )(a_full, u_cols, first, second, second_came)
    chunks = 4
    lines = rows * col_tiles // chunks
    result = pl.pallas_call(
        functools.partial(update_kernel, inner_upper),
        out_shape=shape(rows * col_tiles, tile),
        in_specs=[whole] * 8,
        out_specs=pl.BlockSpec(memory_space=pltpu.HBM),
        scratch_shapes=[
            pltpu.VMEM((nb, nb), F32),
            pltpu.VMEM((3 * nb, cols), BF16),
            pltpu.VMEM((chunks, lines, tile), F32),
            pltpu.SemaphoreType.DMA((chunks,)),
        ],
        compiler_params=VMEM,
        cost_estimate=pl.CostEstimate(flops=6 * nb * rows * cols, bytes_accessed=rows * cols * 8, transcendentals=0),
    )(remainder, u_rows, u_cols, zc, *near_inner)
    return result.reshape(trailing.shape)


def solution(mesh):
    return jax.shard_map(
        per_device,
        mesh=mesh,
        in_specs=(P(None, "prow", None, None, "pcol", None), P(None, "prow", None, "pcol"), P()),
        out_specs=P(None, "prow", None, None, "pcol", None),
        check_vma=False,
    )
```

```python
import functools

import jax
import jax.numpy as jnp
from jax import lax
from jax.experimental import pallas as pl
from jax.experimental.pallas import tpu as pltpu
from jax.sharding import PartitionSpec as P

BOTH = ("prow", "pcol")
F32 = jnp.float32
BF16 = jnp.bfloat16
VMEM = pltpu.CompilerParams(vmem_limit_bytes=8 * 1024 * 1024)


def split(values):
    high = values.astype(BF16)
    return high, (values - high.astype(F32)).astype(BF16)


def dot(left, right, dims=((1,), (0,))):
    return lax.dot_general(left, right, (dims, ((), ())), preferred_element_type=F32)


def dot3(left, right, dims=((1,), (0,))):
    (lh, ll), (rh, rl) = left, right
    return dot(lh, rh, dims) + (dot(lh, rl, dims) + dot(ll, rh, dims))


def swap(values, axis, mask):
    n = lax.axis_size(axis)
    return lax.ppermute(values, axis, [(i, i ^ mask) for i in range(n)])


def halving(n):
    masks = []
    while n > 1:
        n //= 2
        masks.append(n)
    return masks


def pick(values, index):
    start = (index,) + (jnp.uint32(0),) * (values.ndim - 1)
    return lax.dynamic_slice(values, start, (1,) + values.shape[1:])[0]


def join(values, other, high):
    pair = jnp.stack([jnp.where(high, other, values), jnp.where(high, values, other)])
    return pair.reshape((-1,) + values.shape[1:])


def gather(values, axis, masks, above):
    values = values[None]
    for mask in masks:
        values = join(values, swap(values, axis, mask), above[mask])
    return values


def slot(index, masks):
    return sum(1 << j for j, mask in enumerate(masks) if index & mask)


def swap_three(values, axis):
    return [swap(values, axis, mask) for mask in (1, 2, 3)]


def split_block_kernel(col_tiles, tile, a_ref, high_ref, low_ref, copy_ref):
    rows = high_ref.shape[0]
    for b in range(col_tiles):
        cols = slice(b * tile, (b + 1) * tile)
        values = a_ref[pl.ds(b, rows, stride=col_tiles), :]
        copy_ref[:, cols] = values
        high, low = split(values)
        high_ref[:, cols] = high
        low_ref[:, cols] = low


def product_kernel(orders, ah_ref, al_ref, first_ref, second_ref, y_ref, keep_ref, send_ref, yh, yl, total):
    nc, half, width, tile = first_ref.shape
    for chunk, (ref, masks) in enumerate(zip((first_ref, second_ref), orders)):
        for a in range(half):
            at = chunk * half + a
            for j in range(nc):
                y_ref[at, j * width : (j + 1) * width, :] = ref[slot(j, masks), a]
            cols = slice(at * tile, (at + 1) * tile)
            yh[:, cols], yl[:, cols] = split(y_ref[at])
    total[...] = dot3((yh[...], yl[...]), (ah_ref[...], al_ref[...]))
    core = lax.axis_index("prow") & 1
    count, part = keep_ref.shape[:2]
    for y in range(count):
        keep_ref[y] = total[pl.ds(pl.multiple_of((2 * y + core) * part, part), part), :]
        send_ref[y] = total[pl.ds(pl.multiple_of((2 * y + 1 - core) * part, part), part), :]


def inner_kernel(first_ref, second_ref, y_ref, inner_ref):
    row_tiles, nb, tile = y_ref.shape
    ratio, half, cols = first_ref.shape
    inner = jnp.zeros((2 * half, nb), F32)
    for g in range(ratio):
        for b in range(cols // tile):
            at = slice(b * tile, (b + 1) * tile)
            left = jnp.concatenate([first_ref[g, :, at], second_ref[g, :, at]], axis=0)
            inner += dot3(split(left), split(y_ref[b * ratio + g]), ((1,), (1,)))
    for side in range(2):
        inner_ref[:, side * nb : (side + 1) * nb] = inner[side * half : (side + 1) * half]


def stack_left(values):
    high, low = split(values)
    return jnp.concatenate([high, high, low], axis=1)


def stack_right(ref, values):
    rows = values.shape[0]
    high, low = split(values)
    ref[:rows, :] = high
    ref[rows : 2 * rows, :] = low
    ref[2 * rows :, :] = high


def row_factor_kernel(t_ref, y_ref, out_ref):
    row_tiles, nb, tile = y_ref.shape
    factor = split(t_ref[...])
    for a in range(row_tiles):
        out_ref[a * tile : (a + 1) * tile, :] = stack_left(dot3(factor, split(y_ref[a])).T)


def column_factor_kernel(order, t_ref, cols_ref, out_ref, z_ref, y):
    slots, _, half, _ = cols_ref.shape
    for s in range(slots):
        for side in range(2):
            rows = slice((2 * s + side) * half, (2 * s + side + 1) * half)
            z_ref[rows, :] = cols_ref[slot(s, order), side]
            y[rows, :] = cols_ref[slot(s, order), 2 + side]
    stack_right(out_ref, dot3(split(t_ref[...]), split(y[...])))


def rows_kernel(orders, col_tiles, a_ref, uc_ref, first_ref, second_ref, came_ref, out_ref, zt):
    ratio, nb, cols = zt.shape
    half = first_ref.shape[1]
    slots = nb // (2 * half)
    tile = cols // col_tiles
    first_order, second_order = orders
    last = second_order[-1]
    bit = (lax.axis_index("pcol") // last) & 1
    for g in range(ratio):
        for s in range(slots):
            zt[g, 2 * s * half : (2 * s + 1) * half, :] = first_ref[slot(g * slots + s, first_order)]
            if s & last == 0:
                for ref, place in ((second_ref, bit), (came_ref, 1 - bit)):
                    at = pl.multiple_of((2 * s + 1) * half + place * (2 * last * half), half)
                    zt[g, pl.ds(at, half), :] = ref[slot(g * slots + s, second_order[:-1])]
    wide = 2
    for i in range(0, col_tiles, wide):
        turned = [zt[g, :, b * tile : (b + 1) * tile].T for b in range(i, i + wide) for g in range(ratio)]
        total = dot(stack_left(jnp.concatenate(turned, axis=0)), uc_ref[...])
        for g in range(ratio * wide):
            at = i * ratio + g
            cut = slice(at * tile, (at + 1) * tile)
            out_ref[cut, :] = a_ref[cut, :] - total[g * tile : (g + 1) * tile, :]


def update_kernel(inner_upper, rest_ref, ur_ref, uc_ref, zc_ref, *refs):
    inners, (out_ref, inner, w, result, write) = refs[:4], refs[4:]
    near = lax.axis_index("pcol") & 3
    nb, cols = zc_ref.shape
    half = inners[0].shape[1]
    slots = nb // (2 * half)
    chunks, lines, tile = result.shape
    col_tiles = cols // tile
    rows = lines // col_tiles
    writes = [pltpu.make_async_copy(result.at[i], out_ref.at[pl.ds(i * lines, lines)], write.at[i]) for i in range(chunks)]
    for r in range(4):
        for u in range(slots // 4):
            for side in range(2):
                at = pl.multiple_of((2 * (u * 4 + (near ^ r)) + side) * half, half)
                inner[pl.ds(at, half), :] = inners[r][slot(u, inner_upper), :, side * nb : (side + 1) * nb]
    stack_right(w, zc_ref[...] - dot3(split(inner[...]), (uc_ref[:nb, :], uc_ref[nb : 2 * nb, :])))
    for i in range(chunks):
        at = slice(i * rows, (i + 1) * rows)
        total = rest_ref[at, :] - dot(ur_ref[at, :], w[...])
        for g in range(rows // tile):
            for b in range(col_tiles):
                line = pl.ds(g * tile * col_tiles + b, tile, stride=col_tiles)
                result[i, line, :] = total[g * tile : (g + 1) * tile, b * tile : (b + 1) * tile]
        writes[i].start()
    for copy in writes:
        copy.wait()


def shape(*dims, dtype=F32):
    return jax.ShapeDtypeStruct(dims, dtype)


def per_device(trailing, reflectors, tfactor):
    row_tiles, _, tile, col_tiles = trailing.shape[:4]
    np_, nc = lax.axis_size("prow"), lax.axis_size("pcol")
    ratio = nc // np_
    ny = np_ // 2
    rows, cols = row_tiles * tile, col_tiles * tile
    nb = tfactor.shape[0]
    part = nb // np_
    half = row_tiles // 2
    block = trailing.reshape(rows * col_tiles, tile)
    mine = jnp.transpose(reflectors.reshape(row_tiles, tile, -1), (0, 2, 1))

    masks, cols_order = halving(nc), halving(np_)
    lead, rest = masks[: len(masks) - len(cols_order)], masks[len(masks) - len(cols_order) :]
    shift = len(cols_order)
    prow, pcol = lax.axis_index("prow").astype(jnp.int32), lax.axis_index("pcol").astype(jnp.int32)
    group = pcol >> shift
    where = {
        "group": group.astype(jnp.uint32),
        "rounds": [((prow >> 1) ^ r).astype(jnp.uint32) for r in range(ny)],
        "share": ((pcol & (np_ - 1)) * part).astype(jnp.uint32),
        "col": {mask: (pcol & mask) != 0 for mask in masks},
        "row": {mask: (prow & mask) != 0 for mask in cols_order},
        "half": {mask: [((prow >> (mask.bit_length() - 1) & 1) ^ side).astype(jnp.uint32) for side in range(2)] for mask in cols_order},
    }
    mine, where = lax.optimization_barrier((mine, where))
    group, col, row = where["group"], where["col"], where["row"]
    whole = pl.BlockSpec(memory_space=pltpu.VMEM)

    def flat(p, q):
        return p * nc + q

    def turn(values, r):
        perm = [
            (flat(p, g * np_ + s), flat(s, g * np_ + (p ^ r))) for p in range(np_) for g in range(ratio) for s in range(np_)
        ]
        return lax.ppermute(values, BOTH, perm)

    inner_upper = [mask // 4 for mask in rest[:-2]]
    far, close = rest[-2:]
    orders = (masks, masks[:-2] + [close, far])
    a_high, a_low, a_full = pl.pallas_call(
        functools.partial(split_block_kernel, col_tiles, tile),
        out_shape=[shape(rows, cols, dtype=BF16)] * 2 + [shape(rows, cols)],
        in_specs=[whole],
        out_specs=[whole] * 3,
        compiler_params=VMEM,
        cost_estimate=pl.CostEstimate(flops=rows * cols * 4, bytes_accessed=rows * cols * 8, transcendentals=0),
    )(block)
    first, second = lax.optimization_barrier(mine[None, :half]), lax.optimization_barrier(mine[None, half:])
    for at, (mask, other) in enumerate(zip(*orders)):
        first_came, second_came = swap(first, "pcol", mask), swap(second, "pcol", other)
        if at == 0:
            second_came, a_high, a_low = lax.optimization_barrier((second_came, a_high, a_low))
        first, second = join(first, first_came, col[mask]), join(second, second_came, col[other])

    y_rows, keep, send = pl.pallas_call(
        functools.partial(product_kernel, orders),
        out_shape=[shape(row_tiles, nb, tile), shape(ny, part, cols), shape(ny, part, cols)],
        in_specs=[whole] * 4,
        out_specs=[whole] * 3,
        scratch_shapes=[pltpu.VMEM((nb, rows), BF16), pltpu.VMEM((nb, rows), BF16), pltpu.VMEM((nb, cols), F32)],
        compiler_params=VMEM,
        cost_estimate=pl.CostEstimate(flops=6 * nb * rows * cols, bytes_accessed=rows * cols * 8, transcendentals=0),
    )(a_high, a_low, first, second)
    other = swap(send, "prow", 1)
    kept = keep + other
    zero = jnp.uint32(0)
    y_piece = lax.dynamic_slice(
        y_rows.reshape(col_tiles, ratio, nb, tile), (zero, group, where["share"], zero), (col_tiles, 1, part, tile)
    )
    y_piece = jnp.transpose(y_piece.reshape(col_tiles, part, tile), (1, 0, 2)).reshape(part, cols)

    turned = []
    for r in range(ny):
        message = pick(kept, where["rounds"][r])
        turned.append(turn(message, 2 * r))
    turned = sum(turned[1:], turned[0])
    y_piece, kept = lax.optimization_barrier((y_piece, kept))
    for mask in cols_order[:-1]:
        low, high = where["half"][mask]
        pair = kept.reshape(2, mask // 2, part, cols)
        kept = pick(pair, low)
        kept = kept + swap(pick(pair, high), "prow", mask)
    piece = kept.reshape(part, cols)
    y_cols = turn(y_piece, 0).reshape(2, part // 2, cols)
    u_rows = pl.pallas_call(
        row_factor_kernel,
        out_shape=shape(rows, 3 * nb, dtype=BF16),
        in_specs=[whole] * 2,
        out_specs=whole,
        compiler_params=VMEM,
        cost_estimate=pl.CostEstimate(flops=6 * nb * nb * rows, bytes_accessed=rows * nb * 8, transcendentals=0),
    )(tfactor, y_rows)
    turned, u_rows = lax.optimization_barrier((turned, u_rows))
    first, second = turned[None, : part // 2], turned[None, part // 2 :]
    first, second = lax.optimization_barrier(first), lax.optimization_barrier(second)
    columns = jnp.concatenate([piece.reshape(2, part // 2, cols), y_cols])
    for mask in lead:
        first = join(first, swap(first, "pcol", mask), col[mask])
        second = join(second, swap(second, "pcol", mask), col[mask])
    first, columns = lax.optimization_barrier((first, columns))
    first_group, second_group = first, second
    for mask in rest[:-2]:
        first = join(first, swap(first, "pcol", mask), col[mask])
        second = join(second, swap(second, "pcol", mask), col[mask])
    first = join(first, swap(first, "pcol", far), col[far])
    second = join(second, swap(second, "pcol", close), col[close])

    columns = gather(columns, "prow", cols_order, row)
    first, y_rows = lax.optimization_barrier((first, y_rows))
    inner = pl.pallas_call(
        inner_kernel,
        out_shape=shape(part // 2, 2 * nb),
        in_specs=[whole] * 3,
        out_specs=whole,
        compiler_params=VMEM,
        cost_estimate=pl.CostEstimate(flops=6 * nb * part * cols, bytes_accessed=cols * nb * 4, transcendentals=0),
    )(first_group, second_group, y_rows)
    for mask in cols_order[::-1]:
        inner = inner + swap(inner, "prow", mask)
    inner = inner[None]
    for mask in rest[:-2]:
        inner = join(inner, swap(inner, "pcol", mask), col[mask])
    u_cols, zc = pl.pallas_call(
        functools.partial(column_factor_kernel, cols_order),
        out_shape=[shape(3 * nb, cols, dtype=BF16), shape(nb, cols)],
        in_specs=[whole] * 2,
        out_specs=[whole] * 2,
        scratch_shapes=[pltpu.VMEM((nb, cols), F32)],
        compiler_params=VMEM,
        cost_estimate=pl.CostEstimate(flops=6 * nb * nb * cols, bytes_accessed=cols * nb * 8, transcendentals=0),
    )(tfactor, columns)

    near_inner = [inner] + [swap(inner, "pcol", mask) for mask in (close, far, close + far)]
    first = join(first, swap(first, "pcol", close), col[close])
    second_came = swap(second, "pcol", far)

    remainder = pl.pallas_call(
        functools.partial(rows_kernel, orders, col_tiles),
        out_shape=shape(rows, cols),
        in_specs=[whole] * 5,
        out_specs=whole,
        scratch_shapes=[pltpu.VMEM((ratio, nb, cols), F32)],
        compiler_params=VMEM,
        cost_estimate=pl.CostEstimate(flops=6 * nb * rows * cols, bytes_accessed=rows * cols * 8, transcendentals=0),
    )(a_full, u_cols, first, second, second_came)
    chunks = 4
    lines = rows * col_tiles // chunks
    result = pl.pallas_call(
        functools.partial(update_kernel, inner_upper),
        out_shape=shape(rows * col_tiles, tile),
        in_specs=[whole] * 8,
        out_specs=pl.BlockSpec(memory_space=pltpu.HBM),
        scratch_shapes=[
            pltpu.VMEM((nb, nb), F32),
            pltpu.VMEM((3 * nb, cols), BF16),
            pltpu.VMEM((chunks, lines, tile), F32),
            pltpu.SemaphoreType.DMA((chunks,)),
        ],
        compiler_params=VMEM,
        cost_estimate=pl.CostEstimate(flops=6 * nb * rows * cols, bytes_accessed=rows * cols * 8, transcendentals=0),
    )(remainder, u_rows, u_cols, zc, *near_inner)
    return result.reshape(trailing.shape)


def solution(mesh):
    return jax.shard_map(
        per_device,
        mesh=mesh,
        in_specs=(P(None, "prow", None, None, "pcol", None), P(None, "prow", None, "pcol"), P()),
        out_specs=P(None, "prow", None, None, "pcol", None),
        check_vma=False,
    )
```

```python
import functools

import jax
import jax.numpy as jnp
from jax import lax
from jax.experimental import pallas as pl
from jax.experimental.pallas import tpu as pltpu
from jax.sharding import PartitionSpec as P

BOTH = ("prow", "pcol")
F32 = jnp.float32
BF16 = jnp.bfloat16
VMEM = pltpu.CompilerParams(vmem_limit_bytes=8 * 1024 * 1024)


def split(values):
    high = values.astype(BF16)
    return high, (values - high.astype(F32)).astype(BF16)


def dot(left, right, dims=((1,), (0,))):
    return lax.dot_general(left, right, (dims, ((), ())), preferred_element_type=F32)


def dot3(left, right, dims=((1,), (0,))):
    (lh, ll), (rh, rl) = left, right
    return dot(lh, rh, dims) + (dot(lh, rl, dims) + dot(ll, rh, dims))


def swap(values, axis, mask):
    n = lax.axis_size(axis)
    return lax.ppermute(values, axis, [(i, i ^ mask) for i in range(n)])


def halving(n):
    masks = []
    while n > 1:
        n //= 2
        masks.append(n)
    return masks


def pick(values, index):
    start = (index,) + (jnp.uint32(0),) * (values.ndim - 1)
    return lax.dynamic_slice(values, start, (1,) + values.shape[1:])[0]


def join(values, other, high):
    pair = jnp.stack([jnp.where(high, other, values), jnp.where(high, values, other)])
    return pair.reshape((-1,) + values.shape[1:])


def gather(values, axis, masks, above):
    values = values[None]
    for mask in masks:
        values = join(values, swap(values, axis, mask), above[mask])
    return values


def slot(index, masks):
    return sum(1 << j for j, mask in enumerate(masks) if index & mask)


def swap_three(values, axis):
    return [swap(values, axis, mask) for mask in (1, 2, 3)]


def split_block_kernel(col_tiles, tile, a_ref, y_ref, high_ref, low_ref, copy_ref, y_copy_ref):
    y_copy_ref[...] = y_ref[...]
    rows = high_ref.shape[0]
    for b in range(col_tiles):
        cols = slice(b * tile, (b + 1) * tile)
        values = a_ref[pl.ds(b, rows, stride=col_tiles), :]
        copy_ref[:, cols] = values
        high, low = split(values)
        high_ref[:, cols] = high
        low_ref[:, cols] = low


def product_kernel(orders, ah_ref, al_ref, first_ref, second_ref, y_ref, keep_ref, send_ref, yh, yl, total):
    nc, half, width, tile = first_ref.shape
    for chunk, (ref, masks) in enumerate(zip((first_ref, second_ref), orders)):
        for a in range(half):
            at = chunk * half + a
            for j in range(nc):
                y_ref[at, j * width : (j + 1) * width, :] = ref[slot(j, masks), a]
            cols = slice(at * tile, (at + 1) * tile)
            yh[:, cols], yl[:, cols] = split(y_ref[at])
    total[...] = dot3((yh[...], yl[...]), (ah_ref[...], al_ref[...]))
    core = lax.axis_index("prow") & 1
    count, part = keep_ref.shape[:2]
    for y in range(count):
        keep_ref[y] = total[pl.ds(pl.multiple_of((2 * y + core) * part, part), part), :]
        send_ref[y] = total[pl.ds(pl.multiple_of((2 * y + 1 - core) * part, part), part), :]


def inner_kernel(first_ref, second_ref, y_ref, inner_ref):
    row_tiles, nb, tile = y_ref.shape
    ratio, half, cols = first_ref.shape
    inner = jnp.zeros((2 * half, nb), F32)
    for g in range(ratio):
        for b in range(cols // tile):
            at = slice(b * tile, (b + 1) * tile)
            left = jnp.concatenate([first_ref[g, :, at], second_ref[g, :, at]], axis=0)
            inner += dot3(split(left), split(y_ref[b * ratio + g]), ((1,), (1,)))
    for side in range(2):
        inner_ref[:, side * nb : (side + 1) * nb] = inner[side * half : (side + 1) * half]


def stack_left(values):
    high, low = split(values)
    return jnp.concatenate([high, high, low], axis=1)


def stack_right(ref, values):
    rows = values.shape[0]
    high, low = split(values)
    ref[:rows, :] = high
    ref[rows : 2 * rows, :] = low
    ref[2 * rows :, :] = high


def row_factor_kernel(t_ref, y_ref, out_ref):
    row_tiles, nb, tile = y_ref.shape
    factor = split(t_ref[...])
    for a in range(row_tiles):
        out_ref[a * tile : (a + 1) * tile, :] = stack_left(dot3(factor, split(y_ref[a])).T)


def column_factor_kernel(order, t_ref, cols_ref, out_ref, z_ref, y):
    slots, _, half, _ = cols_ref.shape
    for s in range(slots):
        for side in range(2):
            rows = slice((2 * s + side) * half, (2 * s + side + 1) * half)
            z_ref[rows, :] = cols_ref[slot(s, order), side]
            y[rows, :] = cols_ref[slot(s, order), 2 + side]
    stack_right(out_ref, dot3(split(t_ref[...]), split(y[...])))


def rows_kernel(orders, col_tiles, a_ref, uc_ref, first_ref, second_ref, came_ref, out_ref, zt):
    ratio, nb, cols = zt.shape
    half = first_ref.shape[1]
    slots = nb // (2 * half)
    tile = cols // col_tiles
    first_order, second_order = orders
    last = second_order[-1]
    bit = (lax.axis_index("pcol") // last) & 1
    for g in range(ratio):
        for s in range(slots):
            zt[g, 2 * s * half : (2 * s + 1) * half, :] = first_ref[slot(g * slots + s, first_order)]
            if s & last == 0:
                for ref, place in ((second_ref, bit), (came_ref, 1 - bit)):
                    at = pl.multiple_of((2 * s + 1) * half + place * (2 * last * half), half)
                    zt[g, pl.ds(at, half), :] = ref[slot(g * slots + s, second_order[:-1])]
    wide = 2
    for i in range(0, col_tiles, wide):
        turned = [zt[g, :, b * tile : (b + 1) * tile].T for b in range(i, i + wide) for g in range(ratio)]
        total = dot(stack_left(jnp.concatenate(turned, axis=0)), uc_ref[...])
        for g in range(ratio * wide):
            at = i * ratio + g
            cut = slice(at * tile, (at + 1) * tile)
            out_ref[cut, :] = a_ref[cut, :] - total[g * tile : (g + 1) * tile, :]


def update_kernel(inner_upper, rest_ref, ur_ref, uc_ref, zc_ref, *refs):
    inners, (out_ref, inner, w, result, write) = refs[:4], refs[4:]
    near = lax.axis_index("pcol") & 3
    nb, cols = zc_ref.shape
    half = inners[0].shape[1]
    slots = nb // (2 * half)
    chunks, lines, tile = result.shape
    col_tiles = cols // tile
    rows = lines // col_tiles
    writes = [pltpu.make_async_copy(result.at[i], out_ref.at[pl.ds(i * lines, lines)], write.at[i]) for i in range(chunks)]
    for r in range(4):
        for u in range(slots // 4):
            for side in range(2):
                at = pl.multiple_of((2 * (u * 4 + (near ^ r)) + side) * half, half)
                inner[pl.ds(at, half), :] = inners[r][slot(u, inner_upper), :, side * nb : (side + 1) * nb]
    stack_right(w, zc_ref[...] - dot3(split(inner[...]), (uc_ref[:nb, :], uc_ref[nb : 2 * nb, :])))
    for i in range(chunks):
        at = slice(i * rows, (i + 1) * rows)
        total = rest_ref[at, :] - dot(ur_ref[at, :], w[...])
        for g in range(rows // tile):
            for b in range(col_tiles):
                line = pl.ds(g * tile * col_tiles + b, tile, stride=col_tiles)
                result[i, line, :] = total[g * tile : (g + 1) * tile, b * tile : (b + 1) * tile]
        writes[i].start()
    for copy in writes:
        copy.wait()


def shape(*dims, dtype=F32):
    return jax.ShapeDtypeStruct(dims, dtype)


def per_device(trailing, reflectors, tfactor):
    row_tiles, _, tile, col_tiles = trailing.shape[:4]
    np_, nc = lax.axis_size("prow"), lax.axis_size("pcol")
    ratio = nc // np_
    ny = np_ // 2
    rows, cols = row_tiles * tile, col_tiles * tile
    nb = tfactor.shape[0]
    part = nb // np_
    half = row_tiles // 2
    block = trailing.reshape(rows * col_tiles, tile)
    mine = jnp.transpose(reflectors.reshape(row_tiles, tile, -1), (0, 2, 1))

    masks, cols_order = halving(nc), halving(np_)
    lead, rest = masks[: len(masks) - len(cols_order)], masks[len(masks) - len(cols_order) :]
    shift = len(cols_order)
    prow, pcol = lax.axis_index("prow").astype(jnp.int32), lax.axis_index("pcol").astype(jnp.int32)
    group = pcol >> shift
    where = {
        "group": group.astype(jnp.uint32),
        "rounds": [((prow >> 1) ^ r).astype(jnp.uint32) for r in range(ny)],
        "share": ((pcol & (np_ - 1)) * part).astype(jnp.uint32),
        "col": {mask: (pcol & mask) != 0 for mask in masks},
        "row": {mask: (prow & mask) != 0 for mask in cols_order},
        "half": {mask: [((prow >> (mask.bit_length() - 1) & 1) ^ side).astype(jnp.uint32) for side in range(2)] for mask in cols_order},
    }
    mine, where = lax.optimization_barrier((mine, where))
    group, col, row = where["group"], where["col"], where["row"]
    whole = pl.BlockSpec(memory_space=pltpu.VMEM)

    def flat(p, q):
        return p * nc + q

    def turn(values, r):
        perm = [
            (flat(p, g * np_ + s), flat(s, g * np_ + (p ^ r))) for p in range(np_) for g in range(ratio) for s in range(np_)
        ]
        return lax.ppermute(values, BOTH, perm)

    inner_upper = [mask // 4 for mask in rest[:-2]]
    far, close = rest[-2:]
    orders = (masks, masks[:-2] + [close, far])
    a_high, a_low, a_full, y = pl.pallas_call(
        functools.partial(split_block_kernel, col_tiles, tile),
        out_shape=[shape(rows, cols, dtype=BF16)] * 2 + [shape(rows, cols), shape(*mine.shape)],
        in_specs=[whole] * 2,
        out_specs=[whole] * 4,
        compiler_params=VMEM,
        cost_estimate=pl.CostEstimate(flops=rows * cols * 4, bytes_accessed=rows * cols * 8, transcendentals=0),
    )(block, mine)
    y = y[None]
    for at, mask in enumerate(lead):
        y = join(y, swap(mine[None] if at == 0 else y, "pcol", mask), col[mask])
    first, second = lax.optimization_barrier(y[:, :half]), lax.optimization_barrier(y[:, half:])
    for mask, other in zip(orders[0][len(lead) :], orders[1][len(lead) :]):
        first_came, second_came = swap(first, "pcol", mask), swap(second, "pcol", other)
        first, second = join(first, first_came, col[mask]), join(second, second_came, col[other])

    y_rows, keep, send = pl.pallas_call(
        functools.partial(product_kernel, orders),
        out_shape=[shape(row_tiles, nb, tile), shape(ny, part, cols), shape(ny, part, cols)],
        in_specs=[whole] * 4,
        out_specs=[whole] * 3,
        scratch_shapes=[pltpu.VMEM((nb, rows), BF16), pltpu.VMEM((nb, rows), BF16), pltpu.VMEM((nb, cols), F32)],
        compiler_params=VMEM,
        cost_estimate=pl.CostEstimate(flops=6 * nb * rows * cols, bytes_accessed=rows * cols * 8, transcendentals=0),
    )(a_high, a_low, first, second)
    other = swap(send, "prow", 1)
    kept = keep + other
    zero = jnp.uint32(0)
    y_piece = lax.dynamic_slice(
        y_rows.reshape(col_tiles, ratio, nb, tile), (zero, group, where["share"], zero), (col_tiles, 1, part, tile)
    )
    y_piece = jnp.transpose(y_piece.reshape(col_tiles, part, tile), (1, 0, 2)).reshape(part, cols)

    turned = []
    for r in range(ny):
        message = pick(kept, where["rounds"][r])
        turned.append(turn(message, 2 * r))
    turned = sum(turned[1:], turned[0])
    y_piece, kept = lax.optimization_barrier((y_piece, kept))
    for mask in cols_order[:-1]:
        low, high = where["half"][mask]
        pair = kept.reshape(2, mask // 2, part, cols)
        kept = pick(pair, low)
        kept = kept + swap(pick(pair, high), "prow", mask)
    piece = kept.reshape(part, cols)
    y_cols = turn(y_piece, 0).reshape(2, part // 2, cols)
    u_rows = pl.pallas_call(
        row_factor_kernel,
        out_shape=shape(rows, 3 * nb, dtype=BF16),
        in_specs=[whole] * 2,
        out_specs=whole,
        compiler_params=VMEM,
        cost_estimate=pl.CostEstimate(flops=6 * nb * nb * rows, bytes_accessed=rows * nb * 8, transcendentals=0),
    )(tfactor, y_rows)
    turned, u_rows = lax.optimization_barrier((turned, u_rows))
    first, second = turned[None, : part // 2], turned[None, part // 2 :]
    first, second = lax.optimization_barrier(first), lax.optimization_barrier(second)
    columns = jnp.concatenate([piece.reshape(2, part // 2, cols), y_cols])
    for mask in lead:
        first = join(first, swap(first, "pcol", mask), col[mask])
        second = join(second, swap(second, "pcol", mask), col[mask])
    first, columns = lax.optimization_barrier((first, columns))
    first_group, second_group = first, second
    for mask in rest[:-2]:
        first = join(first, swap(first, "pcol", mask), col[mask])
        second = join(second, swap(second, "pcol", mask), col[mask])
    first = join(first, swap(first, "pcol", far), col[far])
    second = join(second, swap(second, "pcol", close), col[close])

    columns = gather(columns, "prow", cols_order, row)
    first, y_rows = lax.optimization_barrier((first, y_rows))
    inner = pl.pallas_call(
        inner_kernel,
        out_shape=shape(part // 2, 2 * nb),
        in_specs=[whole] * 3,
        out_specs=whole,
        compiler_params=VMEM,
        cost_estimate=pl.CostEstimate(flops=6 * nb * part * cols, bytes_accessed=cols * nb * 4, transcendentals=0),
    )(first_group, second_group, y_rows)
    for mask in cols_order[::-1]:
        inner = inner + swap(inner, "prow", mask)
    inner = inner[None]
    for mask in rest[:-2]:
        inner = join(inner, swap(inner, "pcol", mask), col[mask])
    u_cols, zc = pl.pallas_call(
        functools.partial(column_factor_kernel, cols_order),
        out_shape=[shape(3 * nb, cols, dtype=BF16), shape(nb, cols)],
        in_specs=[whole] * 2,
        out_specs=[whole] * 2,
        scratch_shapes=[pltpu.VMEM((nb, cols), F32)],
        compiler_params=VMEM,
        cost_estimate=pl.CostEstimate(flops=6 * nb * nb * cols, bytes_accessed=cols * nb * 8, transcendentals=0),
    )(tfactor, columns)

    near_inner = [inner] + [swap(inner, "pcol", mask) for mask in (close, far, close + far)]
    first = join(first, swap(first, "pcol", close), col[close])
    second_came = swap(second, "pcol", far)

    remainder = pl.pallas_call(
        functools.partial(rows_kernel, orders, col_tiles),
        out_shape=shape(rows, cols),
        in_specs=[whole] * 5,
        out_specs=whole,
        scratch_shapes=[pltpu.VMEM((ratio, nb, cols), F32)],
        compiler_params=VMEM,
        cost_estimate=pl.CostEstimate(flops=6 * nb * rows * cols, bytes_accessed=rows * cols * 8, transcendentals=0),
    )(a_full, u_cols, first, second, second_came)
    chunks = 4
    lines = rows * col_tiles // chunks
    result = pl.pallas_call(
        functools.partial(update_kernel, inner_upper),
        out_shape=shape(rows * col_tiles, tile),
        in_specs=[whole] * 8,
        out_specs=pl.BlockSpec(memory_space=pltpu.HBM),
        scratch_shapes=[
            pltpu.VMEM((nb, nb), F32),
            pltpu.VMEM((3 * nb, cols), BF16),
            pltpu.VMEM((chunks, lines, tile), F32),
            pltpu.SemaphoreType.DMA((chunks,)),
        ],
        compiler_params=VMEM,
        cost_estimate=pl.CostEstimate(flops=6 * nb * rows * cols, bytes_accessed=rows * cols * 8, transcendentals=0),
    )(remainder, u_rows, u_cols, zc, *near_inner)
    return result.reshape(trailing.shape)


def solution(mesh):
    return jax.shard_map(
        per_device,
        mesh=mesh,
        in_specs=(P(None, "prow", None, None, "pcol", None), P(None, "prow", None, "pcol"), P()),
        out_specs=P(None, "prow", None, None, "pcol", None),
        check_vma=False,
    )
```

```python
import functools

import jax
import jax.numpy as jnp
from jax import lax
from jax.experimental import pallas as pl
from jax.experimental.pallas import tpu as pltpu
from jax.sharding import PartitionSpec as P

BOTH = ("prow", "pcol")
F32 = jnp.float32
BF16 = jnp.bfloat16
VMEM = pltpu.CompilerParams(vmem_limit_bytes=8 * 1024 * 1024)


def split(values):
    high = values.astype(BF16)
    return high, (values - high.astype(F32)).astype(BF16)


def dot(left, right, dims=((1,), (0,))):
    return lax.dot_general(left, right, (dims, ((), ())), preferred_element_type=F32)


def dot3(left, right, dims=((1,), (0,))):
    (lh, ll), (rh, rl) = left, right
    return dot(lh, rh, dims) + (dot(lh, rl, dims) + dot(ll, rh, dims))


def swap(values, axis, mask):
    n = lax.axis_size(axis)
    return lax.ppermute(values, axis, [(i, i ^ mask) for i in range(n)])


def halving(n):
    masks = []
    while n > 1:
        n //= 2
        masks.append(n)
    return masks


def pick(values, index):
    start = (index,) + (jnp.uint32(0),) * (values.ndim - 1)
    return lax.dynamic_slice(values, start, (1,) + values.shape[1:])[0]


def join(values, other, high):
    pair = jnp.stack([jnp.where(high, other, values), jnp.where(high, values, other)])
    return pair.reshape((-1,) + values.shape[1:])


def gather(values, axis, masks, above):
    values = values[None]
    for mask in masks:
        values = join(values, swap(values, axis, mask), above[mask])
    return values


def slot(index, masks):
    return sum(1 << j for j, mask in enumerate(masks) if index & mask)


def swap_three(values, axis):
    return [swap(values, axis, mask) for mask in (1, 2, 3)]


def split_block_kernel(col_tiles, tile, a_ref, high_ref, low_ref, copy_ref):
    rows = high_ref.shape[0]
    for b in range(col_tiles):
        cols = slice(b * tile, (b + 1) * tile)
        values = a_ref[pl.ds(b, rows, stride=col_tiles), :]
        copy_ref[:, cols] = values
        high, low = split(values)
        high_ref[:, cols] = high
        low_ref[:, cols] = low


def product_kernel(orders, ah_ref, al_ref, first_ref, second_ref, y_ref, keep_ref, send_ref, yh, yl, total):
    nc, half, width, tile = first_ref.shape
    for chunk, (ref, masks) in enumerate(zip((first_ref, second_ref), orders)):
        for a in range(half):
            at = chunk * half + a
            for j in range(nc):
                y_ref[at, j * width : (j + 1) * width, :] = ref[slot(j, masks), a]
            cols = slice(at * tile, (at + 1) * tile)
            yh[:, cols], yl[:, cols] = split(y_ref[at])
    total[...] = dot3((yh[...], yl[...]), (ah_ref[...], al_ref[...]))
    core = lax.axis_index("prow") & 1
    count, part = keep_ref.shape[:2]
    for y in range(count):
        keep_ref[y] = total[pl.ds(pl.multiple_of((2 * y + core) * part, part), part), :]
        send_ref[y] = total[pl.ds(pl.multiple_of((2 * y + 1 - core) * part, part), part), :]


def inner_kernel(first_ref, second_ref, y_ref, inner_ref):
    row_tiles, nb, tile = y_ref.shape
    ratio, half, cols = first_ref.shape
    inner = jnp.zeros((2 * half, nb), F32)
    for g in range(ratio):
        for b in range(cols // tile):
            at = slice(b * tile, (b + 1) * tile)
            left = jnp.concatenate([first_ref[g, :, at], second_ref[g, :, at]], axis=0)
            inner += dot3(split(left), split(y_ref[b * ratio + g]), ((1,), (1,)))
    for side in range(2):
        inner_ref[:, side * nb : (side + 1) * nb] = inner[side * half : (side + 1) * half]


def stack_left(values):
    high, low = split(values)
    return jnp.concatenate([high, high, low], axis=1)


def stack_right(ref, values):
    rows = values.shape[0]
    high, low = split(values)
    ref[:rows, :] = high
    ref[rows : 2 * rows, :] = low
    ref[2 * rows :, :] = high


def row_factor_kernel(t_ref, y_ref, out_ref):
    row_tiles, nb, tile = y_ref.shape
    factor = split(t_ref[...])
    for a in range(row_tiles):
        out_ref[a * tile : (a + 1) * tile, :] = stack_left(dot3(factor, split(y_ref[a])).T)


def column_factor_kernel(order, t_ref, cols_ref, out_ref, z_ref, y):
    slots, _, half, _ = cols_ref.shape
    for s in range(slots):
        for side in range(2):
            rows = slice((2 * s + side) * half, (2 * s + side + 1) * half)
            z_ref[rows, :] = cols_ref[slot(s, order), side]
            y[rows, :] = cols_ref[slot(s, order), 2 + side]
    stack_right(out_ref, dot3(split(t_ref[...]), split(y[...])))


def rows_kernel(orders, col_tiles, a_ref, uc_ref, first_ref, second_ref, came_ref, out_ref, zt):
    ratio, nb, cols = zt.shape
    half = first_ref.shape[1]
    slots = nb // (2 * half)
    tile = cols // col_tiles
    first_order, second_order = orders
    last = second_order[-1]
    bit = (lax.axis_index("pcol") // last) & 1
    for g in range(ratio):
        for s in range(slots):
            zt[g, 2 * s * half : (2 * s + 1) * half, :] = first_ref[slot(g * slots + s, first_order)]
            if s & last == 0:
                for ref, place in ((second_ref, bit), (came_ref, 1 - bit)):
                    at = pl.multiple_of((2 * s + 1) * half + place * (2 * last * half), half)
                    zt[g, pl.ds(at, half), :] = ref[slot(g * slots + s, second_order[:-1])]
    wide = 2
    for i in range(0, col_tiles, wide):
        turned = [zt[g, :, b * tile : (b + 1) * tile].T for b in range(i, i + wide) for g in range(ratio)]
        total = dot(stack_left(jnp.concatenate(turned, axis=0)), uc_ref[...])
        for g in range(ratio * wide):
            at = i * ratio + g
            cut = slice(at * tile, (at + 1) * tile)
            out_ref[cut, :] = a_ref[cut, :] - total[g * tile : (g + 1) * tile, :]


def update_kernel(inner_upper, rest_ref, ur_ref, uc_ref, zc_ref, *refs):
    inners, (out_ref, inner, w, result, write) = refs[:4], refs[4:]
    near = lax.axis_index("pcol") & 3
    nb, cols = zc_ref.shape
    half = inners[0].shape[1]
    slots = nb // (2 * half)
    chunks, lines, tile = result.shape
    col_tiles = cols // tile
    rows = lines // col_tiles
    writes = [pltpu.make_async_copy(result.at[i], out_ref.at[pl.ds(i * lines, lines)], write.at[i]) for i in range(chunks)]
    for r in range(4):
        for u in range(slots // 4):
            for side in range(2):
                at = pl.multiple_of((2 * (u * 4 + (near ^ r)) + side) * half, half)
                inner[pl.ds(at, half), :] = inners[r][slot(u, inner_upper), :, side * nb : (side + 1) * nb]
    stack_right(w, zc_ref[...] - dot3(split(inner[...]), (uc_ref[:nb, :], uc_ref[nb : 2 * nb, :])))
    for i in range(chunks):
        at = slice(i * rows, (i + 1) * rows)
        total = rest_ref[at, :] - dot(ur_ref[at, :], w[...])
        for g in range(rows // tile):
            for b in range(col_tiles):
                line = pl.ds(g * tile * col_tiles + b, tile, stride=col_tiles)
                result[i, line, :] = total[g * tile : (g + 1) * tile, b * tile : (b + 1) * tile]
        writes[i].start()
    for copy in writes:
        copy.wait()


def shape(*dims, dtype=F32):
    return jax.ShapeDtypeStruct(dims, dtype)


def per_device(trailing, reflectors, tfactor):
    row_tiles, _, tile, col_tiles = trailing.shape[:4]
    np_, nc = lax.axis_size("prow"), lax.axis_size("pcol")
    ratio = nc // np_
    ny = np_ // 2
    rows, cols = row_tiles * tile, col_tiles * tile
    nb = tfactor.shape[0]
    part = nb // np_
    half = row_tiles // 2
    block = trailing.reshape(rows * col_tiles, tile)
    mine = jnp.transpose(reflectors.reshape(row_tiles, tile, -1), (0, 2, 1))

    masks, cols_order = halving(nc), halving(np_)
    lead, rest = masks[: len(masks) - len(cols_order)], masks[len(masks) - len(cols_order) :]
    shift = len(cols_order)
    prow, pcol = lax.axis_index("prow").astype(jnp.int32), lax.axis_index("pcol").astype(jnp.int32)
    group = pcol >> shift
    where = {
        "group": group.astype(jnp.uint32),
        "rounds": [((prow >> 1) ^ r).astype(jnp.uint32) for r in range(ny)],
        "share": ((pcol & (np_ - 1)) * part).astype(jnp.uint32),
        "col": {mask: (pcol & mask) != 0 for mask in masks},
        "row": {mask: (prow & mask) != 0 for mask in cols_order},
        "half": {mask: [((prow >> (mask.bit_length() - 1) & 1) ^ side).astype(jnp.uint32) for side in range(2)] for mask in cols_order},
    }
    mine, where = lax.optimization_barrier((mine, where))
    group, col, row = where["group"], where["col"], where["row"]
    whole = pl.BlockSpec(memory_space=pltpu.VMEM)

    def flat(p, q):
        return p * nc + q

    def turn(values, r):
        perm = [
            (flat(p, g * np_ + s), flat(s, g * np_ + (p ^ r))) for p in range(np_) for g in range(ratio) for s in range(np_)
        ]
        return lax.ppermute(values, BOTH, perm)

    inner_upper = [mask // 4 for mask in rest[:-2]]
    far, close = rest[-2:]
    orders = (masks, masks[:-2] + [close, far])
    a_high, a_low, a_full = pl.pallas_call(
        functools.partial(split_block_kernel, col_tiles, tile),
        out_shape=[shape(rows, cols, dtype=BF16)] * 2 + [shape(rows, cols)],
        in_specs=[whole],
        out_specs=[whole] * 3,
        compiler_params=VMEM,
        cost_estimate=pl.CostEstimate(flops=rows * cols * 4, bytes_accessed=rows * cols * 8, transcendentals=0),
    )(block)
    first, second = lax.optimization_barrier(mine[None, :half]), lax.optimization_barrier(mine[None, half:])
    for at, (mask, other) in enumerate(zip(*orders)):
        first_came, second_came = swap(first, "pcol", mask), swap(second, "pcol", other)
        if at == 0:
            second_came, a_high, a_low = lax.optimization_barrier((second_came, a_high, a_low))
        first, second = join(first, first_came, col[mask]), join(second, second_came, col[other])

    y_rows, keep, send = pl.pallas_call(
        functools.partial(product_kernel, orders),
        out_shape=[shape(row_tiles, nb, tile), shape(ny, part, cols), shape(ny, part, cols)],
        in_specs=[whole] * 4,
        out_specs=[whole] * 3,
        scratch_shapes=[pltpu.VMEM((nb, rows), BF16), pltpu.VMEM((nb, rows), BF16), pltpu.VMEM((nb, cols), F32)],
        compiler_params=VMEM,
        cost_estimate=pl.CostEstimate(flops=6 * nb * rows * cols, bytes_accessed=rows * cols * 8, transcendentals=0),
    )(a_high, a_low, first, second)
    other = swap(send, "prow", 1)
    kept = keep + other
    zero = jnp.uint32(0)
    y_piece = lax.dynamic_slice(
        y_rows.reshape(col_tiles, ratio, nb, tile), (zero, group, where["share"], zero), (col_tiles, 1, part, tile)
    )
    y_piece = jnp.transpose(y_piece.reshape(col_tiles, part, tile), (1, 0, 2)).reshape(part, cols)

    turned = []
    for r in range(ny):
        message = pick(kept, where["rounds"][r])
        turned.append(turn(message, 2 * r))
    turned = sum(turned[1:], turned[0])
    y_piece, kept = lax.optimization_barrier((y_piece, kept))
    for mask in cols_order[:-1]:
        low, high = where["half"][mask]
        pair = kept.reshape(2, mask // 2, part, cols)
        kept = pick(pair, low)
        kept = kept + swap(pick(pair, high), "prow", mask)
    piece = kept.reshape(part, cols)
    y_cols = turn(y_piece, 0).reshape(2, part // 2, cols)
    u_rows = pl.pallas_call(
        row_factor_kernel,
        out_shape=shape(rows, 3 * nb, dtype=BF16),
        in_specs=[whole] * 2,
        out_specs=whole,
        compiler_params=VMEM,
        cost_estimate=pl.CostEstimate(flops=6 * nb * nb * rows, bytes_accessed=rows * nb * 8, transcendentals=0),
    )(tfactor, y_rows)
    turned, u_rows = lax.optimization_barrier((turned, u_rows))
    first, second = turned[None, : part // 2], turned[None, part // 2 :]
    first, second = lax.optimization_barrier(first), lax.optimization_barrier(second)
    columns = jnp.concatenate([piece.reshape(2, part // 2, cols), y_cols])
    for mask in lead:
        first = join(first, swap(first, "pcol", mask), col[mask])
        second = join(second, swap(second, "pcol", mask), col[mask])
    first, columns = lax.optimization_barrier((first, columns))
    first_group, second_group = first, second
    for mask in rest[:-2]:
        first = join(first, swap(first, "pcol", mask), col[mask])
        second = join(second, swap(second, "pcol", mask), col[mask])
    first = join(first, swap(first, "pcol", far), col[far])
    second = join(second, swap(second, "pcol", close), col[close])

    columns = gather(columns, "prow", cols_order, row)
    first, y_rows = lax.optimization_barrier((first, y_rows))
    inner = pl.pallas_call(
        inner_kernel,
        out_shape=shape(part // 2, 2 * nb),
        in_specs=[whole] * 3,
        out_specs=whole,
        compiler_params=VMEM,
        cost_estimate=pl.CostEstimate(flops=6 * nb * part * cols, bytes_accessed=cols * nb * 4, transcendentals=0),
    )(first_group, second_group, y_rows)
    for mask in cols_order[::-1]:
        inner = inner + swap(inner, "prow", mask)
    inner = inner[None]
    for mask in rest[:-2]:
        inner = join(inner, swap(inner, "pcol", mask), col[mask])
    u_cols, zc = pl.pallas_call(
        functools.partial(column_factor_kernel, cols_order),
        out_shape=[shape(3 * nb, cols, dtype=BF16), shape(nb, cols)],
        in_specs=[whole] * 2,
        out_specs=[whole] * 2,
        scratch_shapes=[pltpu.VMEM((nb, cols), F32)],
        compiler_params=VMEM,
        cost_estimate=pl.CostEstimate(flops=6 * nb * nb * cols, bytes_accessed=cols * nb * 8, transcendentals=0),
    )(tfactor, columns)

    near_inner = [inner] + [swap(inner, "pcol", mask) for mask in (close, far, close + far)]
    first = join(first, swap(first, "pcol", close), col[close])
    second_came = swap(second, "pcol", far)

    remainder = pl.pallas_call(
        functools.partial(rows_kernel, orders, col_tiles),
        out_shape=shape(rows, cols),
        in_specs=[whole] * 5,
        out_specs=whole,
        scratch_shapes=[pltpu.VMEM((ratio, nb, cols), F32)],
        compiler_params=VMEM,
        cost_estimate=pl.CostEstimate(flops=6 * nb * rows * cols, bytes_accessed=rows * cols * 8, transcendentals=0),
    )(a_full, u_cols, first, second, second_came)
    chunks = 8
    lines = rows * col_tiles // chunks
    result = pl.pallas_call(
        functools.partial(update_kernel, inner_upper),
        out_shape=shape(rows * col_tiles, tile),
        in_specs=[whole] * 8,
        out_specs=pl.BlockSpec(memory_space=pltpu.HBM),
        scratch_shapes=[
            pltpu.VMEM((nb, nb), F32),
            pltpu.VMEM((3 * nb, cols), BF16),
            pltpu.VMEM((chunks, lines, tile), F32),
            pltpu.SemaphoreType.DMA((chunks,)),
        ],
        compiler_params=VMEM,
        cost_estimate=pl.CostEstimate(flops=6 * nb * rows * cols, bytes_accessed=rows * cols * 8, transcendentals=0),
    )(remainder, u_rows, u_cols, zc, *near_inner)
    return result.reshape(trailing.shape)


def solution(mesh):
    return jax.shard_map(
        per_device,
        mesh=mesh,
        in_specs=(P(None, "prow", None, None, "pcol", None), P(None, "prow", None, "pcol"), P()),
        out_specs=P(None, "prow", None, None, "pcol", None),
        check_vma=False,
    )
```
